32 devices in a mesh: blk: 8 (over z, x), span: 4 (over y, core).
Axes of the slice: x: 2, y: 2, z: 4, core: 2. Of those that a mesh axis runs over, the one named last changes fastest.
Arguments:
- fluid_adjoint_in: float32 [5, 64, 128, 128], P(None, 'blk', 'span'), may hold values from -4 to 4
- fluid_source: float32 [5, 64, 128, 128], P(None, 'blk', 'span'), may hold values from -24 to 24
- velocity: float32 [3, 64, 128, 128], P(None, 'blk', 'span'), may hold values from 0.1 to 1
- diffusion: float32 [5], replicated, may hold values from 0.5 to 2
- jacobian: float32 [5, 5], replicated, may hold values from -0.4 to 0.4
- wall_coefficient: float32 [8, 128, 128], P('blk', 'span'), may hold values from 0.5 to 2
- metal_costate_prior: float32 [128, 128, 128], P('blk', 'span'), may hold values from -4 to 4
- solid_source: float32 [128, 128, 128], P('blk', 'span'), may hold values from -12 to 12
- conductivity: float32 [128, 128, 128], P('blk', 'span'), may hold values from 0.3 to 3
- tile_owner: int32 [4, 256, 1], P('span', 'blk'), may hold values from 0 to 7; in each aligned block of 32 rows (0 to 31, 32 to 63, ..., all dimensions but the last counted through in order) at most 12 rows name the same one
- tile_target: int32 [4, 256], P('span', 'blk'), may hold values from 0 to 31
Outputs:
- fluid_adjoint: float32 [5, 64, 128, 128], P(None, 'blk', 'span')
- solid_adjoint: float32 [128, 128, 128], P('blk', 'span')
- residual_norms: float32 [6], replicated
The draws below stay inside these ranges and needn't reach their ends.
Inputs may be any that keep to these rules, and one draw needn't show every extreme that they name: `tile_owner`: within the 32 wall tiles of one fluid block (the rows of one device), no owner is named more than 12 times, a bound that some block reaches; every owner is named by some tile.
All inputs are finite; a program needn't handle non-finite values.
Results may differ from the reference program's by a relative error of at most 0.004.
Values sent between devices are 32-bit elements; how exact they have to be, the bound alone decides.
No kernel may reach another device: no remote copies, remote signals or barrier semaphores. Data moves between devices by JAX's collectives and lax.ppermute only.
A program may use at most 64 MiB of HBM per device.

```python
import math
import jax
import jax.numpy as jnp
import numpy as np
from jax import lax

FIELDS = 5
CX = 8
CY = 32
AXIAL_VOLUMES = 128
CHANNEL_VOLUMES = 16
FSWEEPS = 4
SSWEEPS = 4
CAP = 12
NXF = 64
NXS = 128
RADIAL_VOLUMES = 128
N_BLK = 8
N_SPAN = 4


def place_ends(values, key, low, high):
    extent = values.shape
    index_at = [jax.random.randint(jax.random.fold_in(key, axis), (), 0, extent[axis]) for axis in range(len(extent))]
    values = values.at[tuple(index_at)].set(low)
    longest = extent.index(max(extent))
    index_at[longest] = (index_at[longest] + 1) % extent[longest]
    return values.at[tuple(index_at)].set(high)


def level_of(rng, shape, split, least, high):
    level = 1.0
    for axis_at, parts in split:
        steps = jax.random.uniform(jax.random.fold_in(jax.random.fold_in(rng, 6), axis_at), (parts,), jnp.float32, least / len(split), high / len(split))
        level = level * jnp.repeat(jnp.exp(steps), shape[axis_at] // parts).reshape((-1,) + (1,) * (len(shape) - 1 - axis_at))
    return level


def assign_block(key, own, number, rows, count, top, limit, lean):
    order = jax.random.permutation(key, count)
    heavy_load, ordinary = load_shares(count, rows * top, limit, lean, True), load_shares(count, rows * top, limit, lean, False)
    places = jnp.arange(count)

    def named(lengths, rotation):
        used = int((lengths > 0).sum())
        fixed = max(1, used // 4)
        shifted = fixed + (places - fixed + rotation * (used - fixed)) % max(1, count - fixed)
        return jnp.zeros((count,), jnp.int32).at[order[jnp.where(places < fixed, places, shifted)]].set(jnp.asarray(lengths, jnp.int32))

    lengths = jnp.where(number % 4 == 0, named(heavy_load, number // 4), named(ordinary, number - number // 4 - 1))
    mixed = jax.random.permutation(jax.random.fold_in(own, 3), count)
    source_of, receiver = mixed[0:count // 2 * 2:2], mixed[1:count // 2 * 2:2]
    margin = jnp.minimum(lengths[source_of] - 1, limit - lengths[receiver]) // 2
    margin = jnp.where((source_of == order[0]) | (receiver == order[0]) | (lengths[receiver] == 0), 0, jnp.maximum(margin, 0))
    shifted = jax.random.randint(jax.random.fold_in(own, 4), (count // 2,), 0, 1 << 20) % (margin + 1)
    lengths = lengths.at[source_of].add(-shifted).at[receiver].add(shifted)
    labels = jnp.searchsorted(jnp.cumsum(lengths), jnp.arange(rows * top), side="right").astype(jnp.int32)
    listing = labels.reshape(top, rows).T
    listing = listing[jax.random.permutation(jax.random.fold_in(own, 1), rows)]
    rotation = jax.random.randint(jax.random.fold_in(own, 2), (rows, 1), 0, top)
    return jnp.take_along_axis(listing, (jnp.arange(top)[None, :] + rotation) % top, axis=1)


def load_shares(number_of, total, limit, slope, full):
    portions = [(1 << 20) // math.isqrt(grade ** slope) + 1 for grade in range(1, number_of + 1)]
    largest = limit if full else min(limit, max(-(-total // number_of), total * portions[0] // sum(portions)))
    least = 1 if total - largest >= number_of - 1 else 0
    given, surplus = [largest] + [least] * (number_of - 1), total - largest - least * (number_of - 1)
    while surplus > 0:
        movable = [i for i in range(1, number_of) if given[i] < largest] or [i for i in range(1, number_of) if given[i] < limit]
        whole, budget = sum([portions[i] for i in movable]), surplus
        for i in movable:
            extra = min(limit - given[i], max(1, budget * portions[i] // whole), surplus)
            given[i] = given[i] + extra
            surplus = surplus - extra
    return np.array(given)


def gaussian(own_key, shape, scale, limit, split=(), kind=jnp.bfloat16):
    drawn = jax.random.normal(own_key, shape, jnp.float32) * scale
    if len(split) > 0:
        drawn = level_of(own_key, shape, split, -0.22, 0.18) * drawn
    return jnp.clip(drawn, min=-limit, max=limit).astype(kind)


def setup_inputs(seed: int = 0) -> dict:
    seeds = jax.random.split(jax.random.key(seed), 12)
    fluid_adjoint_in = gaussian(seeds[0], (FIELDS, NXF, RADIAL_VOLUMES, AXIAL_VOLUMES), 0.5, 4.0, ((1, 8), (2, 4)), jnp.float32)
    fluid_source = gaussian(seeds[1], (FIELDS, NXF, RADIAL_VOLUMES, AXIAL_VOLUMES), 4.0, 24.0, ((1, 8), (2, 4)), jnp.float32)
    velocity = jnp.clip(jnp.exp(math.log(1.0) - 2.3025851 * jax.random.uniform(seeds[2], (3, NXF, RADIAL_VOLUMES, AXIAL_VOLUMES), jnp.float32) ** level_of(seeds[2], (3, NXF, RADIAL_VOLUMES, AXIAL_VOLUMES), ((1, 8), (2, 4)), -0.2, 0.2)), 0.1, 1.0)
    diffusion = jnp.clip(jnp.exp(jax.random.uniform(seeds[3], (FIELDS,), jnp.float32, math.log(0.5), math.log(2.0))), 0.5, 2.0)
    jacobian = jnp.clip(jax.random.uniform(seeds[4], (FIELDS, FIELDS), jnp.float32, -0.4, 0.4), -0.4, 0.4)
    wall_coefficient = jnp.clip(jnp.exp(math.log(2.0) - 1.3862944 * jax.random.uniform(seeds[5], (N_BLK, RADIAL_VOLUMES, AXIAL_VOLUMES), jnp.float32) ** level_of(seeds[5], (N_BLK, RADIAL_VOLUMES, AXIAL_VOLUMES), ((0, 8), (1, 4)), -0.2, 0.2)), 0.5, 2.0)
    metal_costate_prior = gaussian(seeds[6], (NXS, RADIAL_VOLUMES, AXIAL_VOLUMES), 0.5, 4.0, ((0, 8), (1, 4)), jnp.float32)
    solid_source = gaussian(seeds[7], (NXS, RADIAL_VOLUMES, AXIAL_VOLUMES), 2.0, 12.0, ((0, 8), (1, 4)), jnp.float32)
    conductivity = jnp.clip(jnp.exp(math.log(3.0) - 2.3025851 * jax.random.uniform(seeds[8], (NXS, RADIAL_VOLUMES, AXIAL_VOLUMES), jnp.float32) ** level_of(seeds[8], (NXS, RADIAL_VOLUMES, AXIAL_VOLUMES), ((0, 8), (1, 4)), -0.2, 0.2)), 0.3, 3.0)
    tile_owner_keys = jax.random.split(jax.random.fold_in(seeds[9], 1), N_SPAN * (N_BLK * CY) // CY)
    tile_owner_turns = jax.random.permutation(jax.random.fold_in(seeds[9], 3), N_SPAN * (N_BLK * CY) // CY)
    tile_owner = jax.vmap(lambda own, number: assign_block(jax.random.fold_in(seeds[9], 2), own, number, CY, N_BLK, 1, CAP, 2))(tile_owner_keys, tile_owner_turns).reshape((N_SPAN, N_BLK * CY, 1))
    tile_target = place_ends(jax.random.randint(seeds[10], (N_SPAN, N_BLK * CY), 0, CY), jax.random.fold_in(seeds[10], 1), 0, CY - 1).astype(jnp.int32)
    return {"fluid_adjoint_in": fluid_adjoint_in, "fluid_source": fluid_source, "velocity": velocity, "diffusion": diffusion, "jacobian": jacobian, "wall_coefficient": wall_coefficient, "metal_costate_prior": metal_costate_prior, "solid_source": solid_source, "conductivity": conductivity, "tile_owner": tile_owner, "tile_target": tile_target}


damping_weight = 0.8

def fluid_operator(bordered_grid_data, velocity, spread, jacobian):
    centre = bordered_grid_data[:, 1:-1, 1:-1, 1:-1]
    x_next = bordered_grid_data[:, 2:, 1:-1, 1:-1]
    y_next = bordered_grid_data[:, 1:-1, 2:, 1:-1]
    z_next = bordered_grid_data[:, 1:-1, 1:-1, 2:]
    beside_all = x_next + bordered_grid_data[:, :-2, 1:-1, 1:-1] + y_next + bordered_grid_data[:, 1:-1, :-2, 1:-1] + z_next + bordered_grid_data[:, 1:-1, 1:-1, :-2]
    mixing = jnp.einsum('fg,gxyz->fxyz', jacobian, centre, precision=lax.Precision.HIGHEST)
    velocity_sum = velocity[0] + velocity[1] + velocity[2]
    return (6.0 * spread + velocity_sum) * centre - spread * beside_all - velocity[0] * x_next - velocity[1] * y_next - velocity[2] * z_next + mixing

def face_conductance(kappa_rim):
    centre = kappa_rim[1:-1, 1:-1, 1:-1]
    return (0.5 * (centre + kappa_rim[2:, 1:-1, 1:-1]), 0.5 * (centre + kappa_rim[:-2, 1:-1, 1:-1]), 0.5 * (centre + kappa_rim[1:-1, 2:, 1:-1]), 0.5 * (centre + kappa_rim[1:-1, :-2, 1:-1]), 0.5 * (centre + kappa_rim[1:-1, 1:-1, 2:]), 0.5 * (centre + kappa_rim[1:-1, 1:-1, :-2]))

def solid_operator(bordered_grid_data, faces, diagonal):
    centre = bordered_grid_data[1:-1, 1:-1, 1:-1]
    flows = faces[0] * bordered_grid_data[2:, 1:-1, 1:-1] + faces[1] * bordered_grid_data[:-2, 1:-1, 1:-1]
    flows = flows + faces[2] * bordered_grid_data[1:-1, 2:, 1:-1] + faces[3] * bordered_grid_data[1:-1, :-2, 1:-1]
    flows = flows + faces[4] * bordered_grid_data[1:-1, 1:-1, 2:] + faces[5] * bordered_grid_data[1:-1, 1:-1, :-2]
    return diagonal * centre - flows

def reference(fluid_adjoint_in, fluid_source, velocity, diffusion, jacobian, wall_coefficient, metal_costate_prior, solid_source, conductivity, tile_owner, tile_target):
    spread = diffusion[:, None, None, None]
    fluid_diagonal = 6.0 * spread + (velocity[0] + velocity[1] + velocity[2]) + jnp.diagonal(jacobian)[:, None, None, None]
    adjoint = fluid_adjoint_in
    for iteration in range(FSWEEPS):
        bordered_grid_data = jnp.pad(adjoint, ((0, 0), (1, 1), (1, 1), (1, 1)))
        fluid_residual = fluid_source - fluid_operator(bordered_grid_data, velocity, spread, jacobian)
        adjoint = adjoint + damping_weight * fluid_residual / fluid_diagonal
    owner = tile_owner[:, :, 0].reshape(N_SPAN, N_BLK, CY).transpose(1, 0, 2).reshape(N_BLK, RADIAL_VOLUMES).astype(jnp.int32)
    target = tile_target.reshape(N_SPAN, N_BLK, CY).transpose(1, 0, 2).reshape(N_BLK, RADIAL_VOLUMES).astype(jnp.int32)
    row_base = (jnp.arange(RADIAL_VOLUMES, dtype=jnp.int32) // CY * CY).astype(jnp.int32)
    destination_rank = (owner * RADIAL_VOLUMES + row_base[None, :] + target).reshape(-1).astype(jnp.int32)
    wall_flux = wall_coefficient * adjoint[4, ::CX]
    surface = jax.ops.segment_sum(wall_flux.reshape(N_BLK * RADIAL_VOLUMES, AXIAL_VOLUMES), destination_rank, num_segments=N_BLK * RADIAL_VOLUMES).reshape(N_BLK, RADIAL_VOLUMES, AXIAL_VOLUMES)
    heat_source = solid_source.at[CHANNEL_VOLUMES - 1::CHANNEL_VOLUMES].add(surface)
    kappa_rim = jnp.pad(conductivity, 1)
    faces = face_conductance(kappa_rim)
    metal_pivot_entries = faces[0] + faces[1] + faces[2] + faces[3] + faces[4] + faces[5]
    thermal_state_grid = metal_costate_prior
    for iteration in range(SSWEEPS):
        bordered_grid_data = jnp.pad(thermal_state_grid, 1)
        metal_imbalance_grid = heat_source - solid_operator(bordered_grid_data, faces, metal_pivot_entries)
        thermal_state_grid = thermal_state_grid + damping_weight * metal_imbalance_grid / metal_pivot_entries
    interface_heat_level = thermal_state_grid[CHANNEL_VOLUMES - 1::CHANNEL_VOLUMES].reshape(N_BLK * RADIAL_VOLUMES, AXIAL_VOLUMES)
    output_entries = jnp.take(interface_heat_level, destination_rank, axis=0).reshape(N_BLK, RADIAL_VOLUMES, AXIAL_VOLUMES)
    gas_outcome = adjoint.at[4, ::CX].add(wall_coefficient * output_entries)
    squares = jnp.concatenate([lax.optimization_barrier(jnp.sum(fluid_residual * fluid_residual, axis=(1, 2, 3))), jnp.sum(metal_imbalance_grid * metal_imbalance_grid)[None]])
    fluid_cells = float(NXF * RADIAL_VOLUMES * AXIAL_VOLUMES)
    solid_cells = float(NXS * RADIAL_VOLUMES * AXIAL_VOLUMES)
    counts = jnp.array([fluid_cells] * 5 + [solid_cells], jnp.float32)
    magnitude_list = jnp.sqrt(squares / counts)
    return (gas_outcome, thermal_state_grid, magnitude_list)
```

```python
import functools

import jax
import jax.numpy as jnp
from jax import lax
from jax.experimental import pallas as pl
from jax.experimental.pallas import tpu as pltpu
from jax.sharding import PartitionSpec as P

SWEEPS = 4
DAMPING = 0.8
HIGHEST = lax.Precision.HIGHEST
F32 = jnp.float32
VMEM = pl.BlockSpec(memory_space=pltpu.VMEM)
SMEM = pl.BlockSpec(memory_space=pltpu.SMEM)
LIMIT = 40 * 1024 * 1024
G = 8
W = 4
GD = 12


def call(kernel, outs, scratch, specs, *args):
    return pl.pallas_call(
        kernel,
        out_shape=[jax.ShapeDtypeStruct(s, F32) for s in outs],
        in_specs=specs,
        out_specs=[VMEM] * len(outs),
        scratch_shapes=[pltpu.VMEM(s, F32) for s in scratch],
        compiler_params=pltpu.CompilerParams(vmem_limit_bytes=LIMIT),
    )(*args)


def beside(x):
    lane = lax.broadcasted_iota(jnp.int32, x.shape, 1)
    last = x.shape[1] - 1
    before = jnp.where(lane == 0, 0.0, pltpu.roll(x, 1, 1))
    after = jnp.where(lane == last, 0.0, pltpu.roll(x, last, 1))
    return before, after


def unless(flag, x):
    return jnp.where(flag, 0.0, x)


def pack_first_kernel(p, t, k, xf, xb, yf, yb):
    fields, depth, rows = p.shape[0], p.shape[1], p.shape[2]
    thick = t.shape[0]
    for f in range(fields):
        xf[f * rows : (f + 1) * rows] = p[f, depth - 1]
        xb[f * rows : (f + 1) * rows] = p[f, 0]
    for j, q in enumerate((t, k)):
        n = fields + j
        xf[n * rows : (n + 1) * rows] = q[thick - 1]
        xb[n * rows : (n + 1) * rows] = q[0]
    for f in range(fields):
        for i in range(depth):
            n = f * depth + i
            yf[n : n + 1] = p[f, i, rows - 1 :]
            yb[n : n + 1] = p[f, i, :1]
    base = fields * depth
    for i in range(thick):
        yf[base + i : base + i + 1] = t[i, rows - 1 :]
        yb[base + i : base + i + 1] = t[i, :1]
    base = base + thick
    for i in range(thick):
        yf[base + W * i : base + W * (i + 1)] = k[i, rows - W :]
        yb[base + W * i : base + W * (i + 1)] = k[i, :W]


def sweep_kernel(level, blocks, spans, *refs):
    first, last = level == 0, level == SWEEPS - 1
    names = ["spread", "jacobian", "p", "src", "vel", "t", "heat", "xl", "xr", "yl", "yr"]
    names += ["k"] if first else ["w", "he", "hx", "ws"]
    names += ["coef", "idx"] if last else []
    names += ["pn", "tn"]
    names += ["wo", "heo", "hxo", "wso"] if first else []
    names += ["rb", "sq", "parts"] if last else ["xf", "xb", "yf", "yb"]
    names += ["pe", "te", "hq"]
    r = dict(zip(names, refs, strict=True))
    p, src, vel, t, heat = r["p"], r["src"], r["vel"], r["t"], r["heat"]
    xl, xr, yl, yr = r["xl"], r["xr"], r["yl"], r["yr"]
    pe, te, hq = r["pe"], r["te"], r["hq"]
    pn, tn = r["pn"], r["tn"]
    fields, depth, rows = p.shape[0], p.shape[1], p.shape[2]
    thick = t.shape[0]
    b, s = lax.axis_index("blk"), lax.axis_index("span")
    no_left, no_right = b == 0, b == blocks - 1
    no_low, no_high = s == 0, s == spans - 1
    own = slice(G, G + rows)
    low = slice(G - 1, G - 1 + rows)
    high = slice(G + 1, G + 1 + rows)
    for f in range(fields):
        for i in range(depth):
            n = f * depth + i
            pe[f, i, own] = p[f, i]
            pe[f, i, G - 1 : G] = unless(no_low, yl[n : n + 1])
            pe[f, i, G + rows : G + rows + 1] = unless(no_high, yr[n : n + 1])
    d = [r["spread"][f] for f in range(fields)]
    jac = [[r["jacobian"][f, g] for g in range(fields)] for f in range(fields)]
    total = [None] * fields
    for i in range(depth):
        u0, u1, u2 = vel[0, i], vel[1, i], vel[2, i]
        us = u0 + u1 + u2
        centre = [pe[f, i, own] for f in range(fields)]
        for f in range(fields):
            side = slice(f * rows, (f + 1) * rows)
            diagonal = us + (6.0 * d[f] + jac[f][f])
            if first:
                w = DAMPING / diagonal
                r["wo"][f, i] = w
            else:
                w = r["w"][f, i]
            xm = pe[f, i - 1, own] if i > 0 else unless(no_left, xl[side])
            xp = pe[f, i + 1, own] if i < depth - 1 else unless(no_right, xr[side])
            ym, yp = pe[f, i, low], pe[f, i, high]
            zm, zp = beside(centre[f])
            res = src[f, i] - diagonal * centre[f]
            res = res + d[f] * ((xm + xp) + (ym + yp) + (zm + zp))
            res = res + u0 * xp + u1 * yp + u2 * zp
            for g in range(fields):
                if g != f:
                    res = res - jac[f][g] * centre[g]
            new = centre[f] + w * res
            pn[f, i] = new
            if last:
                square = res * res
                total[f] = square if total[f] is None else total[f] + square
            else:
                if i == depth - 1:
                    r["xf"][side] = new
                if i == 0:
                    r["xb"][side] = new
                n = f * depth + i
                r["yf"][n : n + 1] = new[rows - 1 :]
                r["yb"][n : n + 1] = new[:1]
    base = fields * depth
    side = slice(fields * rows, (fields + 1) * rows)
    tl, tr = unless(no_left, xl[side]), unless(no_right, xr[side])
    if first:
        he, hx = r["heo"], r["hxo"]
        side = slice((fields + 1) * rows, (fields + 2) * rows)
        hx[0] = unless(no_left, 0.5 * xl[side])
        hx[1] = unless(no_right, 0.5 * xr[side])
        he[...] = jnp.zeros_like(he)
        kbase = base + thick
        for i in range(thick):
            he[i, own] = 0.5 * r["k"][i]
            n = kbase + W * i
            he[i, G - W : G] = unless(no_low, 0.5 * yl[n : n + W])
            he[i, G + rows : G + rows + W] = unless(no_high, 0.5 * yr[n : n + W])
    else:
        he, hx = r["he"], r["hx"]
    for i in range(thick):
        te[i, own] = t[i]
        te[i, G - 1 : G] = unless(no_low, yl[base + i : base + i + 1])
        te[i, G + rows : G + rows + 1] = unless(no_high, yr[base + i : base + i + 1])
        hq[i] = he[i] * te[i]
    hl, hr = hx[0], hx[1]
    hql, hqr = hl * tl, hr * tr
    middle = None

    def around(buf, i, left, right):
        centre = buf[i, own]
        zm, zp = beside(centre)
        xm = buf[i - 1, own] if i > 0 else left
        xp = buf[i + 1, own] if i < thick - 1 else right
        return (xm + xp) + (buf[i, low] + buf[i, high]) + (zm + zp)

    kept = 0
    for i in range(thick):
        h, q = he[i, own], te[i, own]
        diagonal = 6.0 * h + around(he, i, hl, hr)
        if first:
            w = DAMPING / diagonal
            r["wso"][i] = w
        else:
            w = r["ws"][i]
        res = heat[i] - diagonal * q + h * around(te, i, tl, tr) + around(hq, i, hql, hqr)
        new = q + w * res
        tn[i] = new
        if last:
            if i < 3 or i >= thick - 4:
                r["rb"][kept] = res
                kept = kept + 1
            else:
                square = res * res
                middle = square if middle is None else middle + square
        else:
            if i == thick - 1:
                r["xf"][fields * rows : (fields + 1) * rows] = new
            if i == 0:
                r["xb"][fields * rows : (fields + 1) * rows] = new
            r["yf"][base + i : base + i + 1] = new[rows - 1 :]
            r["yb"][base + i : base + i + 1] = new[:1]
    if first:
        tall = rows + 2 * W
        n = (fields + 1) * rows
        for j in range(3):
            r["xf"][n + j * tall : n + (j + 1) * tall] = he[thick - 3 + j, G - W : G + rows + W]
        for j in range(2):
            r["xb"][n + j * tall : n + (j + 1) * tall] = he[j, G - W : G + rows + W]
    if last:
        sq, parts = r["sq"], r["parts"]
        sq[...] = jnp.zeros_like(sq)
        for f in range(fields):
            sq[f : f + 1] = jnp.sum(total[f], axis=0, keepdims=True)
        sq[fields : fields + 1] = jnp.sum(middle, axis=0, keepdims=True)
        flux = r["coef"][0] * pn[fields - 1, 0]
        n = lax.broadcasted_iota(jnp.int32, (blocks * 2 * rows, rows), 0)
        key = n // (2 * rows) * rows + n % (2 * rows) - rows
        hot = jnp.where(key == r["idx"][...], 1.0, 0.0)
        parts[...] = jnp.dot(hot, flux, precision=HIGHEST, preferred_element_type=F32)


def surface_kernel(blocks, arrived, surface, yf, yb):
    rows = surface.shape[0] // 2
    whole = arrived[0]
    for j in range(1, blocks):
        whole = whole + arrived[j]
    surface[...] = whole
    yf[:W] = whole[rows - W : rows]
    yf[W:] = whole[2 * rows - W :]
    yb[:W] = whole[:W]
    yb[W:] = whole[rows : rows + W]


def response_kernel(
    blocks, spans, surface, yl, yr, he, kl, kr, tb, rb, sqb, tn, out, hk, w, da, db, hd, so
):
    thick, rows = tb.shape[0], tb.shape[1]
    b, s = lax.axis_index("blk"), lax.axis_index("span")
    no_left, no_right = b == 0, b == blocks - 1
    no_low, no_high = s == 0, s == spans - 1
    tall = rows + 2 * W
    low_of = GD - W
    whole = slice(low_of, low_of + tall)
    below = slice(low_of - 1, low_of - 1 + tall)
    above = slice(low_of + 1, low_of + 1 + tall)
    own = slice(GD, GD + rows)
    ext = slice(G - W, G + rows + W)
    for buf in (hk, da, db, hd, so):
        buf[...] = jnp.zeros_like(buf)
    sq = sqb[...]
    gained = jnp.zeros((rows, tb.shape[2]), F32)
    for j in range(3):
        hk[0, j, whole] = unless(no_left, kl[j * tall : (j + 1) * tall])
    for j in range(4):
        hk[0, 3 + j, whole] = he[j, ext]
    for j in range(5):
        hk[1, j, whole] = he[thick - 5 + j, ext]
    for j in range(2):
        hk[1, 5 + j, whole] = unless(no_right, kr[j * tall : (j + 1) * tall])
    for region in range(2):
        edge = slice(region * W, (region + 1) * W)
        so[region, own] = surface[region * rows : (region + 1) * rows]
        so[region, GD - W : GD] = unless(no_low, yl[edge])
        so[region, GD + rows : GD + rows + W] = unless(no_high, yr[edge])

    def around(buf, region, j):
        centre = buf[region, j, whole]
        zm, zp = beside(centre)
        return (
            (buf[region, j - 1, whole] + buf[region, j + 1, whole])
            + (buf[region, j, below] + buf[region, j, above])
            + (zm + zp)
        )

    needed = (((2,), (1, 2, 3), (1, 2, 3, 4), (3, 4, 5)), ((4,), (3, 4, 5), (2, 3, 4, 5), (1, 2, 3, 4)))
    diagonals = {}
    for region in range(2):
        for j in range(1, 6):
            h = hk[region, j, whole]
            diagonal = 6.0 * h + around(hk, region, j)
            w[region, j, whole] = jnp.where(h > 0.0, DAMPING / jnp.where(h > 0.0, diagonal, 1.0), 0.0)
            diagonals[region, j] = diagonal
    for i in range(3, thick - 4):
        tn[i] = tb[i]
    for region in range(2):
        old, new = da, db
        at = 2 if region == 0 else 4
        for sweep in range(SWEEPS):
            final = sweep == SWEEPS - 1
            for j in needed[region][sweep]:
                res = so[region, whole] if j == at else None
                if sweep > 0:
                    q = old[region, j, whole]
                    flow = (
                        hk[region, j, whole] * around(old, region, j)
                        + around(hd, region, j)
                        - diagonals[region, j] * q
                    )
                    res = flow if res is None else res + flow
                    change = q + w[region, j, whole] * res
                else:
                    change = w[region, j, whole] * res
                if final:
                    i = j - 3 if region == 0 else thick - 5 + j
                    kept = i if region == 0 else 2 + j
                    mine = slice(W, W + rows)
                    tn[i] = tb[i] + change[mine]
                    full = rb[kept] + res[mine]
                    gained = gained + full * full
                else:
                    new[region, j, whole] = change
            if not final:
                for j in needed[region][sweep]:
                    hd[region, j, whole] = hk[region, j, whole] * new[region, j, whole]
                old, new = new, old
    extra = jnp.sum(gained, axis=0, keepdims=True)
    row = lax.broadcasted_iota(jnp.int32, sq.shape, 0)
    sq = sq + jnp.where(row == 5, extra, 0.0)
    for j in range(blocks):
        out[j, :rows] = tn[thick - 1]
        out[j, rows:] = sq


def return_kernel(blocks, arrived, column, coef, added, sq):
    rows = added.shape[0]
    lane = lax.broadcasted_iota(jnp.int32, (rows, rows), 1)
    taken, squares = None, None
    for j in range(blocks):
        hot = jnp.where(column[...] - j * rows == lane, 1.0, 0.0)
        got = jnp.dot(hot, arrived[j, :rows], precision=HIGHEST, preferred_element_type=F32)
        taken = got if taken is None else taken + got
        squares = arrived[j, rows:] if squares is None else squares + arrived[j, rows:]
    added[...] = coef[0] * taken
    sq[...] = squares


def shards(
    blocks,
    spans,
    fluid_adjoint_in,
    fluid_source,
    velocity,
    diffusion,
    jacobian,
    wall_coefficient,
    metal_costate_prior,
    solid_source,
    conductivity,
    tile_owner,
    tile_target,
):
    fields, depth, rows, z = fluid_adjoint_in.shape
    thick = metal_costate_prior.shape[0]
    tall = rows + 2 * W
    forward = {
        "blk": [(i, (i + 1) % blocks) for i in range(blocks)],
        "span": [(i, (i + 1) % spans) for i in range(spans)],
    }
    backward = {axis: [(j, i) for i, j in pairs] for axis, pairs in forward.items()}

    def exchange(xf, xb, yf, yb):
        return (
            lax.ppermute(xf, "blk", forward["blk"]),
            lax.ppermute(xb, "blk", backward["blk"]),
            lax.ppermute(yf, "span", forward["span"]),
            lax.ppermute(yb, "span", backward["span"]),
        )

    idx = tile_owner[0, :, 0] * rows + tile_target[0]
    row_idx, column_idx = idx[None, :], idx[:, None]
    xrows = (fields + 1) * rows
    yrows = fields * depth + thick
    p, t = fluid_adjoint_in, metal_costate_prior
    sends = call(
        pack_first_kernel,
        [(xrows + rows, z)] * 2 + [(yrows + W * thick, z)] * 2,
        [],
        [VMEM] * 3,
        p,
        t,
        conductivity,
    )
    scratch = [(fields, depth, rows + 2 * G, z), (thick, rows + 2 * G, z), (thick, rows + 2 * G, z)]
    for level in range(SWEEPS):
        first, last = level == 0, level == SWEEPS - 1
        halos = exchange(*sends)
        xl, xr, yl, yr = halos
        if level == 1:
            kl, kr = xl[xrows:], xr[xrows:]
        args = [diffusion, jacobian, p, fluid_source, velocity, t, solid_source, xl, xr, yl, yr]
        args += [conductivity] if first else list(held)
        args += [wall_coefficient, row_idx] if last else []
        outs = [p.shape, t.shape]
        if first:
            outs += [p.shape, (thick, rows + 2 * G, z), (2, rows, z), t.shape]
        if last:
            outs += [(7, rows, z), (8, z), (blocks * 2 * rows, z)]
        else:
            outs += [(xrows + (3 * tall if first else 0), z), (xrows + (2 * tall if first else 0), z)]
            outs += [(yrows, z)] * 2
        got = call(
            functools.partial(sweep_kernel, level, blocks, spans),
            outs,
            scratch,
            [SMEM] * 2 + [VMEM] * (len(args) - 2),
            *args,
        )
        p, t = got[:2]
        if first:
            held = got[2:6]
        if last:
            rb, sq, parts = got[2:]
        else:
            sends = got[-4:]
    arrived = lax.all_to_all(parts.reshape(blocks, 2 * rows, z), "blk", 0, 0)
    surface, yf, yb = call(
        functools.partial(surface_kernel, blocks),
        [(2 * rows, z), (2 * W, z), (2 * W, z)],
        [],
        [VMEM],
        arrived,
    )
    yl = lax.ppermute(yf, "span", forward["span"])
    yr = lax.ppermute(yb, "span", backward["span"])
    region = (2, 7, rows + 2 * GD, z)
    t, out = call(
        functools.partial(response_kernel, blocks, spans),
        [t.shape, (blocks, rows + 8, z)],
        [region] * 5 + [(2, rows + 2 * GD, z)],
        [VMEM] * 9,
        surface,
        yl,
        yr,
        held[1],
        kl,
        kr,
        t,
        rb,
        sq,
    )
    arrived = lax.all_to_all(out, "blk", 0, 0)
    added, sq = call(
        functools.partial(return_kernel, blocks),
        [(rows, z), (8, z)],
        [],
        [VMEM] * 3,
        arrived,
        column_idx,
        wall_coefficient,
    )
    step = 1
    while step < spans:
        sq = sq + lax.ppermute(sq, "span", [(i, i ^ step) for i in range(spans)])
        step = step * 2
    gas = p.at[fields - 1, 0].add(added)
    everyone = blocks * spans
    counts = [float(depth * rows * z * everyone)] * fields + [float(thick * rows * z * everyone)]
    totals = jnp.sum(sq[: fields + 1], axis=1)
    norms = jnp.sqrt(totals / jnp.array(counts, F32))
    return gas, t, norms


def solution(mesh):
    placed = (
        P(None, "blk", "span", None),
        P(None, "blk", "span", None),
        P(None, "blk", "span", None),
        P(),
        P(),
        P("blk", "span", None),
        P("blk", "span", None),
        P("blk", "span", None),
        P("blk", "span", None),
        P("span", "blk", None),
        P("span", "blk"),
    )
    return jax.shard_map(
        functools.partial(shards, mesh.shape["blk"], mesh.shape["span"]),
        mesh=mesh,
        in_specs=placed,
        out_specs=(P(None, "blk", "span", None), P("blk", "span", None), P()),
        check_vma=False,
    )
```

```python
import functools

import jax
import jax.numpy as jnp
from jax import lax
from jax.experimental import pallas as pl
from jax.experimental.pallas import tpu as pltpu
from jax.sharding import PartitionSpec as P

SWEEPS = 4
DAMPING = 0.8
HIGHEST = lax.Precision.HIGHEST
F32 = jnp.float32
VMEM = pl.BlockSpec(memory_space=pltpu.VMEM)
SMEM = pl.BlockSpec(memory_space=pltpu.SMEM)
HBM = pl.BlockSpec(memory_space=pltpu.HBM)
COSTS = (1.0, 30.0, 0.01, 2.0, 3.0, 3.0)
LIMIT = 12 * 1024 * 1024
W = 4
B = 8


def held(*shapes):
    return [pltpu.VMEM(s, F32) for s in shapes]


def call(kernel, outs, scratch, specs, *args, cost=1.0):
    return pl.pallas_call(
        kernel,
        out_shape=[jax.ShapeDtypeStruct(s, F32) if isinstance(s, tuple) else s for s in outs],
        in_specs=specs,
        out_specs=[VMEM] * len(outs),
        scratch_shapes=[pltpu.VMEM(s, F32) if isinstance(s, tuple) else s for s in scratch],
        compiler_params=pltpu.CompilerParams(vmem_limit_bytes=LIMIT),
        cost_estimate=pl.CostEstimate(
            flops=int(cost * 1e6), bytes_accessed=int(cost * 3e6), transcendentals=0
        ),
    )(*args)


def beside(x):
    lane = lax.broadcasted_iota(jnp.int32, x.shape, 1)
    last = x.shape[1] - 1
    before = jnp.where(lane == 0, 0.0, pltpu.roll(x, 1, 1))
    after = jnp.where(lane == last, 0.0, pltpu.roll(x, last, 1))
    return before, after


def unless(flag, x):
    return jnp.where(flag, 0.0, x)


class Place:
    def __init__(self, rows, blocks, spans):
        b, s = lax.axis_index("blk"), lax.axis_index("span")
        self.rows, self.tall = rows, rows + 2 * W
        self.no_left, self.no_right = b == 0, b == blocks - 1
        self.no_low, self.no_high = s == 0, s == spans - 1
        self.ext = slice(B, B + self.tall)
        self.own = slice(B + W, B + W + rows)
        self.low = slice(B, B + W)
        self.high = slice(B + W + rows, B + self.tall)

    def reach(self, by):
        return slice(B + W - by, B + W + self.rows + by)

    def fill(self, store, own, low, high, hide=None):
        no_low, no_high = self.no_low, self.no_high
        if hide is not None:
            own, no_low, no_high = unless(hide, own), no_low | hide, no_high | hide
        store(self.own, own)
        store(self.low, unless(no_low, low))
        store(self.high, unless(no_high, high))

    def inside(self, z):
        row = lax.broadcasted_iota(jnp.int32, (self.tall, z), 0)
        out = ((row < W) & self.no_low) | ((row >= W + self.rows) & self.no_high)
        return jnp.logical_not(out)


def beyond(sl, by):
    return slice(sl.start + by, sl.stop + by)


def rows_at(ref, n, count):
    return ref[n : n + count]


class Arrivals:
    def __init__(self, first, rows, fields, reaches):
        self.first, self.rows, self.fields, self.reaches = first, rows, fields, reaches

    def window(self, level, f, ext=True):
        n = self.first
        for reach in self.reaches[:level]:
            n = n + self.fields * (self.rows + 2 * reach)
        reach = self.reaches[level]
        n = n + f * (self.rows + 2 * reach)
        if ext:
            return slice(n + reach - W, n + reach + W + self.rows)
        return slice(n + reach, n + reach + self.rows)

    def size(self):
        return self.first + sum(self.fields * (self.rows + 2 * reach) for reach in self.reaches)


class Fluid:
    def __init__(self, spread, jacobian, fields):
        self.n = fields
        self.d = [spread[f] for f in range(fields)]
        self.jac = [[jacobian[f, g] for g in range(fields)] for f in range(fields)]

    def diagonal(self, f, us):
        return us + (6.0 * self.d[f] + self.jac[f][f])

    def advance(self, cur, left, right, vel, w, src, sl, which=None):
        u0, u1, u2 = vel
        us = u0 + u1 + u2
        centre = [cur(f, sl) for f in range(self.n)]
        out = {}
        for f in range(self.n) if which is None else which:
            c = centre[f]
            zm, zp = beside(c)
            yp = cur(f, beyond(sl, 1))
            near = (cur(f, beyond(sl, -1)) + yp) + (zm + zp)
            if left is not None:
                near = near + left(f)
            res = u1 * yp + u2 * zp - self.diagonal(f, us) * c
            if right is not None:
                xp = right(f)
                near = near + xp
                res = res + u0 * xp
            res = res + self.d[f] * near
            for g in range(self.n):
                if g != f:
                    res = res - self.jac[f][g] * centre[g]
            if src is not None:
                res = res + src(f)
            out[f] = (res, c + w(f) * res)
        return out


def at(ref, i):
    return lambda f, sl: ref[f, i, sl]


def at_rows(ref, i, sl):
    return lambda f: ref[f, i, sl]


def early_kernel(*refs):
    bufs = refs[6:12]
    yf, yb, xf, sems = refs[12:]
    copies = [
        pltpu.make_async_copy(ref, buf, sems.at[j])
        for j, (ref, buf) in enumerate(zip(refs[:6], bufs, strict=True))
    ]
    for copy in copies:
        copy.start()
    for copy in copies:
        copy.wait()
    p, src, vel, t, heat, k = bufs
    fields, depth, rows = p.shape[0], p.shape[1], p.shape[2]
    thick = t.shape[0]
    n = 0
    for ref in (p, src, vel):
        for f in range(ref.shape[0]):
            for i in range(depth):
                yf[n : n + W] = ref[f, i, rows - W :]
                yb[n : n + W] = ref[f, i, :W]
                n = n + W
    for ref in (t, k, heat):
        for i in range(thick):
            yf[n : n + W] = ref[i, rows - W :]
            yb[n : n + W] = ref[i, :W]
            n = n + W
    planes = [p[f, depth - 1] for f in range(fields)]
    planes += [vel[f, depth - 1] for f in range(3)]
    planes += [vel[0, depth - 2], vel[0, depth - 2] + vel[1, depth - 2] + vel[2, depth - 2]]
    planes += [t[thick - 4 + j] for j in range(4)]
    planes += [k[thick - 4 + j] for j in range(4)]
    planes += [heat[thick - 3 + j] for j in range(3)]
    for j, plane in enumerate(planes):
        xf[j * rows : (j + 1) * rows] = plane


def ahead_kernel(blocks, spans, spread, jacobian, p, src, vel, yl, yr, _, out, a0, a1, a2, sa, va, wa):
    fields, depth, rows, z = p.shape
    thick = (yl.shape[0] // W - (2 * fields + 3) * depth) // 3
    at_place = Place(rows, blocks, spans)
    ext, own = at_place.ext, at_place.own
    fluid = Fluid(spread, jacobian, fields)
    inside = at_place.inside(z)

    def fill(buf, f, j, ref, first, i):
        def store(sl, x):
            buf[f, j, sl] = x

        n = ((first + f) * depth + i) * W
        at_place.fill(store, ref[f, i], rows_at(yl, n, W), rows_at(yr, n, W))

    for f in range(fields):
        for j in range(4):
            fill(a0, f, j, p, 0, depth - 4 + j)
        for j in range(3):
            fill(sa, f, j, src, fields, depth - 3 + j)
    for f in range(3):
        for j in range(3):
            fill(va, f, j, vel, 2 * fields, depth - 3 + j)
    for j in range(3):
        us = va[0, j, ext] + va[1, j, ext] + va[2, j, ext]
        for f in range(fields):
            wa[f, j, ext] = jnp.where(inside, DAMPING / fluid.diagonal(f, us), 0.0)

    def step(old, i, new, j, shift):
        last = j == 2
        got = fluid.advance(
            at(old, i),
            at_rows(old, i - 1, ext),
            None if last else at_rows(old, i + 1, ext),
            [va[c, j, ext] for c in range(3)],
            at_rows(wa, j, ext),
            at_rows(sa, j, ext),
            ext,
        )
        for f in range(fields):
            new(f, got[f][1])

    def into(buf, j):
        def store(f, x):
            buf[f, j, ext] = x

        return store

    for j in range(3):
        step(a0, j + 1, into(a1, j), j, 0)
    for j in range(1, 3):
        step(a1, j, into(a2, j - 1), j, 0)
    corners = [(f * depth + depth - 1) * W for f in range(fields)]
    corners += [((2 * fields + c) * depth + depth - 1) * W for c in range(3)]
    base = (2 * fields + 3) * depth
    corners += [(base + thick - 3 + j) * W for j in range(3)]
    corners += [(base + thick + thick - 3 + j) * W for j in range(3)]
    corners += [(base + 2 * thick + thick - 2 + j) * W for j in range(2)]
    n = 0
    for m in corners:
        out[n : n + W] = yl[m : m + W]
        out[n + W : n + 2 * W] = yr[m : m + W]
        n = n + 2 * W
    for reach, buf, j in ((2, a1, 2), (1, a2, 1)):
        size = rows + 2 * reach
        for f in range(fields):
            out[n : n + size] = buf[f, j, at_place.reach(reach)]
            n = n + size

    def last(f, x):
        out[n + f * rows : n + (f + 1) * rows] = x[W : W + rows]

    step(a2, 1, last, 2, 0)


def around(buf, j, sl):
    zm, zp = beside(buf[j, sl])
    return (
        (buf[j - 1, sl] + buf[j + 1, sl])
        + (buf[j, beyond(sl, -1)] + buf[j, beyond(sl, 1)])
        + (zm + zp)
    )


def solid_weight(h, diagonal):
    return jnp.where(h > 0.0, DAMPING / jnp.where(h > 0.0, diagonal, 1.0), 0.0)


def inner_kernel(
    blocks, spans, spread, jacobian, p, src, vel, t, heat, k, yl, yr, *outs
):
    p0, s0, v0, w0, p1, p2, p3, te, he, so, ti, tb, sqi, dg, ws, ta, tc, qa, qc = outs
    fields, depth, rows, z = p.shape
    thick = t.shape[0]
    here = Place(rows, blocks, spans)
    ext = here.ext
    fluid = Fluid(spread, jacobian, fields)
    inside = here.inside(z)
    first = 0
    for buf, ref in ((p0, p), (s0, src), (v0, vel)):
        for f in range(ref.shape[0]):
            for i in range(depth):

                def store(sl, x, buf=buf, f=f, i=i):
                    buf[f, i, sl] = x

                n = ((first + f) * depth + i) * W
                here.fill(store, ref[f, i], rows_at(yl, n, W), rows_at(yr, n, W))
        first = first + ref.shape[0]
    for i in range(depth):
        us = v0[0, i, ext] + v0[1, i, ext] + v0[2, i, ext]
        for f in range(fields):
            w0[f, i, ext] = jnp.where(inside, DAMPING / fluid.diagonal(f, us), 0.0)
    for level, (old, new) in enumerate(((p0, p1), (p1, p2), (p2, p3))):
        for i in range(level + 1, depth - 1 - level):
            got = fluid.advance(
                at(old, i - level),
                at_rows(old, i - level - 1, ext),
                at_rows(old, i - level + 1, ext),
                [v0[c, i, ext] for c in range(3)],
                at_rows(w0, i, ext),
                at_rows(s0, i, ext),
                ext,
            )
            for f in range(fields):
                new[f, i - level - 1, ext] = got[f][1]
    base = (2 * fields + 3) * depth
    for j, (buf, ref, scale) in enumerate(((te, t, 1.0), (he, k, 0.5), (so, heat, 1.0))):
        for i in range(thick):

            def store(sl, x, buf=buf, i=i, scale=scale):
                buf[i, sl] = scale * x

            n = (base + j * thick + i) * W
            here.fill(store, ref[i], yl[n : n + W], yr[n : n + W])
    for i in range(1, thick - 1):
        h = he[i, ext]
        diagonal = 6.0 * h + around(he, i, ext)
        dg[i, ext] = diagonal
        ws[i, ext] = solid_weight(h, diagonal)
    for i in range(thick):
        qa[i, ext] = he[i, ext] * te[i, ext]
    old, oldq, new, newq = te, qa, ta, qc
    total = None
    for level in range(SWEEPS):
        last = level == SWEEPS - 1
        sl = here.own if last else ext
        for i in range(level + 1, thick - 1 - level):
            h, q = he[i, sl], old[i, sl]
            res = so[i, sl] - dg[i, sl] * q + h * around(old, i, sl) + around(oldq, i, sl)
            value = q + ws[i, sl] * res
            if last:
                tb[i - SWEEPS] = value
                square = res * res
                total = square if total is None else total + square
            else:
                new[i, sl] = value
                newq[i, sl] = h * value
        if not last:
            one = level + 1
            for j, i in enumerate((one, one + 1, thick - 2 - one, thick - 1 - one)):
                ti[level, j] = new[i]
            old, new = new, (tc if new is ta else ta)
            oldq, newq = newq, oldq
    sqi[...] = jnp.zeros_like(sqi)
    sqi[fields : fields + 1] = jnp.sum(total, axis=0, keepdims=True)


def cone_kernel(blocks, spans, sent, spread, jacobian, *refs):
    p0, s0, v0, w0, p1, p2, _, te, he, so, xe, xn, coef, idx = refs[:14]
    back, parts, first, sq, c2, c3, sl_ = refs[14:21]
    l0, d1, d2, vm, wm, n1, n2 = refs[21:]
    fields = p0.shape[0]
    rows, z = coef.shape[1], coef.shape[2]
    here = Place(rows, blocks, spans)
    ext, own, tall = here.ext, here.own, here.tall
    fluid = Fluid(spread, jacobian, fields)
    inside = jnp.logical_and(here.inside(z), jnp.logical_not(here.no_left))
    mine = slice(W, W + rows)
    corner = 0
    for f in range(fields):

        def store(sl, x, f=f):
            l0[f, sl] = x

        n = corner + f * 2 * W
        here.fill(
            store, xe[f * rows : (f + 1) * rows], xn[n : n + W], xn[n + W : n + 2 * W], here.no_left
        )
    for c in range(3):

        def store(sl, x, c=c):
            vm[c, sl] = x

        n = corner + (fields + c) * 2 * W
        m = (fields + c) * rows
        here.fill(store, xe[m : m + rows], xn[n : n + W], xn[n + W : n + 2 * W])
    um = [vm[c, ext] for c in range(3)]
    usm = um[0] + um[1] + um[2]
    for f in range(fields):
        wm[f] = jnp.where(inside, DAMPING / fluid.diagonal(f, usm), 0.0)
    m = (fields + 3) * rows
    u0mm, usmm = xe[m : m + rows], xe[m + rows : m + 2 * rows]

    def arrived(level, f):
        return unless(here.no_left, xn[sent.window(level - 1, f, level < 3)])

    def plane(cur, i, left, right, sl=ext):
        return fluid.advance(
            cur,
            left,
            right,
            [v0[c, i, sl] for c in range(3)],
            at_rows(w0, i, sl),
            at_rows(s0, i, sl),
            sl,
        )

    def put(new, got):
        for f in range(fields):
            new(f, got[f][1])

    def flat(ref):
        return lambda f, sl: ref[f, sl]

    def flat_rows(ref, sl):
        return lambda f: ref[f, sl]

    def into(ref):
        def store(f, x):
            ref[f, ext] = x

        return store

    def into_plane(ref, i):
        def store(f, x):
            ref[f, i, ext] = x

        return store

    put(into(n1), plane(at(p0, 0), 0, flat_rows(l0, ext), at_rows(p0, 1, ext)))
    for f in range(fields):
        d1[f, ext] = wm[f] * (fluid.d[f] + um[0]) * p0[f, 0, ext]
    put(into(n2), plane(flat(n1), 0, lambda f: arrived(1, f) + d1[f, ext], at_rows(p1, 0, ext)))
    put(into(c2), plane(at(p1, 0), 1, flat_rows(n1, ext), at_rows(p1, 1, ext)))
    got = fluid.advance(
        flat(d1), None, flat_rows(n1, ext), um, lambda f: wm[f], None, ext
    )
    for f in range(fields):
        d2[f, ext] = got[f][1]
    put(
        into_plane(c3, 0),
        plane(flat(n2), 0, lambda f: arrived(2, f) + d2[f, ext], flat_rows(c2, ext)),
    )
    put(into_plane(c3, 1), plane(flat(c2), 1, flat_rows(n2, ext), at_rows(p2, 0, ext)))

    def farther(f):
        w = unless(here.no_left, DAMPING / fluid.diagonal(f, usmm))
        return w * (fluid.d[f] + u0mm) * d1[f, own]

    got = fluid.advance(
        flat(d2),
        farther,
        flat_rows(n2, own),
        [u[mine] for u in um],
        lambda f: wm[f, mine],
        None,
        own,
    )
    third = [got[f][1] for f in range(fields)]
    got = plane(at(c3, 0), 0, lambda f: arrived(3, f) + third[f], at_rows(c3, 1, own), own)
    sq[...] = jnp.zeros_like(sq)
    for f in range(fields):
        res, new = got[f]
        first[f] = new
        sq[f : f + 1] = jnp.sum(res * res, axis=0, keepdims=True)
    flux = coef[0] * first[fields - 1]
    n = lax.broadcasted_iota(jnp.int32, (blocks * 2 * rows, rows), 0)
    key = n // (2 * rows) * rows + n % (2 * rows) - rows
    hot = jnp.where(key == idx[...], 1.0, 0.0)
    parts[...] = jnp.dot(hot, flux, precision=HIGHEST, preferred_element_type=F32)
    n = 0
    for buf, count in ((te, 4), (he, 4), (so, 3)):
        for i in range(count):
            back[n : n + tall] = buf[i, ext]
            n = n + tall
    for reach, read in (
        (3, at(p0, 0)),
        (2, flat(n1)),
        (1, flat(n2)),
        (0, at(c3, 0)),
    ):
        size = rows + 2 * reach
        for f in range(fields):
            back[n : n + size] = read(f, here.reach(reach))
            n = n + size
    corner = corner + (fields + 3) * 2 * W
    early = (fields + 5) * rows
    zero = jnp.zeros((W, z), F32)
    j = 0
    for near, scale in ((4, 1.0), (4, 0.5), (3, 1.0)):
        for i in range(near):

            def store(sl, x, j=j, scale=scale):
                sl_[j, sl.start - B : sl.stop - B] = scale * x

            if i > 0:
                low, high = xn[corner : corner + W], xn[corner + W : corner + 2 * W]
                corner = corner + 2 * W
            else:
                low, high = zero, zero
            here.fill(store, xe[early : early + rows], low, high, here.no_left)
            early = early + rows
            j = j + 1


def rest_kernel(blocks, spans, sent, spread, jacobian, *refs):
    p0, s0, v0, w0, p1, p2, p3, c2, c3, first, sqb, xn, _, gas, sq, n1, n2, n3 = refs
    fields, depth = gas.shape[0], gas.shape[1]
    rows = gas.shape[2]
    here = Place(rows, blocks, spans)
    ext, own, tall = here.ext, here.own, here.tall
    fluid = Fluid(spread, jacobian, fields)
    def arrived(level):
        return lambda f: unless(here.no_right, xn[sent.window(level, f, level < 3)])

    known = [{i: (p0, i) for i in range(depth)}, {}, {}, {}]
    for level, buf in enumerate((p1, p2, p3)):
        for i in range(level + 1, depth - 1 - level):
            known[level + 1][i] = (buf, i - level - 1)
    known[2][1], known[3][0], known[3][1] = (c2, None), (c3, 0), (c3, 1)

    def read(level, i):
        ref, j = known[level][i]
        return (lambda f, sl: ref[f, sl]) if j is None else (lambda f, sl: ref[f, j, sl])

    def plane(level, i, sl=ext):
        right = arrived(level)
        if i < depth - 1:
            right = functools.partial(read(level, i + 1), sl=sl)
        return fluid.advance(
            read(level, i),
            functools.partial(read(level, i - 1), sl=sl),
            right,
            [v0[c, i, sl] for c in range(3)],
            at_rows(w0, i, sl),
            at_rows(s0, i, sl),
            sl,
        )

    todo = ((depth - 1,), (depth - 2, depth - 1), (2, depth - 3, depth - 2, depth - 1))
    for level, new in enumerate((n1, n2, n3)):
        for j, i in enumerate(todo[level]):
            got = plane(level, i)
            for f in range(fields):
                new[f, j, ext] = got[f][1]
            known[level + 1][i] = (new, j)
    total = [None] * fields
    for f in range(fields):
        gas[f, 0] = first[f]
    for i in range(1, depth):
        got = plane(3, i, own)
        for f in range(fields):
            res, new = got[f]
            gas[f, i] = new
            square = res * res
            total[f] = square if total[f] is None else total[f] + square
    sq[...] = sqb[...]
    for f in range(fields):
        sq[f : f + 1] = sq[f : f + 1] + jnp.sum(total[f], axis=0, keepdims=True)


def solid_kernel(blocks, spans, te, he, so, ti, tbi, sqi, dg, ws, sl_, xb, _, *refs):
    tb, rb, sq, rh, rd, rw = refs[:6]
    to, ho, do, wo, heat, t0, q0, t1, q1 = refs[6:]
    thick, rows, z = tb.shape
    here = Place(rows, blocks, spans)
    ext, own, tall = here.ext, here.own, here.tall
    left, right = 0, 0
    for buf, near in ((to, 4), (ho, 4), (heat, 3)):
        for i in range(near):
            buf[4 - near + i, ext] = sl_[left]
            buf[4 + i, ext] = unless(here.no_right, xb[right : right + tall])
            left, right = left + 1, right + tall

    def place(inside, outside, i):
        if 0 <= i < thick:
            return inside, i
        return outside, (i + 4 if i < 0 else i - thick + 4)

    def h_of(i, sl):
        ref, j = place(he, ho, i)
        return ref[j, sl]

    for i in (-3, -2, -1, 0, thick - 1, thick, thick + 1, thick + 2):
        zm, zp = beside(h_of(i, ext))
        h = h_of(i, ext)
        near = (h_of(i - 1, ext) + h_of(i + 1, ext)) + (zm + zp)
        near = near + (h_of(i, beyond(ext, -1)) + h_of(i, beyond(ext, 1)))
        diagonal = 6.0 * h + near
        j = i + 3 if i <= 0 else i - (thick - 1) + 4
        do[j, ext] = diagonal
        wo[j, ext] = solid_weight(h, diagonal)

    def d_of(ref, outer, i, sl):
        if 0 < i < thick - 1:
            return ref[i, sl]
        return outer[i + 3 if i <= 0 else i - (thick - 1) + 4, sl]

    def first(side, level):
        return level - 4 if side == 0 else thick - 2 - level

    sums = None
    for side in range(2):
        old, oldq, new, newq = t0, q0, t1, q1
        for j in range(6):
            i = first(side, 0) + j
            ref, m = place(te, to, i)
            old[j] = ref[m]
            oldq[j, ext] = h_of(i, ext) * ref[m, ext]
        for level in range(SWEEPS):
            last = level == SWEEPS - 1
            sl = own if last else ext
            for j in range(1, 5):
                i = first(side, level) + j
                ref, m = place(so, heat, i)
                h, q = h_of(i, sl), old[j, sl]
                res = ref[m, sl] - d_of(dg, do, i, sl) * q
                res = res + h * around(old, j, sl) + around(oldq, j, sl)
                value = q + d_of(ws, wo, i, sl) * res
                if last:
                    tb[i] = value
                    if i < 3:
                        rb[i] = res
                    elif i >= thick - 4:
                        rb[i - (thick - 7)] = res
                    else:
                        sums = res * res
                else:
                    m = j - 1 if side == 0 else j + 1
                    new[m, ext] = value
                    newq[m, ext] = h * value
            if not last:
                for m in range(2):
                    j = m + 4 if side == 0 else m
                    i = first(side, level + 1) + j
                    new[j] = ti[level, m + 2 * side]
                    newq[j, ext] = h_of(i, ext) * new[j, ext]
            old, oldq, new, newq = new, newq, old, oldq
    for i in range(SWEEPS, thick - SWEEPS):
        tb[i] = tbi[i - SWEEPS]
    sq[...] = sqi[...]
    n = refs[2].shape[0] - 3
    sq[n : n + 1] = sq[n : n + 1] + jnp.sum(sums, axis=0, keepdims=True)
    for region in range(2):
        for j in range(5):
            i = j - 2 if region == 0 else thick - 4 + j
            rh[region, j, ext] = h_of(i, ext)
            rd[region, j, ext] = d_of(dg, do, i, ext)
            rw[region, j, ext] = d_of(ws, wo, i, ext)


def surface_kernel(blocks, arrived, surface, yf, yb):
    rows = surface.shape[0] // 2
    whole = arrived[0]
    for j in range(1, blocks):
        whole = whole + arrived[j]
    surface[...] = whole
    yf[:W] = whole[rows - W : rows]
    yf[W:] = whole[2 * rows - W :]
    yb[:W] = whole[:W]
    yb[W:] = whole[rows : rows + W]


def response_kernel(
    blocks, spans, fields, surface, yl, yr, rh, rd, rw, tb, rb, sqf, sqs, tn, out, da, db, hd, so
):
    thick, rows, z = tb.shape
    here = Place(rows, blocks, spans)
    ext, own = here.ext, here.own
    for buf in (da, db, hd):
        buf[...] = jnp.zeros_like(buf)
    sq = sqf[...] + sqs[...]
    gained = jnp.zeros((rows, z), F32)
    for region in range(2):

        def store(sl, x, region=region):
            so[region, sl] = x

        edge = slice(region * W, (region + 1) * W)
        here.fill(store, surface[region * rows : (region + 1) * rows], yl[edge], yr[edge])

    needed = (((2,), (1, 2, 3), (1, 2, 3, 4), (3, 4, 5)), ((4,), (3, 4, 5), (2, 3, 4, 5), (1, 2, 3, 4)))
    for i in range(3, thick - 4):
        tn[i] = tb[i]
    for region in range(2):
        old, new = da, db
        source = 2 if region == 0 else 4
        for sweep in range(SWEEPS):
            final = sweep == SWEEPS - 1
            for j in needed[region][sweep]:
                res = so[region, ext] if j == source else None
                h, w = rh[region, j - 1, ext], rw[region, j - 1, ext]
                if sweep > 0:
                    q = old[region, j, ext]
                    flow = h * around(old.at[region], j, ext) + around(hd.at[region], j, ext) - rd[region, j - 1, ext] * q
                    res = flow if res is None else res + flow
                    change = q + w * res
                else:
                    change = w * res
                if final:
                    i = j - 3 if region == 0 else thick - 5 + j
                    kept = i if region == 0 else 2 + j
                    mine = slice(W, W + rows)
                    tn[i] = tb[i] + change[mine]
                    full = rb[kept] + res[mine]
                    gained = gained + full * full
                else:
                    new[region, j, ext] = change
            if not final:
                for j in needed[region][sweep]:
                    hd[region, j, ext] = rh[region, j - 1, ext] * new[region, j, ext]
                old, new = new, old
    extra = jnp.sum(gained, axis=0, keepdims=True)
    row = lax.broadcasted_iota(jnp.int32, sq.shape, 0)
    sq = sq + jnp.where(row == fields, extra, 0.0)
    for j in range(blocks):
        out[j, :rows] = tn[thick - 1]
        out[j, rows:] = sq


def return_kernel(blocks, arrived, idx, coef, added, sq):
    rows = added.shape[0]
    row = lax.broadcasted_iota(jnp.int32, (rows, rows), 0)
    taken, squares = None, None
    for j in range(blocks):
        hot = jnp.where(idx[...] - j * rows == row, 1.0, 0.0)
        got = lax.dot_general(
            hot,
            arrived[j, :rows],
            (((0,), (0,)), ((), ())),
            precision=HIGHEST,
            preferred_element_type=F32,
        )
        taken = got if taken is None else taken + got
        squares = arrived[j, rows:] if squares is None else squares + arrived[j, rows:]
    added[...] = coef[0] * taken
    sq[...] = squares


def shards(
    blocks,
    spans,
    fluid_adjoint_in,
    fluid_source,
    velocity,
    diffusion,
    jacobian,
    wall_coefficient,
    metal_costate_prior,
    solid_source,
    conductivity,
    tile_owner,
    tile_target,
):
    p, src, vel = fluid_adjoint_in, fluid_source, velocity
    t, heat, k = metal_costate_prior, solid_source, conductivity
    fields, depth, rows, z = p.shape
    thick = t.shape[0]
    tall = rows + 2 * W
    buf = tall + 2 * B
    forward = {
        "blk": [(i, (i + 1) % blocks) for i in range(blocks)],
        "span": [(i, (i + 1) % spans) for i in range(spans)],
    }
    backward = {axis: [(j, i) for i, j in pairs] for axis, pairs in forward.items()}

    def ahead(x, axis):
        return lax.ppermute(x, axis, forward[axis])

    def behind(x, axis):
        return lax.ppermute(x, axis, backward[axis])

    idx = tile_owner[0, :, 0] * rows + tile_target[0]
    row_idx = idx[None, :]
    yrows = ((2 * fields + 3) * depth + 3 * thick) * W
    inputs = [p, src, vel, t, heat, k]
    p, src, vel, t, heat, k, yf, yb, xf = call(
        early_kernel,
        held(*[x.shape for x in inputs])
        + [(yrows, z), (yrows, z), ((fields + 16) * rows, z)],
        [pltpu.SemaphoreType.DMA((6,))],
        [HBM] * 6,
        *[pltpu.with_memory_space_constraint(x, pltpu.HBM) for x in inputs],
    )
    yl, yr = ahead(yf, "span"), behind(yb, "span")
    xe = ahead(xf, "blk")
    sent_ahead = Arrivals((fields + 11) * 2 * W, rows, fields, (2, 1, 0))
    (out,) = call(
        functools.partial(ahead_kernel, blocks, spans),
        [(sent_ahead.size(), z)],
        [(fields, 4, buf, z), (fields, 3, buf, z), (fields, 2, buf, z), (fields, 3, buf, z)]
        + [(3, 3, buf, z), (fields, 3, buf, z)],
        [SMEM] * 2 + [VMEM] * 6,
        diffusion,
        jacobian,
        p,
        src,
        vel,
        yl,
        yr,
        xe,
        cost=COSTS[1],
    )
    xn = ahead(out, "blk")
    full = (fields, depth, buf, z)
    part = [(fields, depth - 2 * (level + 1), buf, z) for level in range(3)]
    solid = (thick, buf, z)
    p0, s0, v0, w0, p1, p2, p3, te, he, so, ti, tb, sqi, dg, ws = call(
        functools.partial(inner_kernel, blocks, spans),
        held(full, full, (3, depth, buf, z), full, *part, solid, solid, solid)
        + held((3, 4, buf, z), (thick - 2 * SWEEPS, rows, z), (8, z), solid, solid),
        [solid] * 4,
        [SMEM] * 2 + [VMEM] * 8,
        diffusion,
        jacobian,
        p,
        src,
        vel,
        t,
        heat,
        k,
        yl,
        yr,
        cost=COSTS[2],
    )
    sent_back = Arrivals(11 * tall, rows, fields, (3, 2, 1, 0))
    flat = (fields, buf, z)
    back, parts, first, sq, c2, c3, sl_ = call(
        functools.partial(cone_kernel, blocks, spans, sent_ahead),
        [(sent_back.size(), z), (blocks * 2 * rows, z)]
        + held((fields, rows, z), (8, z), flat, (fields, 2, buf, z), (11, tall, z)),
        [flat] * 3 + [(3, buf, z), (fields, tall, z)] + [flat] * 2,
        [SMEM] * 2 + [VMEM] * 14,
        diffusion,
        jacobian,
        p0,
        s0,
        v0,
        w0,
        p1,
        p2,
        p3,
        te,
        he,
        so,
        xe,
        xn,
        wall_coefficient,
        row_idx,
        cost=COSTS[3],
    )
    xr = behind(back, "blk")
    arrived = lax.all_to_all(parts.reshape(blocks, 2 * rows, z), "blk", 0, 0)
    surface, yf, yb = call(
        functools.partial(surface_kernel, blocks),
        [(2 * rows, z), (2 * W, z), (2 * W, z)],
        [],
        [VMEM],
        arrived,
    )
    yl, yr = ahead(yf, "span"), behind(yb, "span")
    gas, sqf = call(
        functools.partial(rest_kernel, blocks, spans, sent_back),
        [p.shape, (8, z)],
        [(fields, 1, buf, z), (fields, 2, buf, z), (fields, 4, buf, z)],
        [SMEM] * 2 + [VMEM] * 13,
        diffusion,
        jacobian,
        p0,
        s0,
        v0,
        w0,
        p1,
        p2,
        p3,
        c2,
        c3,
        first,
        sq,
        xr,
        yf,
        cost=COSTS[4],
    )
    outer, edge = (8, buf, z), (2, 5, buf, z)
    tb, rb, sqs, rh, rd, rw = call(
        functools.partial(solid_kernel, blocks, spans),
        held(t.shape, (7, rows, z), (8, z), edge, edge, edge),
        [outer] * 5 + [(6, buf, z)] * 4,
        [VMEM] * 11,
        te,
        he,
        so,
        ti,
        tb,
        sqi,
        dg,
        ws,
        sl_,
        xr,
        yf,
        cost=COSTS[5],
    )
    region = (2, 7, buf, z)
    t, out = call(
        functools.partial(response_kernel, blocks, spans, fields),
        [t.shape, (blocks, rows + 8, z)],
        [region] * 3 + [(2, buf, z)],
        [VMEM] * 10,
        surface,
        yl,
        yr,
        rh,
        rd,
        rw,
        tb,
        rb,
        sqf,
        sqs,
    )
    arrived = lax.all_to_all(out, "blk", 0, 0)
    added, sq = call(
        functools.partial(return_kernel, blocks),
        [(rows, z), (8, z)],
        [],
        [VMEM] * 3,
        arrived,
        row_idx,
        wall_coefficient,
    )
    step = 1
    while step < spans:
        sq = sq + lax.ppermute(sq, "span", [(i, i ^ step) for i in range(spans)])
        step = step * 2
    gas = gas.at[fields - 1, 0].add(added)
    everyone = blocks * spans
    counts = [float(depth * rows * z * everyone)] * fields + [float(thick * rows * z * everyone)]
    totals = jnp.sum(sq[: fields + 1], axis=1)
    norms = jnp.sqrt(totals / jnp.array(counts, F32))
    return gas, t, norms


def solution(mesh):
    placed = (
        P(None, "blk", "span", None),
        P(None, "blk", "span", None),
        P(None, "blk", "span", None),
        P(),
        P(),
        P("blk", "span", None),
        P("blk", "span", None),
        P("blk", "span", None),
        P("blk", "span", None),
        P("span", "blk", None),
        P("span", "blk"),
    )
    return jax.shard_map(
        functools.partial(shards, mesh.shape["blk"], mesh.shape["span"]),
        mesh=mesh,
        in_specs=placed,
        out_specs=(P(None, "blk", "span", None), P("blk", "span", None), P()),
        check_vma=False,
    )
```

```python
import functools

import jax
import jax.numpy as jnp
from jax import lax
from jax.experimental import pallas as pl
from jax.experimental.pallas import tpu as pltpu
from jax.sharding import PartitionSpec as P

SWEEPS = 4
DAMPING = 0.8
HIGHEST = lax.Precision.HIGHEST
F32 = jnp.float32
VMEM = pl.BlockSpec(memory_space=pltpu.VMEM)
SMEM = pl.BlockSpec(memory_space=pltpu.SMEM)
HBM = pl.BlockSpec(memory_space=pltpu.HBM)
COSTS = (1.0, 30.0, 0.01, 2.0, 3.0, 3.0)
LIMIT = 12 * 1024 * 1024
W = 4
CAP = 12
CHUNK = 32
B = 8


def held(*shapes):
    return [pltpu.VMEM(s, F32) for s in shapes]


def call(kernel, outs, scratch, specs, *args, cost=1.0):
    return pl.pallas_call(
        kernel,
        out_shape=[jax.ShapeDtypeStruct(s, F32) if isinstance(s, tuple) else s for s in outs],
        in_specs=specs,
        out_specs=[VMEM] * len(outs),
        scratch_shapes=[pltpu.VMEM(s, F32) if isinstance(s, tuple) else s for s in scratch],
        compiler_params=pltpu.CompilerParams(vmem_limit_bytes=LIMIT),
        cost_estimate=pl.CostEstimate(
            flops=int(cost * 1e6), bytes_accessed=int(cost * 3e6), transcendentals=0
        ),
    )(*args)


def beside(x):
    lane = lax.broadcasted_iota(jnp.int32, x.shape, 1)
    last = x.shape[1] - 1
    before = jnp.where(lane == 0, 0.0, pltpu.roll(x, 1, 1))
    after = jnp.where(lane == last, 0.0, pltpu.roll(x, last, 1))
    return before, after


def unless(flag, x):
    return jnp.where(flag, 0.0, x)


class Place:
    def __init__(self, rows, blocks, spans):
        b, s = lax.axis_index("blk"), lax.axis_index("span")
        self.rows, self.tall = rows, rows + 2 * W
        self.no_left, self.no_right = b == 0, b == blocks - 1
        self.no_low, self.no_high = s == 0, s == spans - 1
        self.ext = slice(B, B + self.tall)
        self.own = slice(B + W, B + W + rows)
        self.low = slice(B, B + W)
        self.high = slice(B + W + rows, B + self.tall)

    def reach(self, by):
        return slice(B + W - by, B + W + self.rows + by)

    def fill(self, store, own, low, high, hide=None):
        no_low, no_high = self.no_low, self.no_high
        if hide is not None:
            own, no_low, no_high = unless(hide, own), no_low | hide, no_high | hide
        store(self.own, own)
        store(slice(self.low.stop - low.shape[0], self.low.stop), unless(no_low, low))
        store(slice(self.high.start, self.high.start + high.shape[0]), unless(no_high, high))

    def inside(self, z):
        row = lax.broadcasted_iota(jnp.int32, (self.tall, z), 0)
        out = ((row < W) & self.no_low) | ((row >= W + self.rows) & self.no_high)
        return jnp.logical_not(out)


def beyond(sl, by):
    return slice(sl.start + by, sl.stop + by)


def rows_at(ref, n, count):
    return ref[n : n + count]


class Arrivals:
    def __init__(self, first, rows, fields, reaches):
        self.first, self.rows, self.fields, self.reaches = first, rows, fields, reaches

    def window(self, level, f, ext=True):
        n = self.first
        for reach in self.reaches[:level]:
            n = n + self.fields * (self.rows + 2 * reach)
        reach = self.reaches[level]
        n = n + f * (self.rows + 2 * reach)
        if ext:
            return slice(n + reach - W, n + reach + W + self.rows)
        return slice(n + reach, n + reach + self.rows)

    def size(self):
        return self.first + sum(self.fields * (self.rows + 2 * reach) for reach in self.reaches)


class Edges:
    def __init__(self, fields, depth, thick):
        n = 0
        self.fluid, self.outer, self.solid = {}, {}, {}
        for name, count, reach in (("p", fields, W), ("src", fields, W - 1), ("vel", 3, W - 1)):
            for f in range(count):
                for i in range(depth):
                    self.fluid[name, f, i] = slice(n, n + reach)
                    n = n + reach
        for name, near, reach in (("t", 3, W), ("k", 3, W), ("heat", 2, W - 1)):
            for i in range(thick - near, thick):
                self.outer[name, i] = slice(n, n + reach)
                n = n + reach
        self.size = (n + 7) // 8 * 8
        n = 0
        for name, reach in (("t", W), ("k", W), ("heat", W - 1)):
            for i in range(thick):
                self.solid[name, i] = slice(n, n + reach)
                n = n + reach
        self.solid_size = (n + 7) // 8 * 8


class Fluid:
    def __init__(self, spread, jacobian, fields):
        self.n = fields
        self.d = [spread[f] for f in range(fields)]
        self.jac = [[jacobian[f, g] for g in range(fields)] for f in range(fields)]

    def diagonal(self, f, us):
        return us + (6.0 * self.d[f] + self.jac[f][f])

    def advance(self, cur, left, right, vel, w, src, sl, which=None):
        u0, u1, u2 = vel
        us = u0 + u1 + u2
        centre = [cur(f, sl) for f in range(self.n)]
        out = {}
        for f in range(self.n) if which is None else which:
            c = centre[f]
            zm, zp = beside(c)
            yp = cur(f, beyond(sl, 1))
            near = (cur(f, beyond(sl, -1)) + yp) + (zm + zp)
            if left is not None:
                near = near + left(f)
            res = u1 * yp + u2 * zp - self.diagonal(f, us) * c
            if right is not None:
                xp = right(f)
                near = near + xp
                res = res + u0 * xp
            res = res + self.d[f] * near
            for g in range(self.n):
                if g != f:
                    res = res - self.jac[f][g] * centre[g]
            if src is not None:
                res = res + src(f)
            out[f] = (res, c + w(f) * res)
        return out


def at(ref, i):
    return lambda f, sl: ref[f, i, sl]


def at_rows(ref, i, sl):
    return lambda f: ref[f, i, sl]


def early_kernel(edges, *refs):
    bufs = refs[6:12]
    yf, yb, xf, zf, zb, sems = refs[12:]
    copies = [
        pltpu.make_async_copy(ref, buf, sems.at[j])
        for j, (ref, buf) in enumerate(zip(refs[:6], bufs, strict=True))
    ]
    for copy in copies:
        copy.start()
    for copy in copies:
        copy.wait()
    p, src, vel, t, heat, k = bufs
    fields, depth, rows = p.shape[0], p.shape[1], p.shape[2]
    thick = t.shape[0]
    named = {"p": p, "src": src, "vel": vel, "t": t, "heat": heat, "k": k}
    planes = [p[f, depth - 1] for f in range(fields)]
    planes += [vel[f, depth - 1] for f in range(3)]
    planes += [vel[0, depth - 2], vel[0, depth - 2] + vel[1, depth - 2] + vel[2, depth - 2]]
    planes += [t[thick - 4 + j] for j in range(4)]
    planes += [k[thick - 4 + j] for j in range(4)]
    planes += [heat[thick - 3 + j] for j in range(3)]
    for j, plane in enumerate(planes):
        xf[j * rows : (j + 1) * rows] = plane
    for up, down, places in ((yf, yb, edges.fluid), (yf, yb, edges.outer), (zf, zb, edges.solid)):
        for (name, *at_plane), sl in places.items():
            ref, reach = named[name], sl.stop - sl.start
            up[sl] = ref[*at_plane, rows - reach :]
            down[sl] = ref[*at_plane, :reach]


def ahead_kernel(blocks, spans, edges, spread, jacobian, p, src, vel, yl, yr, out, a0, a1, a2, sa, va, wa):
    fields, depth, rows, z = p.shape
    at_place = Place(rows, blocks, spans)
    ext, own = at_place.ext, at_place.own
    fluid = Fluid(spread, jacobian, fields)
    inside = at_place.inside(z)

    def fill(buf, f, j, ref, name, i):
        def store(sl, x):
            buf[f, j, sl] = x

        sl = edges.fluid[name, f, i]
        at_place.fill(store, ref[f, i], yl[sl], yr[sl])

    for f in range(fields):
        for j in range(4):
            fill(a0, f, j, p, "p", depth - 4 + j)
        for j in range(3):
            fill(sa, f, j, src, "src", depth - 3 + j)
    for f in range(3):
        for j in range(3):
            fill(va, f, j, vel, "vel", depth - 3 + j)
    for j in range(3):
        us = va[0, j, ext] + va[1, j, ext] + va[2, j, ext]
        for f in range(fields):
            wa[f, j, ext] = jnp.where(inside, DAMPING / fluid.diagonal(f, us), 0.0)

    def step(old, i, new, j, shift):
        last = j == 2
        got = fluid.advance(
            at(old, i),
            at_rows(old, i - 1, ext),
            None if last else at_rows(old, i + 1, ext),
            [va[c, j, ext] for c in range(3)],
            at_rows(wa, j, ext),
            at_rows(sa, j, ext),
            ext,
        )
        for f in range(fields):
            new(f, got[f][1])

    def into(buf, j):
        def store(f, x):
            buf[f, j, ext] = x

        return store

    for j in range(3):
        step(a0, j + 1, into(a1, j), j, 0)
    for j in range(1, 3):
        step(a1, j, into(a2, j - 1), j, 0)
    corners = [edges.fluid["p", f, depth - 1] for f in range(fields)]
    corners += [edges.fluid["vel", c, depth - 1] for c in range(3)]
    corners += list(edges.outer.values())
    n = 0
    for sl in corners:
        reach = sl.stop - sl.start
        out[n + W - reach : n + W] = yl[sl]
        out[n + W : n + W + reach] = yr[sl]
        n = n + 2 * W
    for reach, buf, j in ((2, a1, 2), (1, a2, 1)):
        size = rows + 2 * reach
        for f in range(fields):
            out[n : n + size] = buf[f, j, at_place.reach(reach)]
            n = n + size

    def last(f, x):
        out[n + f * rows : n + (f + 1) * rows] = x[W : W + rows]

    step(a2, 1, last, 2, 0)


def around(buf, j, sl):
    zm, zp = beside(buf[j, sl])
    return (
        (buf[j - 1, sl] + buf[j + 1, sl])
        + (buf[j, beyond(sl, -1)] + buf[j, beyond(sl, 1)])
        + (zm + zp)
    )


def solid_weight(h, diagonal):
    return jnp.where(h > 0.0, DAMPING / jnp.where(h > 0.0, diagonal, 1.0), 0.0)


def plan(blocks, owner, target, place, meta, idx):
    rows = target.shape[1]
    me = lax.axis_index("blk")
    row = lax.broadcasted_iota(jnp.int32, (rows, rows), 0)
    lane = lax.broadcasted_iota(jnp.int32, (rows, rows), 1)
    owner = owner[...].astype(F32)
    column = jnp.where(row == lane, jnp.broadcast_to(owner, (rows, rows)), 0.0)
    column = jnp.sum(column, axis=1, keepdims=True)
    idx[...] = owner * rows + target[...].astype(F32)
    before = jnp.where((column == owner) & (row < lane), 1.0, 0.0)
    rank = jnp.sum(before, axis=0, keepdims=True)
    n = lax.broadcasted_iota(jnp.int32, (blocks * CHUNK, rows), 0)
    slot = n % CHUNK
    second = slot >= CAP
    named = n // CHUNK - jnp.where(second, 0, 1)
    at_rank = (slot - jnp.where(second, CAP, 0)).astype(F32)
    hot = jnp.where((owner == named.astype(F32)) & (rank == at_rank), 1.0, 0.0)
    hot = jnp.where(slot < 2 * CAP, hot, 0.0)
    place[...] = hot
    targets = jnp.broadcast_to((target[...] + 1).astype(F32), (8, rows))
    lanes = lax.dot_general(
        targets, hot, (((1,), (1,)), ((), ())), precision=HIGHEST, preferred_element_type=F32
    )
    row = lax.broadcasted_iota(jnp.int32, (8, 4 * CHUNK), 0)
    lane = lax.broadcasted_iota(jnp.int32, (8, 4 * CHUNK), 1)
    for j in range(blocks):
        group = lanes[:, j // 4 * 4 * CHUNK : (j // 4 + 1) * 4 * CHUNK]
        group = jnp.where(lane // CHUNK == j % 4, group, 0.0)
        group = pltpu.roll(group, lax.rem(me - j + 4 * blocks, 4) * CHUNK, 1)
        meta[j] = jnp.where(row == me // 4, group, 0.0)


def inner_kernel(
    blocks, spans, edges, spread, jacobian, owner, target, p, src, vel, yl, yr, *outs
):
    p0, s0, v0, w0, p1, p2, p3, place, meta, idx = outs
    plan(blocks, owner, target, place, meta, idx)
    fields, depth, rows, z = p.shape
    here = Place(rows, blocks, spans)
    ext = here.ext
    fluid = Fluid(spread, jacobian, fields)
    inside = here.inside(z)
    for name, buf, ref in (("p", p0, p), ("src", s0, src), ("vel", v0, vel)):
        for f in range(ref.shape[0]):
            for i in range(depth):

                def store(sl, x, buf=buf, f=f, i=i):
                    buf[f, i, sl] = x

                sl = edges.fluid[name, f, i]
                here.fill(store, ref[f, i], yl[sl], yr[sl])
    for i in range(depth):
        us = v0[0, i, ext] + v0[1, i, ext] + v0[2, i, ext]
        for f in range(fields):
            w0[f, i, ext] = jnp.where(inside, DAMPING / fluid.diagonal(f, us), 0.0)
    for level, (old, new) in enumerate(((p0, p1), (p1, p2), (p2, p3))):
        for i in range(level + 1, depth - 1 - level):
            got = fluid.advance(
                at(old, i - level),
                at_rows(old, i - level - 1, ext),
                at_rows(old, i - level + 1, ext),
                [v0[c, i, ext] for c in range(3)],
                at_rows(w0, i, ext),
                at_rows(s0, i, ext),
                ext,
            )
            for f in range(fields):
                new[f, i - level - 1, ext] = got[f][1]


def inner_solid_kernel(blocks, spans, edges, fields, t, heat, k, yl, yr, *refs):
    te, he, so, ti, tb, sqi, dg, ws, ta, tc, qa, qc = refs
    thick, rows, z = t.shape
    here = Place(rows, blocks, spans)
    ext = here.ext
    for name, buf, ref, scale in (("t", te, t, 1.0), ("k", he, k, 0.5), ("heat", so, heat, 1.0)):
        for i in range(thick):

            def store(sl, x, buf=buf, i=i, scale=scale):
                buf[i, sl] = scale * x

            sl = edges.solid[name, i]
            here.fill(store, ref[i], yl[sl], yr[sl])
    for i in range(1, thick - 1):
        h = he[i, ext]
        diagonal = 6.0 * h + around(he, i, ext)
        dg[i, ext] = diagonal
        ws[i, ext] = solid_weight(h, diagonal)
    for i in range(thick):
        qa[i, ext] = he[i, ext] * te[i, ext]
    old, oldq, new, newq = te, qa, ta, qc
    total = None
    for level in range(SWEEPS):
        last = level == SWEEPS - 1
        sl = here.own if last else ext
        for i in range(level + 1, thick - 1 - level):
            h, q = he[i, sl], old[i, sl]
            res = so[i, sl] - dg[i, sl] * q + h * around(old, i, sl) + around(oldq, i, sl)
            value = q + ws[i, sl] * res
            if last:
                tb[i - SWEEPS] = value
                square = res * res
                total = square if total is None else total + square
            else:
                new[i, sl] = value
                newq[i, sl] = h * value
        if not last:
            one = level + 1
            for j, i in enumerate((one, one + 1, thick - 2 - one, thick - 1 - one)):
                ti[level, j] = new[i]
            old, new = new, (tc if new is ta else ta)
            oldq, newq = newq, oldq
    sqi[...] = jnp.zeros_like(sqi)
    sqi[fields : fields + 1] = jnp.sum(total, axis=0, keepdims=True)


def cone_kernel(blocks, spans, sent, spread, jacobian, *refs):
    p0, s0, v0, w0, p1, p2, _, te, he, so, xe, xn, coef, hot, meta = refs[:15]
    back, parts, first, sq, c2, c3, sl_ = refs[15:22]
    l0, d1, d2, vm, wm, n1, n2 = refs[22:]
    fields = p0.shape[0]
    rows, z = coef.shape[1], coef.shape[2]
    here = Place(rows, blocks, spans)
    ext, own, tall = here.ext, here.own, here.tall
    fluid = Fluid(spread, jacobian, fields)
    inside = jnp.logical_and(here.inside(z), jnp.logical_not(here.no_left))
    mine = slice(W, W + rows)
    corner = 0
    for f in range(fields):

        def store(sl, x, f=f):
            l0[f, sl] = x

        n = corner + f * 2 * W
        here.fill(
            store, xe[f * rows : (f + 1) * rows], xn[n : n + W], xn[n + W : n + 2 * W], here.no_left
        )
    for c in range(3):

        def store(sl, x, c=c):
            vm[c, sl] = x

        n = corner + (fields + c) * 2 * W
        m = (fields + c) * rows
        here.fill(store, xe[m : m + rows], xn[n : n + W], xn[n + W : n + 2 * W])
    um = [vm[c, ext] for c in range(3)]
    usm = um[0] + um[1] + um[2]
    for f in range(fields):
        wm[f] = jnp.where(inside, DAMPING / fluid.diagonal(f, usm), 0.0)
    m = (fields + 3) * rows
    u0mm, usmm = xe[m : m + rows], xe[m + rows : m + 2 * rows]

    def arrived(level, f):
        return unless(here.no_left, xn[sent.window(level - 1, f, level < 3)])

    def plane(cur, i, left, right, sl=ext):
        return fluid.advance(
            cur,
            left,
            right,
            [v0[c, i, sl] for c in range(3)],
            at_rows(w0, i, sl),
            at_rows(s0, i, sl),
            sl,
        )

    def put(new, got):
        for f in range(fields):
            new(f, got[f][1])

    def flat(ref):
        return lambda f, sl: ref[f, sl]

    def flat_rows(ref, sl):
        return lambda f: ref[f, sl]

    def into(ref):
        def store(f, x):
            ref[f, ext] = x

        return store

    def into_plane(ref, i):
        def store(f, x):
            ref[f, i, ext] = x

        return store

    put(into(n1), plane(at(p0, 0), 0, flat_rows(l0, ext), at_rows(p0, 1, ext)))
    for f in range(fields):
        d1[f, ext] = wm[f] * (fluid.d[f] + um[0]) * p0[f, 0, ext]
    put(into(n2), plane(flat(n1), 0, lambda f: arrived(1, f) + d1[f, ext], at_rows(p1, 0, ext)))
    put(into(c2), plane(at(p1, 0), 1, flat_rows(n1, ext), at_rows(p1, 1, ext)))
    got = fluid.advance(
        flat(d1), None, flat_rows(n1, ext), um, lambda f: wm[f], None, ext
    )
    for f in range(fields):
        d2[f, ext] = got[f][1]
    put(
        into_plane(c3, 0),
        plane(flat(n2), 0, lambda f: arrived(2, f) + d2[f, ext], flat_rows(c2, ext)),
    )
    put(into_plane(c3, 1), plane(flat(c2), 1, flat_rows(n2, ext), at_rows(p2, 0, ext)))

    def farther(f):
        w = unless(here.no_left, DAMPING / fluid.diagonal(f, usmm))
        return w * (fluid.d[f] + u0mm) * d1[f, own]

    got = fluid.advance(
        flat(d2),
        farther,
        flat_rows(n2, own),
        [u[mine] for u in um],
        lambda f: wm[f, mine],
        None,
        own,
    )
    third = [got[f][1] for f in range(fields)]
    got = plane(at(c3, 0), 0, lambda f: arrived(3, f) + third[f], at_rows(c3, 1, own), own)
    sq[...] = jnp.zeros_like(sq)
    for f in range(fields):
        res, new = got[f]
        first[f] = new
        sq[f : f + 1] = jnp.sum(res * res, axis=0, keepdims=True)
    flux = coef[0] * first[fields - 1]
    parts[...] = jnp.dot(hot[...], flux, precision=HIGHEST, preferred_element_type=F32)
    for j in range(blocks):
        parts[j * CHUNK + 2 * CAP : (j + 1) * CHUNK] = meta[j]
    n = 0
    for buf, count in ((te, 4), (he, 4), (so, 3)):
        for i in range(count):
            back[n : n + tall] = buf[i, ext]
            n = n + tall
    for reach, read in (
        (3, at(p0, 0)),
        (2, flat(n1)),
        (1, flat(n2)),
        (0, at(c3, 0)),
    ):
        size = rows + 2 * reach
        for f in range(fields):
            back[n : n + size] = read(f, here.reach(reach))
            n = n + size
    corner = corner + (fields + 3) * 2 * W
    early = (fields + 5) * rows
    zero = jnp.zeros((W, z), F32)
    j = 0
    for near, scale in ((4, 1.0), (4, 0.5), (3, 1.0)):
        for i in range(near):

            def store(sl, x, j=j, scale=scale):
                sl_[j, sl.start - B : sl.stop - B] = scale * x

            if i > 0:
                low, high = xn[corner : corner + W], xn[corner + W : corner + 2 * W]
                corner = corner + 2 * W
            else:
                low, high = zero, zero
            here.fill(store, xe[early : early + rows], low, high, here.no_left)
            early = early + rows
            j = j + 1


def rest_kernel(blocks, spans, sent, spread, jacobian, *refs):
    p0, s0, v0, w0, p1, p2, p3, c2, c3, first, sqb, xn, _, gas, sq, n1, n2, n3 = refs
    fields, depth = gas.shape[0], gas.shape[1]
    rows = gas.shape[2]
    here = Place(rows, blocks, spans)
    ext, own, tall = here.ext, here.own, here.tall
    fluid = Fluid(spread, jacobian, fields)
    def arrived(level):
        return lambda f: unless(here.no_right, xn[sent.window(level, f, level < 3)])

    known = [{i: (p0, i) for i in range(depth)}, {}, {}, {}]
    for level, buf in enumerate((p1, p2, p3)):
        for i in range(level + 1, depth - 1 - level):
            known[level + 1][i] = (buf, i - level - 1)
    known[2][1], known[3][0], known[3][1] = (c2, None), (c3, 0), (c3, 1)

    def read(level, i):
        ref, j = known[level][i]
        return (lambda f, sl: ref[f, sl]) if j is None else (lambda f, sl: ref[f, j, sl])

    def plane(level, i, sl=ext):
        right = arrived(level)
        if i < depth - 1:
            right = functools.partial(read(level, i + 1), sl=sl)
        return fluid.advance(
            read(level, i),
            functools.partial(read(level, i - 1), sl=sl),
            right,
            [v0[c, i, sl] for c in range(3)],
            at_rows(w0, i, sl),
            at_rows(s0, i, sl),
            sl,
        )

    todo = ((depth - 1,), (depth - 2, depth - 1), (2, depth - 3, depth - 2, depth - 1))
    for level, new in enumerate((n1, n2, n3)):
        for j, i in enumerate(todo[level]):
            got = plane(level, i)
            for f in range(fields):
                new[f, j, ext] = got[f][1]
            known[level + 1][i] = (new, j)
    total = [None] * fields
    for f in range(fields):
        gas[f, 0] = first[f]
    for i in range(1, depth):
        got = plane(3, i, own)
        for f in range(fields):
            res, new = got[f]
            gas[f, i] = new
            square = res * res
            total[f] = square if total[f] is None else total[f] + square
    sq[...] = sqb[...]
    for f in range(fields):
        sq[f : f + 1] = sq[f : f + 1] + jnp.sum(total[f], axis=0, keepdims=True)


def solid_kernel(blocks, spans, te, he, so, ti, tbi, sqi, dg, ws, sl_, xb, _, *refs):
    tb, rb, sq, rh, rd, rw = refs[:6]
    to, ho, do, wo, heat, t0, q0, t1, q1 = refs[6:]
    thick, rows, z = tb.shape
    here = Place(rows, blocks, spans)
    ext, own, tall = here.ext, here.own, here.tall
    left, right = 0, 0
    for buf, near in ((to, 4), (ho, 4), (heat, 3)):
        for i in range(near):
            buf[4 - near + i, ext] = sl_[left]
            buf[4 + i, ext] = unless(here.no_right, xb[right : right + tall])
            left, right = left + 1, right + tall

    def place(inside, outside, i):
        if 0 <= i < thick:
            return inside, i
        return outside, (i + 4 if i < 0 else i - thick + 4)

    def h_of(i, sl):
        ref, j = place(he, ho, i)
        return ref[j, sl]

    for i in (-3, -2, -1, 0, thick - 1, thick, thick + 1, thick + 2):
        zm, zp = beside(h_of(i, ext))
        h = h_of(i, ext)
        near = (h_of(i - 1, ext) + h_of(i + 1, ext)) + (zm + zp)
        near = near + (h_of(i, beyond(ext, -1)) + h_of(i, beyond(ext, 1)))
        diagonal = 6.0 * h + near
        j = i + 3 if i <= 0 else i - (thick - 1) + 4
        do[j, ext] = diagonal
        wo[j, ext] = solid_weight(h, diagonal)

    def d_of(ref, outer, i, sl):
        if 0 < i < thick - 1:
            return ref[i, sl]
        return outer[i + 3 if i <= 0 else i - (thick - 1) + 4, sl]

    def first(side, level):
        return level - 4 if side == 0 else thick - 2 - level

    sums = None
    for side in range(2):
        old, oldq, new, newq = t0, q0, t1, q1
        for j in range(6):
            i = first(side, 0) + j
            ref, m = place(te, to, i)
            old[j] = ref[m]
            oldq[j, ext] = h_of(i, ext) * ref[m, ext]
        for level in range(SWEEPS):
            last = level == SWEEPS - 1
            sl = own if last else ext
            for j in range(1, 5):
                i = first(side, level) + j
                ref, m = place(so, heat, i)
                h, q = h_of(i, sl), old[j, sl]
                res = ref[m, sl] - d_of(dg, do, i, sl) * q
                res = res + h * around(old, j, sl) + around(oldq, j, sl)
                value = q + d_of(ws, wo, i, sl) * res
                if last:
                    tb[i] = value
                    if i < 3:
                        rb[i] = res
                    elif i >= thick - 4:
                        rb[i - (thick - 7)] = res
                    else:
                        sums = res * res
                else:
                    m = j - 1 if side == 0 else j + 1
                    new[m, ext] = value
                    newq[m, ext] = h * value
            if not last:
                for m in range(2):
                    j = m + 4 if side == 0 else m
                    i = first(side, level + 1) + j
                    new[j] = ti[level, m + 2 * side]
                    newq[j, ext] = h_of(i, ext) * new[j, ext]
            old, oldq, new, newq = new, newq, old, oldq
    for i in range(SWEEPS, thick - SWEEPS):
        tb[i] = tbi[i - SWEEPS]
    sq[...] = sqi[...]
    n = refs[2].shape[0] - 3
    sq[n : n + 1] = sq[n : n + 1] + jnp.sum(sums, axis=0, keepdims=True)
    for region in range(2):
        for j in range(5):
            i = j - 2 if region == 0 else thick - 4 + j
            rh[region, j, ext] = h_of(i, ext)
            rd[region, j, ext] = d_of(dg, do, i, ext)
            rw[region, j, ext] = d_of(ws, wo, i, ext)


def surface_kernel(blocks, arrived, surface, yf, yb):
    rows = surface.shape[0] // 2
    meta = arrived[0, 2 * CAP :]
    for j in range(1, blocks):
        meta = meta + arrived[j, 2 * CAP :]
    row = lax.broadcasted_iota(jnp.int32, (2 * rows, 4 * CHUNK), 0)
    slot = lax.broadcasted_iota(jnp.int32, (2 * rows, 4 * CHUNK), 1) % CHUNK
    row = row + 1 - jnp.where(slot < CAP, 0, rows)
    row = jnp.where((row >= 1) & (row <= rows), row, -1).astype(F32)
    whole = None
    for j in range(0, blocks, 4):
        sent = jnp.concatenate([arrived[j + m] for m in range(4)], axis=0)
        hot = jnp.where(row == meta[j // 4 : j // 4 + 1], 1.0, 0.0)
        got = jnp.dot(hot, sent, precision=HIGHEST, preferred_element_type=F32)
        whole = got if whole is None else whole + got
    surface[...] = whole
    yf[:W] = whole[rows - W : rows]
    yf[W:] = whole[2 * rows - W :]
    yb[:W] = whole[:W]
    yb[W:] = whole[rows : rows + W]


def response_kernel(
    blocks, spans, fields, surface, yl, yr, rh, rd, rw, tb, rb, sqf, sqs, tn, out, da, db, hd, so
):
    thick, rows, z = tb.shape
    here = Place(rows, blocks, spans)
    ext, own = here.ext, here.own
    for buf in (da, db, hd):
        buf[...] = jnp.zeros_like(buf)
    sq = sqf[...] + sqs[...]
    gained = jnp.zeros((rows, z), F32)
    for region in range(2):

        def store(sl, x, region=region):
            so[region, sl] = x

        edge = slice(region * W, (region + 1) * W)
        here.fill(store, surface[region * rows : (region + 1) * rows], yl[edge], yr[edge])

    needed = (((2,), (1, 2, 3), (1, 2, 3, 4), (3, 4, 5)), ((4,), (3, 4, 5), (2, 3, 4, 5), (1, 2, 3, 4)))
    for i in range(3, thick - 4):
        tn[i] = tb[i]
    for region in range(2):
        old, new = da, db
        source = 2 if region == 0 else 4
        for sweep in range(SWEEPS):
            final = sweep == SWEEPS - 1
            for j in needed[region][sweep]:
                res = so[region, ext] if j == source else None
                h, w = rh[region, j - 1, ext], rw[region, j - 1, ext]
                if sweep > 0:
                    q = old[region, j, ext]
                    flow = h * around(old.at[region], j, ext) + around(hd.at[region], j, ext) - rd[region, j - 1, ext] * q
                    res = flow if res is None else res + flow
                    change = q + w * res
                else:
                    change = w * res
                if final:
                    i = j - 3 if region == 0 else thick - 5 + j
                    kept = i if region == 0 else 2 + j
                    mine = slice(W, W + rows)
                    tn[i] = tb[i] + change[mine]
                    full = rb[kept] + res[mine]
                    gained = gained + full * full
                else:
                    new[region, j, ext] = change
            if not final:
                for j in needed[region][sweep]:
                    hd[region, j, ext] = rh[region, j - 1, ext] * new[region, j, ext]
                old, new = new, old
    extra = jnp.sum(gained, axis=0, keepdims=True)
    row = lax.broadcasted_iota(jnp.int32, sq.shape, 0)
    sq = sq + jnp.where(row == fields, extra, 0.0)
    for j in range(blocks):
        out[j, :rows] = tn[thick - 1]
        out[j, rows:] = sq


def return_kernel(blocks, arrived, idx, coef, added, sq):
    rows = added.shape[0]
    row = lax.broadcasted_iota(jnp.int32, (rows, rows), 0).astype(F32)
    taken, squares = None, None
    for j in range(blocks):
        hot = jnp.where(idx[...] - float(j * rows) == row, 1.0, 0.0)
        got = lax.dot_general(
            hot,
            arrived[j, :rows],
            (((0,), (0,)), ((), ())),
            precision=HIGHEST,
            preferred_element_type=F32,
        )
        taken = got if taken is None else taken + got
        squares = arrived[j, rows:] if squares is None else squares + arrived[j, rows:]
    added[...] = coef[0] * taken
    sq[...] = squares


def shards(
    blocks,
    spans,
    fluid_adjoint_in,
    fluid_source,
    velocity,
    diffusion,
    jacobian,
    wall_coefficient,
    metal_costate_prior,
    solid_source,
    conductivity,
    tile_owner,
    tile_target,
):
    p, src, vel = fluid_adjoint_in, fluid_source, velocity
    t, heat, k = metal_costate_prior, solid_source, conductivity
    fields, depth, rows, z = p.shape
    thick = t.shape[0]
    tall = rows + 2 * W
    buf = tall + 2 * B
    forward = {
        "blk": [(i, (i + 1) % blocks) for i in range(blocks)],
        "span": [(i, (i + 1) % spans) for i in range(spans)],
    }
    backward = {axis: [(j, i) for i, j in pairs] for axis, pairs in forward.items()}

    def ahead(x, axis):
        return lax.ppermute(x, axis, forward[axis])

    def behind(x, axis):
        return lax.ppermute(x, axis, backward[axis])

    edges = Edges(fields, depth, thick)
    inputs = [p, src, vel, t, heat, k]
    p, src, vel, t, heat, k, yf, yb, xf, zf, zb = call(
        functools.partial(early_kernel, edges),
        held(*[x.shape for x in inputs])
        + [(edges.size, z)] * 2
        + [((fields + 16) * rows, z)]
        + [(edges.solid_size, z)] * 2,
        [pltpu.SemaphoreType.DMA((6,))],
        [HBM] * 6,
        *[pltpu.with_memory_space_constraint(x, pltpu.HBM) for x in inputs],
    )
    yl, yr = ahead(yf, "span"), behind(yb, "span")
    xe = ahead(xf, "blk")
    sent_ahead = Arrivals((fields + 11) * 2 * W, rows, fields, (2, 1, 0))
    (out,) = call(
        functools.partial(ahead_kernel, blocks, spans, edges),
        [(sent_ahead.size(), z)],
        [(fields, 4, buf, z), (fields, 3, buf, z), (fields, 2, buf, z), (fields, 3, buf, z)]
        + [(3, 3, buf, z), (fields, 3, buf, z)],
        [SMEM] * 2 + [VMEM] * 5,
        diffusion,
        jacobian,
        p,
        src,
        vel,
        yl,
        yr,
        cost=COSTS[1],
    )
    xn = ahead(out, "blk")
    full = (fields, depth, buf, z)
    part = [(fields, depth - 2 * (level + 1), buf, z) for level in range(3)]
    solid = (thick, buf, z)
    p0, s0, v0, w0, p1, p2, p3, place, meta, idx = call(
        functools.partial(inner_kernel, blocks, spans, edges),
        held(full, full, (3, depth, buf, z), full, *part)
        + held((blocks * CHUNK, rows), (blocks, 8, z), (1, rows)),
        [],
        [SMEM] * 2 + [VMEM] * 7,
        diffusion,
        jacobian,
        tile_owner.reshape(1, rows),
        tile_target,
        p,
        src,
        vel,
        yl,
        yr,
        cost=COSTS[2],
    )
    zl, zr = ahead(zf, "span"), behind(zb, "span")
    te, he, so, ti, tb, sqi, dg, ws = call(
        functools.partial(inner_solid_kernel, blocks, spans, edges, fields),
        held(solid, solid, solid, (3, 4, buf, z), (thick - 2 * SWEEPS, rows, z), (8, z), solid, solid),
        [solid] * 4,
        [VMEM] * 5,
        t,
        heat,
        k,
        zl,
        zr,
        cost=COSTS[2],
    )
    sent_back = Arrivals(11 * tall, rows, fields, (3, 2, 1, 0))
    flat = (fields, buf, z)
    back, parts, first, sq, c2, c3, sl_ = call(
        functools.partial(cone_kernel, blocks, spans, sent_ahead),
        [(sent_back.size(), z), (blocks * CHUNK, z)]
        + held((fields, rows, z), (8, z), flat, (fields, 2, buf, z), (11, tall, z)),
        [flat] * 3 + [(3, buf, z), (fields, tall, z)] + [flat] * 2,
        [SMEM] * 2 + [VMEM] * 15,
        diffusion,
        jacobian,
        p0,
        s0,
        v0,
        w0,
        p1,
        p2,
        p3,
        te,
        he,
        so,
        xe,
        xn,
        wall_coefficient,
        place,
        meta,
        cost=COSTS[3],
    )
    xr = behind(back, "blk")
    arrived = lax.all_to_all(parts.reshape(blocks, CHUNK, z), "blk", 0, 0)
    surface, yf, yb = call(
        functools.partial(surface_kernel, blocks),
        [(2 * rows, z), (2 * W, z), (2 * W, z)],
        [],
        [VMEM],
        arrived,
    )
    yl, yr = ahead(yf, "span"), behind(yb, "span")
    gas, sqf = call(
        functools.partial(rest_kernel, blocks, spans, sent_back),
        [p.shape, (8, z)],
        [(fields, 1, buf, z), (fields, 2, buf, z), (fields, 4, buf, z)],
        [SMEM] * 2 + [VMEM] * 13,
        diffusion,
        jacobian,
        p0,
        s0,
        v0,
        w0,
        p1,
        p2,
        p3,
        c2,
        c3,
        first,
        sq,
        xr,
        yf,
        cost=COSTS[4],
    )
    outer, edge = (8, buf, z), (2, 5, buf, z)
    tb, rb, sqs, rh, rd, rw = call(
        functools.partial(solid_kernel, blocks, spans),
        held(t.shape, (7, rows, z), (8, z), edge, edge, edge),
        [outer] * 5 + [(6, buf, z)] * 4,
        [VMEM] * 11,
        te,
        he,
        so,
        ti,
        tb,
        sqi,
        dg,
        ws,
        sl_,
        xr,
        yf,
        cost=COSTS[5],
    )
    region = (2, 7, buf, z)
    t, out = call(
        functools.partial(response_kernel, blocks, spans, fields),
        [t.shape, (blocks, rows + 8, z)],
        [region] * 3 + [(2, buf, z)],
        [VMEM] * 10,
        surface,
        yl,
        yr,
        rh,
        rd,
        rw,
        tb,
        rb,
        sqf,
        sqs,
    )
    arrived = lax.all_to_all(out, "blk", 0, 0)
    added, sq = call(
        functools.partial(return_kernel, blocks),
        [(rows, z), (8, z)],
        [],
        [VMEM] * 3,
        arrived,
        idx,
        wall_coefficient,
    )
    step = 1
    while step < spans:
        sq = sq + lax.ppermute(sq, "span", [(i, i ^ step) for i in range(spans)])
        step = step * 2
    gas = gas.at[fields - 1, 0].add(added)
    everyone = blocks * spans
    counts = [float(depth * rows * z * everyone)] * fields + [float(thick * rows * z * everyone)]
    totals = jnp.sum(sq[: fields + 1], axis=1)
    norms = jnp.sqrt(totals / jnp.array(counts, F32))
    return gas, t, norms


def solution(mesh):
    placed = (
        P(None, "blk", "span", None),
        P(None, "blk", "span", None),
        P(None, "blk", "span", None),
        P(),
        P(),
        P("blk", "span", None),
        P("blk", "span", None),
        P("blk", "span", None),
        P("blk", "span", None),
        P("span", "blk", None),
        P("span", "blk"),
    )
    return jax.shard_map(
        functools.partial(shards, mesh.shape["blk"], mesh.shape["span"]),
        mesh=mesh,
        in_specs=placed,
        out_specs=(P(None, "blk", "span", None), P("blk", "span", None), P()),
        check_vma=False,
    )
```

```python
import functools

import jax
import jax.numpy as jnp
from jax import lax
from jax.experimental import pallas as pl
from jax.experimental.pallas import tpu as pltpu
from jax.sharding import PartitionSpec as P

SWEEPS = 4
DAMPING = 0.8
HIGHEST = lax.Precision.HIGHEST
F32 = jnp.float32
VMEM = pl.BlockSpec(memory_space=pltpu.VMEM)
SMEM = pl.BlockSpec(memory_space=pltpu.SMEM)
HBM = pl.BlockSpec(memory_space=pltpu.HBM)
COSTS = (1.0, 30.0, 0.01, 2.0, 3.0, 3.0)
LIMIT = 12 * 1024 * 1024
W = 4
CAP = 12
CHUNK = 32
B = 8


def held(*shapes):
    return [pltpu.VMEM(s, F32) for s in shapes]


def call(kernel, outs, scratch, specs, *args, cost=1.0):
    return pl.pallas_call(
        kernel,
        out_shape=[jax.ShapeDtypeStruct(s, F32) if isinstance(s, tuple) else s for s in outs],
        in_specs=specs,
        out_specs=[VMEM] * len(outs),
        scratch_shapes=[pltpu.VMEM(s, F32) if isinstance(s, tuple) else s for s in scratch],
        compiler_params=pltpu.CompilerParams(vmem_limit_bytes=LIMIT),
        cost_estimate=pl.CostEstimate(
            flops=int(cost * 1e6), bytes_accessed=int(cost * 3e6), transcendentals=0
        ),
    )(*args)


def beside(x):
    lane = lax.broadcasted_iota(jnp.int32, x.shape, 1)
    last = x.shape[1] - 1
    before = jnp.where(lane == 0, 0.0, pltpu.roll(x, 1, 1))
    after = jnp.where(lane == last, 0.0, pltpu.roll(x, last, 1))
    return before, after


def unless(flag, x):
    return jnp.where(flag, 0.0, x)


class Place:
    def __init__(self, rows, blocks, spans):
        b, s = lax.axis_index("blk"), lax.axis_index("span")
        self.rows, self.tall = rows, rows + 2 * W
        self.no_left, self.no_right = b == 0, b == blocks - 1
        self.no_low, self.no_high = s == 0, s == spans - 1
        self.ext = slice(B, B + self.tall)
        self.own = slice(B + W, B + W + rows)
        self.low = slice(B, B + W)
        self.high = slice(B + W + rows, B + self.tall)

    def reach(self, by):
        return slice(B + W - by, B + W + self.rows + by)

    def fill(self, store, own, low, high, hide=None):
        no_low, no_high = self.no_low, self.no_high
        if hide is not None:
            own, no_low, no_high = unless(hide, own), no_low | hide, no_high | hide
        store(self.own, own)
        store(slice(self.low.stop - low.shape[0], self.low.stop), unless(no_low, low))
        store(slice(self.high.start, self.high.start + high.shape[0]), unless(no_high, high))

    def inside(self, z):
        row = lax.broadcasted_iota(jnp.int32, (self.tall, z), 0)
        out = ((row < W) & self.no_low) | ((row >= W + self.rows) & self.no_high)
        return jnp.logical_not(out)


def beyond(sl, by):
    return slice(sl.start + by, sl.stop + by)


def rows_at(ref, n, count):
    return ref[n : n + count]


class Arrivals:
    def __init__(self, first, rows, fields, reaches):
        self.first, self.rows, self.fields, self.reaches = first, rows, fields, reaches

    def window(self, level, f, ext=True):
        n = self.first
        for reach in self.reaches[:level]:
            n = n + self.fields * (self.rows + 2 * reach)
        reach = self.reaches[level]
        n = n + f * (self.rows + 2 * reach)
        if ext:
            return slice(n + reach - W, n + reach + W + self.rows)
        return slice(n + reach, n + reach + self.rows)

    def size(self):
        return self.first + sum(self.fields * (self.rows + 2 * reach) for reach in self.reaches)


class Edges:
    def __init__(self, fields, depth, thick):
        n = 0
        self.fluid, self.outer, self.solid = {}, {}, {}
        for name, count, reach in (("p", fields, W), ("src", fields, W - 1), ("vel", 3, W - 1)):
            for f in range(count):
                for i in range(depth):
                    self.fluid[name, f, i] = slice(n, n + reach)
                    n = n + reach
        for name, near, reach in (("t", 3, W), ("k", 3, W), ("heat", 2, W - 1)):
            for i in range(thick - near, thick):
                self.outer[name, i] = slice(n, n + reach)
                n = n + reach
        self.size = (n + 7) // 8 * 8
        n = 0
        for name, reach in (("t", W), ("k", W), ("heat", W - 1)):
            for i in range(thick):
                self.solid[name, i] = slice(n, n + reach)
                n = n + reach
        self.solid_size = (n + 7) // 8 * 8


class Fluid:
    def __init__(self, spread, jacobian, fields):
        self.n = fields
        self.d = [spread[f] for f in range(fields)]
        self.jac = [[jacobian[f, g] for g in range(fields)] for f in range(fields)]

    def diagonal(self, f, us):
        return us + (6.0 * self.d[f] + self.jac[f][f])

    def advance(self, cur, left, right, vel, w, src, rows, store):
        for n in range(rows.start, rows.stop, 8):
            sl = slice(n, n + 8)
            u0, u1, u2 = (u(sl) for u in vel)
            us = u0 + u1 + u2
            centre = [cur(f, sl) for f in range(self.n)]
            for f in range(self.n):
                c = centre[f]
                zm, zp = beside(c)
                yp = cur(f, beyond(sl, 1))
                near = (cur(f, beyond(sl, -1)) + yp) + (zm + zp)
                if left is not None:
                    near = near + left(f, sl)
                res = u1 * yp + u2 * zp - self.diagonal(f, us) * c
                if right is not None:
                    xp = right(f, sl)
                    near = near + xp
                    res = res + u0 * xp
                res = res + self.d[f] * near
                for g in range(self.n):
                    if g != f:
                        res = res - self.jac[f][g] * centre[g]
                if src is not None:
                    res = res + src(f, sl)
                store(f, sl, res, c + w(f, sl) * res)


def at(ref, i):
    return lambda f, sl: ref[f, i, sl]


def flat(ref):
    return lambda f, sl: ref[f, sl]


def speeds(ref, i):
    return [lambda sl, c=c: ref[c, i, sl] for c in range(3)]


def into(ref, i):
    def store(f, sl, _, value):
        ref[f, i, sl] = value

    return store


def into_flat(ref):
    def store(f, sl, _, value):
        ref[f, sl] = value

    return store


def early_kernel(edges, *refs):
    bufs = refs[6:12]
    yf, yb, xf, zf, zb, sems = refs[12:]
    copies = [
        pltpu.make_async_copy(ref, buf, sems.at[j])
        for j, (ref, buf) in enumerate(zip(refs[:6], bufs, strict=True))
    ]
    for copy in copies:
        copy.start()
    for copy in copies:
        copy.wait()
    p, src, vel, t, heat, k = bufs
    fields, depth, rows = p.shape[0], p.shape[1], p.shape[2]
    thick = t.shape[0]
    named = {"p": p, "src": src, "vel": vel, "t": t, "heat": heat, "k": k}
    planes = [p[f, depth - 1] for f in range(fields)]
    planes += [vel[f, depth - 1] for f in range(3)]
    planes += [vel[0, depth - 2], vel[0, depth - 2] + vel[1, depth - 2] + vel[2, depth - 2]]
    planes += [t[thick - 4 + j] for j in range(4)]
    planes += [k[thick - 4 + j] for j in range(4)]
    planes += [heat[thick - 3 + j] for j in range(3)]
    for j, plane in enumerate(planes):
        xf[j * rows : (j + 1) * rows] = plane
    for up, down, places in ((yf, yb, edges.fluid), (yf, yb, edges.outer), (zf, zb, edges.solid)):
        for (name, *at_plane), sl in places.items():
            ref, reach = named[name], sl.stop - sl.start
            up[sl] = ref[*at_plane, rows - reach :]
            down[sl] = ref[*at_plane, :reach]


def ahead_kernel(blocks, spans, edges, spread, jacobian, p, src, vel, yl, yr, out, a0, a1, a2, sa, va, wa):
    fields, depth, rows, z = p.shape
    at_place = Place(rows, blocks, spans)
    ext, own = at_place.ext, at_place.own
    fluid = Fluid(spread, jacobian, fields)
    inside = at_place.inside(z)

    def fill(buf, f, j, ref, name, i):
        def store(sl, x):
            buf[f, j, sl] = x

        sl = edges.fluid[name, f, i]
        at_place.fill(store, ref[f, i], yl[sl], yr[sl])

    for f in range(fields):
        for j in range(4):
            fill(a0, f, j, p, "p", depth - 4 + j)
        for j in range(3):
            fill(sa, f, j, src, "src", depth - 3 + j)
    for f in range(3):
        for j in range(3):
            fill(va, f, j, vel, "vel", depth - 3 + j)
    for j in range(3):
        us = va[0, j, ext] + va[1, j, ext] + va[2, j, ext]
        for f in range(fields):
            wa[f, j, ext] = jnp.where(inside, DAMPING / fluid.diagonal(f, us), 0.0)

    def step(old, i, store, j):
        fluid.advance(
            at(old, i),
            at(old, i - 1),
            None if j == 2 else at(old, i + 1),
            speeds(va, j),
            at(wa, j),
            at(sa, j),
            ext,
            store,
        )

    for j in range(3):
        step(a0, j + 1, into(a1, j), j)
    for j in range(1, 3):
        step(a1, j, into(a2, j - 1), j)
    corners = [edges.fluid["p", f, depth - 1] for f in range(fields)]
    corners += [edges.fluid["vel", c, depth - 1] for c in range(3)]
    corners += list(edges.outer.values())
    n = 0
    for sl in corners:
        reach = sl.stop - sl.start
        out[n + W - reach : n + W] = yl[sl]
        out[n + W : n + W + reach] = yr[sl]
        n = n + 2 * W
    for reach, buf, j in ((2, a1, 2), (1, a2, 1)):
        size = rows + 2 * reach
        for f in range(fields):
            out[n : n + size] = buf[f, j, at_place.reach(reach)]
            n = n + size

    def last(f, sl, _, value):
        m = n + f * rows + sl.start - own.start
        out[m : m + 8] = value

    fluid.advance(
        at(a2, 1), at(a2, 0), None, speeds(va, 2), at(wa, 2), at(sa, 2), own, last
    )


def around(buf, j, sl):
    zm, zp = beside(buf[j, sl])
    return (
        (buf[j - 1, sl] + buf[j + 1, sl])
        + (buf[j, beyond(sl, -1)] + buf[j, beyond(sl, 1)])
        + (zm + zp)
    )


def solid_diagonal(h_of, i, sl):
    zm, zp = beside(h_of(i, sl))
    near = (h_of(i - 1, sl) + h_of(i + 1, sl)) + (zm + zp)
    near = near + (h_of(i, beyond(sl, -1)) + h_of(i, beyond(sl, 1)))
    return 6.0 * h_of(i, sl) + near


def solid_weight(h, diagonal):
    return jnp.where(h > 0.0, DAMPING / jnp.where(h > 0.0, diagonal, 1.0), 0.0)


def plan(blocks, owner, target, place, meta, idx):
    rows = target.shape[1]
    me = lax.axis_index("blk")
    row = lax.broadcasted_iota(jnp.int32, (rows, rows), 0)
    lane = lax.broadcasted_iota(jnp.int32, (rows, rows), 1)
    owner = owner[...].astype(F32)
    column = jnp.where(row == lane, jnp.broadcast_to(owner, (rows, rows)), 0.0)
    column = jnp.sum(column, axis=1, keepdims=True)
    idx[...] = owner * rows + target[...].astype(F32)
    before = jnp.where((column == owner) & (row < lane), 1.0, 0.0)
    rank = jnp.sum(before, axis=0, keepdims=True)
    n = lax.broadcasted_iota(jnp.int32, (blocks * CHUNK, rows), 0)
    slot = n % CHUNK
    second = slot >= CAP
    named = n // CHUNK - jnp.where(second, 0, 1)
    at_rank = (slot - jnp.where(second, CAP, 0)).astype(F32)
    hot = jnp.where((owner == named.astype(F32)) & (rank == at_rank), 1.0, 0.0)
    hot = jnp.where(slot < 2 * CAP, hot, 0.0)
    place[...] = hot
    targets = jnp.broadcast_to((target[...] + 1).astype(F32), (8, rows))
    lanes = lax.dot_general(
        targets, hot, (((1,), (1,)), ((), ())), precision=HIGHEST, preferred_element_type=F32
    )
    row = lax.broadcasted_iota(jnp.int32, (8, 4 * CHUNK), 0)
    lane = lax.broadcasted_iota(jnp.int32, (8, 4 * CHUNK), 1)
    for j in range(blocks):
        group = lanes[:, j // 4 * 4 * CHUNK : (j // 4 + 1) * 4 * CHUNK]
        group = jnp.where(lane // CHUNK == j % 4, group, 0.0)
        group = pltpu.roll(group, lax.rem(me - j + 4 * blocks, 4) * CHUNK, 1)
        meta[j] = jnp.where(row == me // 4, group, 0.0)


def inner_kernel(
    blocks, spans, edges, spread, jacobian, owner, target, p, src, vel, yl, yr, *outs
):
    p0, s0, v0, w0, p1, p2, p3, place, meta, idx = outs
    plan(blocks, owner, target, place, meta, idx)
    fields, depth, rows, z = p.shape
    here = Place(rows, blocks, spans)
    ext = here.ext
    fluid = Fluid(spread, jacobian, fields)
    inside = here.inside(z)
    for name, buf, ref in (("p", p0, p), ("src", s0, src), ("vel", v0, vel)):
        for f in range(ref.shape[0]):
            for i in range(depth):

                def store(sl, x, buf=buf, f=f, i=i):
                    buf[f, i, sl] = x

                sl = edges.fluid[name, f, i]
                here.fill(store, ref[f, i], yl[sl], yr[sl])
    for i in range(depth):
        us = v0[0, i, ext] + v0[1, i, ext] + v0[2, i, ext]
        for f in range(fields):
            w0[f, i, ext] = jnp.where(inside, DAMPING / fluid.diagonal(f, us), 0.0)
    for level, (old, new) in enumerate(((p0, p1), (p1, p2), (p2, p3))):
        for i in range(level + 1, depth - 1 - level):
            fluid.advance(
                at(old, i - level),
                at(old, i - level - 1),
                at(old, i - level + 1),
                speeds(v0, i),
                at(w0, i),
                at(s0, i),
                ext,
                into(new, i - level - 1),
            )


def inner_solid_kernel(blocks, spans, edges, fields, t, heat, k, yl, yr, _, *refs):
    te, he, so, ti, tb, sqi, dg, ws, ta, tc, qa, qc = refs
    thick, rows, z = t.shape
    here = Place(rows, blocks, spans)
    ext = here.ext
    for name, buf, ref, scale in (("t", te, t, 1.0), ("k", he, k, 0.5), ("heat", so, heat, 1.0)):
        for i in range(thick):

            def store(sl, x, buf=buf, i=i, scale=scale):
                buf[i, sl] = scale * x

            sl = edges.solid[name, i]
            here.fill(store, ref[i], yl[sl], yr[sl])
    for i in range(1, thick - 1):
        h = he[i, ext]
        diagonal = 6.0 * h + around(he, i, ext)
        dg[i, ext] = diagonal
        ws[i, ext] = solid_weight(h, diagonal)
    for i in range(thick):
        qa[i, ext] = he[i, ext] * te[i, ext]
    old, oldq, new, newq = te, qa, ta, qc
    total = None
    for level in range(SWEEPS):
        last = level == SWEEPS - 1
        sl = here.own if last else ext
        for i in range(level + 1, thick - 1 - level):
            h, q = he[i, sl], old[i, sl]
            res = so[i, sl] - dg[i, sl] * q + h * around(old, i, sl) + around(oldq, i, sl)
            value = q + ws[i, sl] * res
            if last:
                tb[i - SWEEPS] = value
                square = res * res
                total = square if total is None else total + square
            else:
                new[i, sl] = value
                newq[i, sl] = h * value
        if not last:
            one = level + 1
            for j, i in enumerate((one, one + 1, thick - 2 - one, thick - 1 - one)):
                ti[level, j] = new[i]
            old, new = new, (tc if new is ta else ta)
            oldq, newq = newq, oldq
    sqi[...] = jnp.zeros_like(sqi)
    sqi[fields : fields + 1] = jnp.sum(total, axis=0, keepdims=True)


def cone_kernel(blocks, spans, sent, spread, jacobian, *refs):
    p0, s0, v0, w0, p1, p2, _, te, he, so, ti, dg, ws, xe, xn, coef, hot, meta = refs[:18]
    back, parts, first, sq, c2, c3, sl_, t0, t1, t2, t3, dl, wl = refs[18:31]
    l0, d1, d2, d3, vm, wm, n1, n2, qa = refs[31:]
    fields = p0.shape[0]
    rows, z = coef.shape[1], coef.shape[2]
    here = Place(rows, blocks, spans)
    ext, own, tall = here.ext, here.own, here.tall
    fluid = Fluid(spread, jacobian, fields)
    inside = jnp.logical_and(here.inside(z), jnp.logical_not(here.no_left))
    corner = 0
    for f in range(fields):

        def store(sl, x, f=f):
            l0[f, sl] = x

        n = corner + f * 2 * W
        here.fill(
            store, xe[f * rows : (f + 1) * rows], xn[n : n + W], xn[n + W : n + 2 * W], here.no_left
        )
    for c in range(3):

        def store(sl, x, c=c):
            vm[c, sl] = x

        n = corner + (fields + c) * 2 * W
        m = (fields + c) * rows
        here.fill(store, xe[m : m + rows], xn[n : n + W], xn[n + W : n + 2 * W])
    um = [vm[c, ext] for c in range(3)]
    usm = um[0] + um[1] + um[2]
    for f in range(fields):
        wm[f, ext] = jnp.where(inside, DAMPING / fluid.diagonal(f, usm), 0.0)
    m = (fields + 3) * rows
    u0mm, usmm = xe[m : m + rows], xe[m + rows : m + 2 * rows]

    def sum_of(level, ref):
        def read(f, sl):
            n = sent.window(level - 1, f).start + sl.start - B
            return unless(here.no_left, xn[n : n + 8]) + ref[f, sl]

        return read

    def plane(cur, i, left, right, store, sl=ext):
        fluid.advance(cur, left, right, speeds(v0, i), at(w0, i), at(s0, i), sl, store)

    outer = [lambda sl, c=c: vm[c, sl] for c in range(3)]
    plane(at(p0, 0), 0, flat(l0), at(p0, 1), into_flat(n1))
    for f in range(fields):
        d1[f, ext] = wm[f, ext] * (fluid.d[f] + um[0]) * p0[f, 0, ext]
    plane(flat(n1), 0, sum_of(1, d1), at(p1, 0), into_flat(n2))
    plane(at(p1, 0), 1, flat(n1), at(p1, 1), into_flat(c2))
    fluid.advance(flat(d1), None, flat(n1), outer, flat(wm), None, ext, into_flat(d2))
    plane(flat(n2), 0, sum_of(2, d2), flat(c2), into(c3, 0))
    plane(flat(c2), 1, flat(n2), at(p2, 0), into(c3, 1))

    def farther(f, sl):
        n = sl.start - own.start
        w = unless(here.no_left, DAMPING / fluid.diagonal(f, usmm[n : n + 8]))
        return w * (fluid.d[f] + u0mm[n : n + 8]) * d1[f, sl]

    fluid.advance(flat(d2), farther, flat(n2), outer, flat(wm), None, own, into_flat(d3))
    sq[...] = jnp.zeros_like(sq)
    squares = [None] * fields

    def final(f, sl, res, value):
        first[f, sl.start - own.start : sl.stop - own.start] = value
        square = res * res
        squares[f] = square if squares[f] is None else squares[f] + square

    plane(at(c3, 0), 0, sum_of(3, d3), at(c3, 1), final, own)
    for f in range(fields):
        sq[f : f + 1] = jnp.sum(squares[f], axis=0, keepdims=True)
    flux = coef[0] * first[fields - 1]
    parts[...] = jnp.dot(hot[...], flux, precision=HIGHEST, preferred_element_type=F32)
    for j in range(blocks):
        parts[j * CHUNK + 2 * CAP : (j + 1) * CHUNK] = meta[j]
    n = 6 * tall
    for reach, read in (
        (3, at(p0, 0)),
        (2, flat(n1)),
        (1, flat(n2)),
        (0, at(c3, 0)),
    ):
        size = rows + 2 * reach
        for f in range(fields):
            back[n : n + size] = read(f, here.reach(reach))
            n = n + size
    corner = corner + (fields + 3) * 2 * W
    early = (fields + 5) * rows
    zero = jnp.zeros((W, z), F32)
    hl, sl_ = sl_.at[0], sl_.at[1]
    for buf, near, scale in ((t0, 4, 1.0), (hl, 4, 0.5), (sl_, 3, 1.0)):
        for i in range(near):

            def store(sl, x, buf=buf, j=4 - near + i, scale=scale):
                buf[j, sl] = scale * x

            if i > 0:
                low, high = xn[corner : corner + W], xn[corner + W : corner + 2 * W]
                corner = corner + 2 * W
            else:
                low, high = zero, zero
            here.fill(store, xe[early : early + rows], low, high, here.no_left)
            early = early + rows

    def h_of(i, sl):
        return hl[i + 4, sl] if i < 0 else he[i, sl]

    for i in range(-3, 1):
        dl[i + 3, ext] = solid_diagonal(h_of, i, ext)
        wl[i + 3, ext] = solid_weight(h_of(i, ext), dl[i + 3, ext])
    for j in range(4, 6):
        t0[j] = te[j - 4]
    for level, (old, new) in enumerate(((t0, t1), (t1, t2), (t2, t3))):
        for j in range(6):
            qa[j, ext] = h_of(level - 4 + j, ext) * old[j, ext]
        for j in range(4):
            i = level - 3 + j
            q = old[j + 1, ext]
            res = sl_[i + 4, ext] if i < 0 else so[i, ext]
            diagonal, w = (dl, wl) if i <= 0 else (dg, ws)
            m = i + 3 if i <= 0 else i
            res = res - diagonal[m, ext] * q
            res = res + h_of(i, ext) * around(old, j + 1, ext) + around(qa, j + 1, ext)
            new[j, ext] = q + w[m, ext] * res
        for j in range(4, 6):
            new[j] = ti[level, j - 4]
    n = 0
    for ref, i in ((he, 0), (he, 1), (t0, 4), (t1, 3)):
        back[n : n + tall] = ref[i, ext]
        n = n + tall
    for ref, i in ((t2, 2), (t3, 1)):
        back[n : n + tall] = ref[i, ext]
        n = n + tall


def rest_kernel(blocks, spans, sent, spread, jacobian, *refs):
    p0, s0, v0, w0, p1, p2, p3, c2, c3, first, sqb, xn, _, gas, sq, n1, n2, n3 = refs
    fields, depth = gas.shape[0], gas.shape[1]
    rows = gas.shape[2]
    here = Place(rows, blocks, spans)
    ext, own, tall = here.ext, here.own, here.tall
    fluid = Fluid(spread, jacobian, fields)
    def arrived(level):
        def read(f, sl):
            n = sent.window(level, f).start + sl.start - B
            return unless(here.no_right, xn[n : n + 8])

        return read

    known = [{i: (p0, i) for i in range(depth)}, {}, {}, {}]
    for level, buf in enumerate((p1, p2, p3)):
        for i in range(level + 1, depth - 1 - level):
            known[level + 1][i] = (buf, i - level - 1)
    known[2][1], known[3][0], known[3][1] = (c2, None), (c3, 0), (c3, 1)

    def read(level, i):
        ref, j = known[level][i]
        return (lambda f, sl: ref[f, sl]) if j is None else (lambda f, sl: ref[f, j, sl])

    def plane(level, i, store, sl=ext):
        fluid.advance(
            read(level, i),
            read(level, i - 1),
            read(level, i + 1) if i < depth - 1 else arrived(level),
            speeds(v0, i),
            at(w0, i),
            at(s0, i),
            sl,
            store,
        )

    todo = ((depth - 1,), (depth - 2, depth - 1), (2, depth - 3, depth - 2, depth - 1))
    for level, new in enumerate((n1, n2, n3)):
        for j, i in enumerate(todo[level]):
            plane(level, i, into(new, j))
            known[level + 1][i] = (new, j)
    total = [None] * fields
    for f in range(fields):
        gas[f, 0] = first[f]
    for i in range(1, depth):

        def final(f, sl, res, value, i=i):
            gas[f, i, sl.start - own.start : sl.stop - own.start] = value
            square = res * res
            total[f] = square if total[f] is None else total[f] + square

        plane(3, i, final, own)
    sq[...] = sqb[...]
    for f in range(fields):
        sq[f : f + 1] = sq[f : f + 1] + jnp.sum(total[f], axis=0, keepdims=True)


def solid_kernel(
    blocks, spans, te, he, so, ti, tbi, sqi, dg, ws, sl_, tl0, tl1, tl2, tl3, dl, wl, xb, _, *refs
):
    tb, rb, sq, rh, rd, rw = refs[:6]
    hr, dr, wr, ta, tc, qa = refs[6:]
    thick, rows, z = tb.shape
    here = Place(rows, blocks, spans)
    ext, own, tall = here.ext, here.own, here.tall
    hl = sl_.at[0]

    def arrived(n):
        return unless(here.no_right, xb[n * tall : (n + 1) * tall])

    for j in range(2):
        hr[j, ext] = arrived(j)

    def h_of(i, sl):
        if i < 0:
            return hl[i + 4, sl]
        return he[i, sl] if i < thick else hr[i - thick, sl]

    for j in range(2):
        i = thick - 1 + j
        dr[j, ext] = solid_diagonal(h_of, i, ext)
        wr[j, ext] = solid_weight(h_of(i, ext), dr[j, ext])

    def d_of(left, inside, right, i, sl):
        if i <= 0:
            return left[i + 3, sl]
        return inside[i, sl] if i < thick - 1 else right[i - thick + 1, sl]

    def residual(old, j, i, sl):
        res = so[i, sl] - d_of(dl, dg, dr, i, sl) * old[j, sl]
        return res + h_of(i, sl) * around(old, j, sl) + around(qa, j, sl)

    sums = None
    for j in range(6):
        qa[j, ext] = h_of(j - 1, ext) * tl3[j, ext]
    for i in range(4):
        res = residual(tl3, i + 1, i, own)
        tb[i] = tl3[i + 1, own] + d_of(wl, ws, wr, i, own) * res
        if i < 3:
            rb[i] = res
        else:
            sums = res * res
    old, new = ta, tc
    old[0], old[1] = te[thick - 2], te[thick - 1]
    old[2, ext] = arrived(2)
    for level in range(SWEEPS):
        last = level == SWEEPS - 1
        sl = own if last else ext
        low = thick - 2 - level
        for j in range(level + 3):
            qa[j, ext] = h_of(low + j, ext) * old[j, ext]
        for j in range(1, level + 2):
            i = low + j
            res = residual(old, j, i, sl)
            value = old[j, sl] + d_of(wl, ws, wr, i, sl) * res
            if last:
                tb[i] = value
                rb[i - (thick - 7)] = res
            else:
                new[j + 1, ext] = value
        if not last:
            for j in range(2):
                new[j] = ti[level, j + 2]
            new[level + 3, ext] = arrived(3 + level)
            old, new = new, old
    for i in range(SWEEPS, thick - SWEEPS):
        tb[i] = tbi[i - SWEEPS]
    sq[...] = sqi[...]
    n = sq.shape[0] - 3
    sq[n : n + 1] = sq[n : n + 1] + jnp.sum(sums, axis=0, keepdims=True)
    for region in range(2):
        for j in range(5):
            i = j - 2 if region == 0 else thick - 4 + j
            rh[region, j, ext] = h_of(i, ext)
            rd[region, j, ext] = d_of(dl, dg, dr, i, ext)
            rw[region, j, ext] = d_of(wl, ws, wr, i, ext)


def surface_kernel(blocks, arrived, surface, yf, yb):
    rows = surface.shape[0] // 2
    meta = arrived[0, 2 * CAP :]
    for j in range(1, blocks):
        meta = meta + arrived[j, 2 * CAP :]
    row = lax.broadcasted_iota(jnp.int32, (2 * rows, 4 * CHUNK), 0)
    slot = lax.broadcasted_iota(jnp.int32, (2 * rows, 4 * CHUNK), 1) % CHUNK
    row = row + 1 - jnp.where(slot < CAP, 0, rows)
    row = jnp.where((row >= 1) & (row <= rows), row, -1).astype(F32)
    whole = None
    for j in range(0, blocks, 4):
        sent = jnp.concatenate([arrived[j + m] for m in range(4)], axis=0)
        hot = jnp.where(row == meta[j // 4 : j // 4 + 1], 1.0, 0.0)
        got = jnp.dot(hot, sent, precision=HIGHEST, preferred_element_type=F32)
        whole = got if whole is None else whole + got
    surface[...] = whole
    yf[:W] = whole[rows - W : rows]
    yf[W:] = whole[2 * rows - W :]
    yb[:W] = whole[:W]
    yb[W:] = whole[rows : rows + W]


def response_kernel(
    blocks, spans, fields, surface, yl, yr, rh, rd, rw, tb, rb, sqf, sqs, tn, out, da, db, hd, so
):
    thick, rows, z = tb.shape
    here = Place(rows, blocks, spans)
    ext, own = here.ext, here.own
    for buf in (da, db, hd):
        buf[...] = jnp.zeros_like(buf)
    sq = sqf[...] + sqs[...]
    gained = jnp.zeros((rows, z), F32)
    for region in range(2):

        def store(sl, x, region=region):
            so[region, sl] = x

        edge = slice(region * W, (region + 1) * W)
        here.fill(store, surface[region * rows : (region + 1) * rows], yl[edge], yr[edge])

    needed = (((2,), (1, 2, 3), (1, 2, 3, 4), (3, 4, 5)), ((4,), (3, 4, 5), (2, 3, 4, 5), (1, 2, 3, 4)))
    for i in range(3, thick - 4):
        tn[i] = tb[i]
    for region in range(2):
        old, new = da, db
        source = 2 if region == 0 else 4
        for sweep in range(SWEEPS):
            final = sweep == SWEEPS - 1
            for j in needed[region][sweep]:
                res = so[region, ext] if j == source else None
                h, w = rh[region, j - 1, ext], rw[region, j - 1, ext]
                if sweep > 0:
                    q = old[region, j, ext]
                    flow = h * around(old.at[region], j, ext) + around(hd.at[region], j, ext) - rd[region, j - 1, ext] * q
                    res = flow if res is None else res + flow
                    change = q + w * res
                else:
                    change = w * res
                if final:
                    i = j - 3 if region == 0 else thick - 5 + j
                    kept = i if region == 0 else 2 + j
                    mine = slice(W, W + rows)
                    tn[i] = tb[i] + change[mine]
                    full = rb[kept] + res[mine]
                    gained = gained + full * full
                else:
                    new[region, j, ext] = change
            if not final:
                for j in needed[region][sweep]:
                    hd[region, j, ext] = rh[region, j - 1, ext] * new[region, j, ext]
                old, new = new, old
    extra = jnp.sum(gained, axis=0, keepdims=True)
    row = lax.broadcasted_iota(jnp.int32, sq.shape, 0)
    sq = sq + jnp.where(row == fields, extra, 0.0)
    for j in range(blocks):
        out[j, :rows] = tn[thick - 1]
        out[j, rows:] = sq


def return_kernel(blocks, arrived, idx, coef, added, sq):
    rows = added.shape[0]
    row = lax.broadcasted_iota(jnp.int32, (rows, rows), 0).astype(F32)
    taken, squares = None, None
    for j in range(blocks):
        hot = jnp.where(idx[...] - float(j * rows) == row, 1.0, 0.0)
        got = lax.dot_general(
            hot,
            arrived[j, :rows],
            (((0,), (0,)), ((), ())),
            precision=HIGHEST,
            preferred_element_type=F32,
        )
        taken = got if taken is None else taken + got
        squares = arrived[j, rows:] if squares is None else squares + arrived[j, rows:]
    added[...] = coef[0] * taken
    sq[...] = squares


def shards(
    blocks,
    spans,
    fluid_adjoint_in,
    fluid_source,
    velocity,
    diffusion,
    jacobian,
    wall_coefficient,
    metal_costate_prior,
    solid_source,
    conductivity,
    tile_owner,
    tile_target,
):
    p, src, vel = fluid_adjoint_in, fluid_source, velocity
    t, heat, k = metal_costate_prior, solid_source, conductivity
    fields, depth, rows, z = p.shape
    thick = t.shape[0]
    tall = rows + 2 * W
    buf = tall + 2 * B
    forward = {
        "blk": [(i, (i + 1) % blocks) for i in range(blocks)],
        "span": [(i, (i + 1) % spans) for i in range(spans)],
    }
    backward = {axis: [(j, i) for i, j in pairs] for axis, pairs in forward.items()}

    def ahead(x, axis):
        return lax.ppermute(x, axis, forward[axis])

    def behind(x, axis):
        return lax.ppermute(x, axis, backward[axis])

    edges = Edges(fields, depth, thick)
    inputs = [p, src, vel, t, heat, k]
    p, src, vel, t, heat, k, yf, yb, xf, zf, zb = call(
        functools.partial(early_kernel, edges),
        held(*[x.shape for x in inputs])
        + [(edges.size, z)] * 2
        + [((fields + 16) * rows, z)]
        + [(edges.solid_size, z)] * 2,
        [pltpu.SemaphoreType.DMA((6,))],
        [HBM] * 6,
        *[pltpu.with_memory_space_constraint(x, pltpu.HBM) for x in inputs],
    )
    yl, yr = ahead(yf, "span"), behind(yb, "span")
    xe = ahead(xf, "blk")
    sent_ahead = Arrivals((fields + 11) * 2 * W, rows, fields, (2, 1, 0))
    (out,) = call(
        functools.partial(ahead_kernel, blocks, spans, edges),
        [(sent_ahead.size(), z)],
        [(fields, 4, buf, z), (fields, 3, buf, z), (fields, 2, buf, z), (fields, 3, buf, z)]
        + [(3, 3, buf, z), (fields, 3, buf, z)],
        [SMEM] * 2 + [VMEM] * 5,
        diffusion,
        jacobian,
        p,
        src,
        vel,
        yl,
        yr,
        cost=COSTS[1],
    )
    xn = ahead(out, "blk")
    full = (fields, depth, buf, z)
    part = [(fields, depth - 2 * (level + 1), buf, z) for level in range(3)]
    solid = (thick, buf, z)
    p0, s0, v0, w0, p1, p2, p3, place, meta, idx = call(
        functools.partial(inner_kernel, blocks, spans, edges),
        held(full, full, (3, depth, buf, z), full, *part)
        + held((blocks * CHUNK, rows), (blocks, 8, z), (1, rows)),
        [],
        [SMEM] * 2 + [VMEM] * 7,
        diffusion,
        jacobian,
        tile_owner.reshape(1, rows),
        tile_target,
        p,
        src,
        vel,
        yl,
        yr,
        cost=COSTS[2],
    )
    zl, zr = ahead(zf, "span"), behind(zb, "span")
    te, he, so, ti, tb, sqi, dg, ws = call(
        functools.partial(inner_solid_kernel, blocks, spans, edges, fields),
        held(solid, solid, solid, (3, 4, buf, z), (thick - 2 * SWEEPS, rows, z), (8, z), solid, solid),
        [solid] * 4,
        [VMEM] * 6,
        t,
        heat,
        k,
        zl,
        zr,
        idx,
        cost=COSTS[2],
    )
    sent_back = Arrivals(6 * tall, rows, fields, (3, 2, 1, 0))
    one, six = (fields, buf, z), (6, buf, z)
    back, parts, first, sq, c2, c3, sl_, *lefts = call(
        functools.partial(cone_kernel, blocks, spans, sent_ahead),
        [(sent_back.size(), z), (blocks * CHUNK, z)]
        + held((fields, rows, z), (8, z), one, (fields, 2, buf, z), (2, 4, buf, z))
        + held(six, six, six, six, (4, buf, z), (4, buf, z)),
        [one] * 4 + [(3, buf, z)] + [one] * 3 + [six],
        [SMEM] * 2 + [VMEM] * 18,
        diffusion,
        jacobian,
        p0,
        s0,
        v0,
        w0,
        p1,
        p2,
        p3,
        te,
        he,
        so,
        ti,
        dg,
        ws,
        xe,
        xn,
        wall_coefficient,
        place,
        meta,
        cost=COSTS[3],
    )
    xr = behind(back, "blk")
    arrived = lax.all_to_all(parts.reshape(blocks, CHUNK, z), "blk", 0, 0)
    surface, yf, yb = call(
        functools.partial(surface_kernel, blocks),
        [(2 * rows, z), (2 * W, z), (2 * W, z)],
        [],
        [VMEM],
        arrived,
    )
    yl, yr = ahead(yf, "span"), behind(yb, "span")
    gas, sqf = call(
        functools.partial(rest_kernel, blocks, spans, sent_back),
        held(p.shape, (8, z)),
        [(fields, 1, buf, z), (fields, 2, buf, z), (fields, 4, buf, z)],
        [SMEM] * 2 + [VMEM] * 13,
        diffusion,
        jacobian,
        p0,
        s0,
        v0,
        w0,
        p1,
        p2,
        p3,
        c2,
        c3,
        first,
        sq,
        xr,
        yf,
        cost=COSTS[4],
    )
    two, edge = (2, buf, z), (2, 5, buf, z)
    tb, rb, sqs, rh, rd, rw = call(
        functools.partial(solid_kernel, blocks, spans),
        held(t.shape, (7, rows, z), (8, z), edge, edge, edge),
        [two] * 3 + [six] * 3,
        [VMEM] * 17,
        te,
        he,
        so,
        ti,
        tb,
        sqi,
        dg,
        ws,
        sl_,
        *lefts,
        xr,
        yf,
        cost=COSTS[5],
    )
    region = (2, 7, buf, z)
    t, out = call(
        functools.partial(response_kernel, blocks, spans, fields),
        held(t.shape, (blocks, rows + 8, z)),
        [region] * 3 + [(2, buf, z)],
        [VMEM] * 10,
        surface,
        yl,
        yr,
        rh,
        rd,
        rw,
        tb,
        rb,
        sqf,
        sqs,
    )
    arrived = lax.all_to_all(out, "blk", 0, 0)
    added, sq = call(
        functools.partial(return_kernel, blocks),
        [(rows, z), (8, z)],
        [],
        [VMEM] * 3,
        arrived,
        idx,
        wall_coefficient,
    )
    step = 1
    while step < spans:
        sq = sq + lax.ppermute(sq, "span", [(i, i ^ step) for i in range(spans)])
        step = step * 2
    gas = gas.at[fields - 1, 0].add(added)
    everyone = blocks * spans
    counts = [float(depth * rows * z * everyone)] * fields + [float(thick * rows * z * everyone)]
    totals = jnp.sum(sq[: fields + 1], axis=1)
    norms = jnp.sqrt(totals / jnp.array(counts, F32))
    return gas, t, norms


def solution(mesh):
    placed = (
        P(None, "blk", "span", None),
        P(None, "blk", "span", None),
        P(None, "blk", "span", None),
        P(),
        P(),
        P("blk", "span", None),
        P("blk", "span", None),
        P("blk", "span", None),
        P("blk", "span", None),
        P("span", "blk", None),
        P("span", "blk"),
    )
    return jax.shard_map(
        functools.partial(shards, mesh.shape["blk"], mesh.shape["span"]),
        mesh=mesh,
        in_specs=placed,
        out_specs=(P(None, "blk", "span", None), P("blk", "span", None), P()),
        check_vma=False,
    )
```

```python
import functools

import jax
import jax.numpy as jnp
from jax import lax
from jax.experimental import pallas as pl
from jax.experimental.pallas import tpu as pltpu
from jax.sharding import PartitionSpec as P

SWEEPS = 4
DAMPING = 0.8
HIGHEST = lax.Precision.HIGHEST
F32 = jnp.float32
VMEM = pl.BlockSpec(memory_space=pltpu.VMEM)
SMEM = pl.BlockSpec(memory_space=pltpu.SMEM)
HBM = pl.BlockSpec(memory_space=pltpu.HBM)
COSTS = (1.0, 30.0, 0.01, 2.0, 3.0, 3.0)
LIMIT = 12 * 1024 * 1024
W = 4
CAP = 12
CHUNK = 32
B = 8


def held(*shapes):
    return [pltpu.VMEM(s, F32) for s in shapes]


def call(kernel, outs, scratch, specs, *args, cost=1.0):
    return pl.pallas_call(
        kernel,
        out_shape=[jax.ShapeDtypeStruct(s, F32) if isinstance(s, tuple) else s for s in outs],
        in_specs=specs,
        out_specs=[VMEM] * len(outs),
        scratch_shapes=[pltpu.VMEM(s, F32) if isinstance(s, tuple) else s for s in scratch],
        compiler_params=pltpu.CompilerParams(vmem_limit_bytes=LIMIT),
        cost_estimate=pl.CostEstimate(
            flops=int(cost * 1e6), bytes_accessed=int(cost * 3e6), transcendentals=0
        ),
    )(*args)


def beside(x):
    lane = lax.broadcasted_iota(jnp.int32, x.shape, 1)
    last = x.shape[1] - 1
    before = jnp.where(lane == 0, 0.0, pltpu.roll(x, 1, 1))
    after = jnp.where(lane == last, 0.0, pltpu.roll(x, last, 1))
    return before, after


def unless(flag, x):
    return jnp.where(flag, 0.0, x)


class Place:
    def __init__(self, rows, blocks, spans):
        b, s = lax.axis_index("blk"), lax.axis_index("span")
        self.rows, self.tall = rows, rows + 2 * W
        self.no_left, self.no_right = b == 0, b == blocks - 1
        self.no_low, self.no_high = s == 0, s == spans - 1
        self.ext = slice(B, B + self.tall)
        self.own = slice(B + W, B + W + rows)
        self.low = slice(B, B + W)
        self.high = slice(B + W + rows, B + self.tall)

    def reach(self, by):
        return slice(B + W - by, B + W + self.rows + by)

    def fill(self, store, own, low, high, hide=None):
        no_low, no_high = self.no_low, self.no_high
        if hide is not None:
            own, no_low, no_high = unless(hide, own), no_low | hide, no_high | hide
        store(self.own, own)
        store(slice(self.low.stop - low.shape[0], self.low.stop), unless(no_low, low))
        store(slice(self.high.start, self.high.start + high.shape[0]), unless(no_high, high))

    def inside(self, z):
        row = lax.broadcasted_iota(jnp.int32, (self.tall, z), 0)
        out = ((row < W) & self.no_low) | ((row >= W + self.rows) & self.no_high)
        return jnp.logical_not(out)


def beyond(sl, by):
    return slice(sl.start + by, sl.stop + by)


def rows_at(ref, n, count):
    return ref[n : n + count]


class Arrivals:
    def __init__(self, first, rows, fields, reaches):
        self.first, self.rows, self.fields, self.reaches = first, rows, fields, reaches

    def window(self, level, f, ext=True):
        n = self.first
        for reach in self.reaches[:level]:
            n = n + self.fields * (self.rows + 2 * reach)
        reach = self.reaches[level]
        n = n + f * (self.rows + 2 * reach)
        if ext:
            return slice(n + reach - W, n + reach + W + self.rows)
        return slice(n + reach, n + reach + self.rows)

    def size(self):
        return self.first + sum(self.fields * (self.rows + 2 * reach) for reach in self.reaches)


class Edges:
    def __init__(self, fields, depth, thick):
        n = 0
        self.fluid, self.outer, self.solid = {}, {}, {}
        for name, count, reach in (("p", fields, W), ("src", fields, W - 1), ("vel", 3, W - 1)):
            for f in range(count):
                for i in range(depth):
                    self.fluid[name, f, i] = slice(n, n + reach)
                    n = n + reach
        for name, near, reach in (("t", 3, W), ("k", 3, W), ("heat", 2, W - 1)):
            for i in range(thick - near, thick):
                self.outer[name, i] = slice(n, n + reach)
                n = n + reach
        self.size = (n + 7) // 8 * 8
        n = 0
        for name, reach in (("t", W), ("k", W), ("heat", W - 1)):
            for i in range(thick):
                self.solid[name, i] = slice(n, n + reach)
                n = n + reach
        self.solid_size = (n + 7) // 8 * 8


class Fluid:
    def __init__(self, spread, jacobian, fields):
        self.n = fields
        self.d = [spread[f] for f in range(fields)]
        self.jac = [[jacobian[f, g] for g in range(fields)] for f in range(fields)]

    def diagonal(self, f, us):
        return us + (6.0 * self.d[f] + self.jac[f][f])

    def advance(self, cur, left, right, vel, w, src, rows, store):
        for n in range(rows.start, rows.stop, 8):
            sl = slice(n, n + 8)
            u0, u1, u2 = (u(sl) for u in vel)
            us = u0 + u1 + u2
            centre = [cur(f, sl) for f in range(self.n)]
            for f in range(self.n):
                c = centre[f]
                zm, zp = beside(c)
                yp = cur(f, beyond(sl, 1))
                near = (cur(f, beyond(sl, -1)) + yp) + (zm + zp)
                if left is not None:
                    near = near + left(f, sl)
                res = u1 * yp + u2 * zp - self.diagonal(f, us) * c
                if right is not None:
                    xp = right(f, sl)
                    near = near + xp
                    res = res + u0 * xp
                res = res + self.d[f] * near
                for g in range(self.n):
                    if g != f:
                        res = res - self.jac[f][g] * centre[g]
                if src is not None:
                    res = res + src(f, sl)
                store(f, sl, res, c + w(f, sl) * res)


def at(ref, i):
    return lambda f, sl: ref[f, i, sl]


def flat(ref):
    return lambda f, sl: ref[f, sl]


def speeds(ref, i):
    return [lambda sl, c=c: ref[c, i, sl] for c in range(3)]


def into(ref, i):
    def store(f, sl, _, value):
        ref[f, i, sl] = value

    return store


def into_flat(ref):
    def store(f, sl, _, value):
        ref[f, sl] = value

    return store


def early_kernel(edges, *refs):
    bufs = refs[6:12]
    yf, yb, xf, zf, zb, sems = refs[12:]
    copies = [
        pltpu.make_async_copy(ref, buf, sems.at[j])
        for j, (ref, buf) in enumerate(zip(refs[:6], bufs, strict=True))
    ]
    for copy in copies:
        copy.start()
    for copy in copies:
        copy.wait()
    p, src, vel, t, heat, k = bufs
    fields, depth, rows = p.shape[0], p.shape[1], p.shape[2]
    thick = t.shape[0]
    named = {"p": p, "src": src, "vel": vel, "t": t, "heat": heat, "k": k}
    planes = [p[f, depth - 1] for f in range(fields)]
    planes += [vel[f, depth - 1] for f in range(3)]
    planes += [vel[0, depth - 2], vel[0, depth - 2] + vel[1, depth - 2] + vel[2, depth - 2]]
    planes += [t[thick - 4 + j] for j in range(4)]
    planes += [k[thick - 4 + j] for j in range(4)]
    planes += [heat[thick - 3 + j] for j in range(3)]
    for j, plane in enumerate(planes):
        xf[j * rows : (j + 1) * rows] = plane
    for up, down, places in ((yf, yb, edges.fluid), (yf, yb, edges.outer), (zf, zb, edges.solid)):
        for (name, *at_plane), sl in places.items():
            ref, reach = named[name], sl.stop - sl.start
            up[sl] = ref[*at_plane, rows - reach :]
            down[sl] = ref[*at_plane, :reach]


def ahead_kernel(blocks, spans, edges, spread, jacobian, p, src, vel, yl, yr, out, a0, a1, a2, sa, va, wa):
    fields, depth, rows, z = p.shape
    at_place = Place(rows, blocks, spans)
    ext, own = at_place.ext, at_place.own
    fluid = Fluid(spread, jacobian, fields)
    inside = at_place.inside(z)

    def fill(buf, f, j, ref, name, i):
        def store(sl, x):
            buf[f, j, sl] = x

        sl = edges.fluid[name, f, i]
        at_place.fill(store, ref[f, i], yl[sl], yr[sl])

    for f in range(fields):
        for j in range(4):
            fill(a0, f, j, p, "p", depth - 4 + j)
        for j in range(3):
            fill(sa, f, j, src, "src", depth - 3 + j)
    for f in range(3):
        for j in range(3):
            fill(va, f, j, vel, "vel", depth - 3 + j)
    for j in range(3):
        us = va[0, j, ext] + va[1, j, ext] + va[2, j, ext]
        for f in range(fields):
            wa[f, j, ext] = jnp.where(inside, DAMPING / fluid.diagonal(f, us), 0.0)

    def step(old, i, store, j):
        fluid.advance(
            at(old, i),
            at(old, i - 1),
            None if j == 2 else at(old, i + 1),
            speeds(va, j),
            at(wa, j),
            at(sa, j),
            ext,
            store,
        )

    for j in range(3):
        step(a0, j + 1, into(a1, j), j)
    for j in range(1, 3):
        step(a1, j, into(a2, j - 1), j)
    corners = [edges.fluid["p", f, depth - 1] for f in range(fields)]
    corners += [edges.fluid["vel", c, depth - 1] for c in range(3)]
    corners += list(edges.outer.values())
    n = 0
    for sl in corners:
        reach = sl.stop - sl.start
        out[n + W - reach : n + W] = yl[sl]
        out[n + W : n + W + reach] = yr[sl]
        n = n + 2 * W
    for reach, buf, j in ((2, a1, 2), (1, a2, 1)):
        size = rows + 2 * reach
        for f in range(fields):
            out[n : n + size] = buf[f, j, at_place.reach(reach)]
            n = n + size

    def last(f, sl, _, value):
        m = n + f * rows + sl.start - own.start
        out[m : m + 8] = value

    fluid.advance(
        at(a2, 1), at(a2, 0), None, speeds(va, 2), at(wa, 2), at(sa, 2), own, last
    )


def around(buf, j, sl):
    zm, zp = beside(buf[j, sl])
    return (
        (buf[j - 1, sl] + buf[j + 1, sl])
        + (buf[j, beyond(sl, -1)] + buf[j, beyond(sl, 1)])
        + (zm + zp)
    )


def solid_diagonal(h_of, i, sl):
    zm, zp = beside(h_of(i, sl))
    near = (h_of(i - 1, sl) + h_of(i + 1, sl)) + (zm + zp)
    near = near + (h_of(i, beyond(sl, -1)) + h_of(i, beyond(sl, 1)))
    return 6.0 * h_of(i, sl) + near


def solid_weight(h, diagonal):
    return jnp.where(h > 0.0, DAMPING / jnp.where(h > 0.0, diagonal, 1.0), 0.0)


def plan(blocks, owner, target, place, meta, idx):
    rows = target.shape[1]
    me = lax.axis_index("blk")
    row = lax.broadcasted_iota(jnp.int32, (rows, rows), 0)
    lane = lax.broadcasted_iota(jnp.int32, (rows, rows), 1)
    owner = owner[...].astype(F32)
    column = jnp.where(row == lane, jnp.broadcast_to(owner, (rows, rows)), 0.0)
    column = jnp.sum(column, axis=1, keepdims=True)
    idx[...] = owner * rows + target[...].astype(F32)
    before = jnp.where((column == owner) & (row < lane), 1.0, 0.0)
    rank = jnp.sum(before, axis=0, keepdims=True)
    n = lax.broadcasted_iota(jnp.int32, (blocks * CHUNK, rows), 0)
    slot = n % CHUNK
    second = slot >= CAP
    named = n // CHUNK - jnp.where(second, 0, 1)
    at_rank = (slot - jnp.where(second, CAP, 0)).astype(F32)
    hot = jnp.where((owner == named.astype(F32)) & (rank == at_rank), 1.0, 0.0)
    hot = jnp.where(slot < 2 * CAP, hot, 0.0)
    place[...] = hot
    targets = jnp.broadcast_to((target[...] + 1).astype(F32), (8, rows))
    lanes = lax.dot_general(
        targets, hot, (((1,), (1,)), ((), ())), precision=HIGHEST, preferred_element_type=F32
    )
    row = lax.broadcasted_iota(jnp.int32, (8, 4 * CHUNK), 0)
    lane = lax.broadcasted_iota(jnp.int32, (8, 4 * CHUNK), 1)
    for j in range(blocks):
        group = lanes[:, j // 4 * 4 * CHUNK : (j // 4 + 1) * 4 * CHUNK]
        group = jnp.where(lane // CHUNK == j % 4, group, 0.0)
        group = pltpu.roll(group, lax.rem(me - j + 4 * blocks, 4) * CHUNK, 1)
        meta[j] = jnp.where(row == me // 4, group, 0.0)


def inner_kernel(
    blocks, spans, edges, spread, jacobian, owner, target, p, src, vel, yl, yr, *outs
):
    p0, s0, v0, w0, p1, p2, p3, place, meta, idx = outs
    plan(blocks, owner, target, place, meta, idx)
    fields, depth, rows, z = p.shape
    here = Place(rows, blocks, spans)
    ext = here.ext
    fluid = Fluid(spread, jacobian, fields)
    inside = here.inside(z)
    for name, buf, ref in (("p", p0, p), ("src", s0, src), ("vel", v0, vel)):
        for f in range(ref.shape[0]):
            for i in range(depth):

                def store(sl, x, buf=buf, f=f, i=i):
                    buf[f, i, sl] = x

                sl = edges.fluid[name, f, i]
                here.fill(store, ref[f, i], yl[sl], yr[sl])
    for i in range(depth):
        us = v0[0, i, ext] + v0[1, i, ext] + v0[2, i, ext]
        for f in range(fields):
            w0[f, i, ext] = jnp.where(inside, DAMPING / fluid.diagonal(f, us), 0.0)
    for level, (old, new) in enumerate(((p0, p1), (p1, p2), (p2, p3))):
        for i in range(level + 1, depth - 1 - level):
            fluid.advance(
                at(old, i - level),
                at(old, i - level - 1),
                at(old, i - level + 1),
                speeds(v0, i),
                at(w0, i),
                at(s0, i),
                ext,
                into(new, i - level - 1),
            )


def inner_solid_kernel(blocks, spans, edges, fields, t, heat, k, yl, yr, _, *refs):
    te, he, so, ti, tb, sqi, dg, ws, ta, tc, qa, qc = refs
    thick, rows, z = t.shape
    here = Place(rows, blocks, spans)
    ext = here.ext
    for name, buf, ref, scale in (("t", te, t, 1.0), ("k", he, k, 0.5), ("heat", so, heat, 1.0)):
        for i in range(thick):

            def store(sl, x, buf=buf, i=i, scale=scale):
                buf[i, sl] = scale * x

            sl = edges.solid[name, i]
            here.fill(store, ref[i], yl[sl], yr[sl])
    for i in range(1, thick - 1):
        h = he[i, ext]
        diagonal = 6.0 * h + around(he, i, ext)
        dg[i, ext] = diagonal
        ws[i, ext] = solid_weight(h, diagonal)
    for i in range(thick):
        qa[i, ext] = he[i, ext] * te[i, ext]
    old, oldq, new, newq = te, qa, ta, qc
    total = None
    for level in range(SWEEPS):
        last = level == SWEEPS - 1
        sl = here.own if last else ext
        for i in range(level + 1, thick - 1 - level):
            h, q = he[i, sl], old[i, sl]
            res = so[i, sl] - dg[i, sl] * q + h * around(old, i, sl) + around(oldq, i, sl)
            value = q + ws[i, sl] * res
            if last:
                tb[i - SWEEPS] = value
                square = res * res
                total = square if total is None else total + square
            else:
                new[i, sl] = value
                newq[i, sl] = h * value
        if not last:
            one = level + 1
            for j, i in enumerate((one, one + 1, thick - 2 - one, thick - 1 - one)):
                ti[level, j] = new[i]
            old, new = new, (tc if new is ta else ta)
            oldq, newq = newq, oldq
    sqi[...] = jnp.zeros_like(sqi)
    sqi[fields : fields + 1] = jnp.sum(total, axis=0, keepdims=True)


def cone_kernel(blocks, spans, sent, spread, jacobian, *refs):
    p0, s0, v0, w0, p1, te, he, so, ti, dg, ws, xe, xn = refs[:13]
    back, n2, c2, c3, d1, d2, vm, wm, sl_, t0, t1, t2, t3, dl, wl = refs[13:28]
    l0, n1, qa = refs[28:]
    fields, z = p0.shape[0], p0.shape[3]
    rows = p0.shape[2] - 2 * (B + W)
    here = Place(rows, blocks, spans)
    ext, own, tall = here.ext, here.own, here.tall
    fluid = Fluid(spread, jacobian, fields)
    inside = jnp.logical_and(here.inside(z), jnp.logical_not(here.no_left))
    corner = 0
    for f in range(fields):

        def store(sl, x, f=f):
            l0[f, sl] = x

        n = corner + f * 2 * W
        here.fill(
            store, xe[f * rows : (f + 1) * rows], xn[n : n + W], xn[n + W : n + 2 * W], here.no_left
        )
    for c in range(3):

        def store(sl, x, c=c):
            vm[c, sl] = x

        n = corner + (fields + c) * 2 * W
        m = (fields + c) * rows
        here.fill(store, xe[m : m + rows], xn[n : n + W], xn[n + W : n + 2 * W])
    um = [vm[c, ext] for c in range(3)]
    usm = um[0] + um[1] + um[2]
    for f in range(fields):
        wm[f, ext] = jnp.where(inside, DAMPING / fluid.diagonal(f, usm), 0.0)
    def sum_of(level, ref):
        def read(f, sl):
            n = sent.window(level - 1, f).start + sl.start - B
            return unless(here.no_left, xn[n : n + 8]) + ref[f, sl]

        return read

    def plane(cur, i, left, right, store, sl=ext):
        fluid.advance(cur, left, right, speeds(v0, i), at(w0, i), at(s0, i), sl, store)

    outer = [lambda sl, c=c: vm[c, sl] for c in range(3)]
    plane(at(p0, 0), 0, flat(l0), at(p0, 1), into_flat(n1))
    for f in range(fields):
        d1[f, ext] = wm[f, ext] * (fluid.d[f] + um[0]) * p0[f, 0, ext]
    plane(flat(n1), 0, sum_of(1, d1), at(p1, 0), into_flat(n2))
    plane(at(p1, 0), 1, flat(n1), at(p1, 1), into_flat(c2))
    fluid.advance(flat(d1), None, flat(n1), outer, flat(wm), None, ext, into_flat(d2))
    plane(flat(n2), 0, sum_of(2, d2), flat(c2), into_flat(c3))
    n = 6 * tall
    for reach, read in (
        (3, at(p0, 0)),
        (2, flat(n1)),
        (1, flat(n2)),
        (0, flat(c3)),
    ):
        size = rows + 2 * reach
        for f in range(fields):
            back[n : n + size] = read(f, here.reach(reach))
            n = n + size
    corner = corner + (fields + 3) * 2 * W
    early = (fields + 5) * rows
    zero = jnp.zeros((W, z), F32)
    hl, sl_ = sl_.at[0], sl_.at[1]
    for buf, near, scale in ((t0, 4, 1.0), (hl, 4, 0.5), (sl_, 3, 1.0)):
        for i in range(near):

            def store(sl, x, buf=buf, j=4 - near + i, scale=scale):
                buf[j, sl] = scale * x

            if i > 0:
                low, high = xn[corner : corner + W], xn[corner + W : corner + 2 * W]
                corner = corner + 2 * W
            else:
                low, high = zero, zero
            here.fill(store, xe[early : early + rows], low, high, here.no_left)
            early = early + rows

    def h_of(i, sl):
        return hl[i + 4, sl] if i < 0 else he[i, sl]

    for i in range(-3, 1):
        dl[i + 3, ext] = solid_diagonal(h_of, i, ext)
        wl[i + 3, ext] = solid_weight(h_of(i, ext), dl[i + 3, ext])
    for j in range(4, 6):
        t0[j] = te[j - 4]
    for level, (old, new) in enumerate(((t0, t1), (t1, t2), (t2, t3))):
        for j in range(6):
            qa[j, ext] = h_of(level - 4 + j, ext) * old[j, ext]
        for j in range(4):
            i = level - 3 + j
            q = old[j + 1, ext]
            res = sl_[i + 4, ext] if i < 0 else so[i, ext]
            diagonal, w = (dl, wl) if i <= 0 else (dg, ws)
            m = i + 3 if i <= 0 else i
            res = res - diagonal[m, ext] * q
            res = res + h_of(i, ext) * around(old, j + 1, ext) + around(qa, j + 1, ext)
            new[j, ext] = q + w[m, ext] * res
        for j in range(4, 6):
            new[j] = ti[level, j - 4]
    n = 0
    for ref, i in ((he, 0), (he, 1), (t0, 4), (t1, 3)):
        back[n : n + tall] = ref[i, ext]
        n = n + tall
    for ref, i in ((t2, 2), (t3, 1)):
        back[n : n + tall] = ref[i, ext]
        n = n + tall


def flux_kernel(blocks, spans, sent, spread, jacobian, *refs):
    s0, v0, w0, p2, p3, n2, c2, c3, d1, d2, vm, wm, xe, xn, coef, hot, meta = refs[:17]
    parts, left, sq, m3, d3 = refs[17:]
    fields, rows, z = left.shape[0], left.shape[2], left.shape[3]
    here = Place(rows, blocks, spans)
    ext, own = here.ext, here.own
    fluid = Fluid(spread, jacobian, fields)
    m = (fields + 3) * rows
    u0mm, usmm = xe[m : m + rows], xe[m + rows : m + 2 * rows]
    outer = [lambda sl, c=c: vm[c, sl] for c in range(3)]

    def third(f, sl):
        n = sent.window(2, f).start + sl.start - B
        return unless(here.no_left, xn[n : n + 8]) + d3[f, sl]

    def plane(cur, i, before, after, store, sl=ext):
        fluid.advance(cur, before, after, speeds(v0, i), at(w0, i), at(s0, i), sl, store)

    def farther(f, sl):
        n = sl.start - own.start
        w = unless(here.no_left, DAMPING / fluid.diagonal(f, usmm[n : n + 8]))
        return w * (fluid.d[f] + u0mm[n : n + 8]) * d1[f, sl]

    fluid.advance(flat(d2), farther, flat(n2), outer, flat(wm), None, own, into_flat(d3))
    plane(flat(c2), 1, flat(n2), at(p2, 0), into(m3, 0))
    plane(at(p2, 0), 2, flat(c2), at(p2, 1), into(m3, 1))
    squares = [None] * fields
    third_of = [flat(c3), at(m3, 0), at(m3, 1), at(p3, 0), at(p3, 1)]
    for i in range(4):

        def final(f, sl, res, value, i=i):
            left[f, i, sl.start - own.start : sl.stop - own.start] = value
            square = res * res
            squares[f] = square if squares[f] is None else squares[f] + square

        plane(third_of[i], i, third_of[i - 1] if i > 0 else third, third_of[i + 1], final, own)
    sq[...] = jnp.zeros_like(sq)
    for f in range(fields):
        sq[f : f + 1] = jnp.sum(squares[f], axis=0, keepdims=True)
    flux = coef[0] * left[fields - 1, 0]
    parts[...] = jnp.dot(hot[...], flux, precision=HIGHEST, preferred_element_type=F32)
    for j in range(blocks):
        parts[j * CHUNK + 2 * CAP : (j + 1) * CHUNK] = meta[j]


def rest_kernel(blocks, spans, sent, spread, jacobian, *refs):
    p0, s0, v0, w0, p1, p2, p3, left, sqb, xn, _, gas, sq, n1, n2, n3 = refs
    fields, depth = gas.shape[0], gas.shape[1]
    rows = gas.shape[2]
    here = Place(rows, blocks, spans)
    ext, own, tall = here.ext, here.own, here.tall
    fluid = Fluid(spread, jacobian, fields)
    def arrived(level):
        def read(f, sl):
            n = sent.window(level, f).start + sl.start - B
            return unless(here.no_right, xn[n : n + 8])

        return read

    known = [{i: (p0, i) for i in range(depth)}, {}, {}, {}]
    for level, buf in enumerate((p1, p2, p3)):
        for i in range(level + 1, depth - 1 - level):
            known[level + 1][i] = (buf, i - level - 1)

    def read(level, i):
        ref, j = known[level][i]
        return at(ref, j)

    def plane(level, i, store, sl=ext):
        fluid.advance(
            read(level, i),
            read(level, i - 1),
            read(level, i + 1) if i < depth - 1 else arrived(level),
            speeds(v0, i),
            at(w0, i),
            at(s0, i),
            sl,
            store,
        )

    todo = ((depth - 1,), (depth - 2, depth - 1), (depth - 3, depth - 2, depth - 1))
    for level, new in enumerate((n1, n2, n3)):
        for j, i in enumerate(todo[level]):
            plane(level, i, into(new, j))
            known[level + 1][i] = (new, j)
    total = [None] * fields
    for f in range(fields):
        for i in range(4):
            gas[f, i] = left[f, i]
    for i in range(4, depth):

        def final(f, sl, res, value, i=i):
            gas[f, i, sl.start - own.start : sl.stop - own.start] = value
            square = res * res
            total[f] = square if total[f] is None else total[f] + square

        plane(3, i, final, own)
    sq[...] = sqb[...]
    for f in range(fields):
        sq[f : f + 1] = sq[f : f + 1] + jnp.sum(total[f], axis=0, keepdims=True)


def solid_kernel(
    blocks, spans, te, he, so, ti, tbi, sqi, dg, ws, sl_, tl0, tl1, tl2, tl3, dl, wl, xb, _, *refs
):
    tb, rb, sq, rh, rd, rw = refs[:6]
    hr, dr, wr, ta, tc, qa = refs[6:]
    thick, rows, z = tb.shape
    here = Place(rows, blocks, spans)
    ext, own, tall = here.ext, here.own, here.tall
    hl = sl_.at[0]

    def arrived(n):
        return unless(here.no_right, xb[n * tall : (n + 1) * tall])

    for j in range(2):
        hr[j, ext] = arrived(j)

    def h_of(i, sl):
        if i < 0:
            return hl[i + 4, sl]
        return he[i, sl] if i < thick else hr[i - thick, sl]

    for j in range(2):
        i = thick - 1 + j
        dr[j, ext] = solid_diagonal(h_of, i, ext)
        wr[j, ext] = solid_weight(h_of(i, ext), dr[j, ext])

    def d_of(left, inside, right, i, sl):
        if i <= 0:
            return left[i + 3, sl]
        return inside[i, sl] if i < thick - 1 else right[i - thick + 1, sl]

    def residual(old, j, i, sl):
        res = so[i, sl] - d_of(dl, dg, dr, i, sl) * old[j, sl]
        return res + h_of(i, sl) * around(old, j, sl) + around(qa, j, sl)

    sums = None
    for j in range(6):
        qa[j, ext] = h_of(j - 1, ext) * tl3[j, ext]
    for i in range(4):
        res = residual(tl3, i + 1, i, own)
        tb[i] = tl3[i + 1, own] + d_of(wl, ws, wr, i, own) * res
        if i < 3:
            rb[i] = res
        else:
            sums = res * res
    old, new = ta, tc
    old[0], old[1] = te[thick - 2], te[thick - 1]
    old[2, ext] = arrived(2)
    for level in range(SWEEPS):
        last = level == SWEEPS - 1
        sl = own if last else ext
        low = thick - 2 - level
        for j in range(level + 3):
            qa[j, ext] = h_of(low + j, ext) * old[j, ext]
        for j in range(1, level + 2):
            i = low + j
            res = residual(old, j, i, sl)
            value = old[j, sl] + d_of(wl, ws, wr, i, sl) * res
            if last:
                tb[i] = value
                rb[i - (thick - 7)] = res
            else:
                new[j + 1, ext] = value
        if not last:
            for j in range(2):
                new[j] = ti[level, j + 2]
            new[level + 3, ext] = arrived(3 + level)
            old, new = new, old
    for i in range(SWEEPS, thick - SWEEPS):
        tb[i] = tbi[i - SWEEPS]
    sq[...] = sqi[...]
    n = sq.shape[0] - 3
    sq[n : n + 1] = sq[n : n + 1] + jnp.sum(sums, axis=0, keepdims=True)
    for region in range(2):
        for j in range(5):
            i = j - 2 if region == 0 else thick - 4 + j
            rh[region, j, ext] = h_of(i, ext)
            rd[region, j, ext] = d_of(dl, dg, dr, i, ext)
            rw[region, j, ext] = d_of(wl, ws, wr, i, ext)


def surface_kernel(blocks, arrived, surface, yf, yb):
    rows = surface.shape[0] // 2
    meta = arrived[0, 2 * CAP :]
    for j in range(1, blocks):
        meta = meta + arrived[j, 2 * CAP :]
    row = lax.broadcasted_iota(jnp.int32, (2 * rows, 4 * CHUNK), 0)
    slot = lax.broadcasted_iota(jnp.int32, (2 * rows, 4 * CHUNK), 1) % CHUNK
    row = row + 1 - jnp.where(slot < CAP, 0, rows)
    row = jnp.where((row >= 1) & (row <= rows), row, -1).astype(F32)
    whole = None
    for j in range(0, blocks, 4):
        sent = jnp.concatenate([arrived[j + m] for m in range(4)], axis=0)
        hot = jnp.where(row == meta[j // 4 : j // 4 + 1], 1.0, 0.0)
        got = jnp.dot(hot, sent, precision=HIGHEST, preferred_element_type=F32)
        whole = got if whole is None else whole + got
    surface[...] = whole
    yf[:W] = whole[rows - W : rows]
    yf[W:] = whole[2 * rows - W :]
    yb[:W] = whole[:W]
    yb[W:] = whole[rows : rows + W]


def response_kernel(
    blocks, spans, fields, surface, yl, yr, rh, rd, rw, tb, rb, sqf, sqs, tn, out, da, db, hd, so
):
    thick, rows, z = tb.shape
    here = Place(rows, blocks, spans)
    ext, own = here.ext, here.own
    for buf in (da, db, hd):
        buf[...] = jnp.zeros_like(buf)
    sq = sqf[...] + sqs[...]
    gained = jnp.zeros((rows, z), F32)
    for region in range(2):

        def store(sl, x, region=region):
            so[region, sl] = x

        edge = slice(region * W, (region + 1) * W)
        here.fill(store, surface[region * rows : (region + 1) * rows], yl[edge], yr[edge])

    needed = (((2,), (1, 2, 3), (1, 2, 3, 4), (3, 4, 5)), ((4,), (3, 4, 5), (2, 3, 4, 5), (1, 2, 3, 4)))
    for i in range(3, thick - 4):
        tn[i] = tb[i]
    for region in range(2):
        old, new = da, db
        source = 2 if region == 0 else 4
        for sweep in range(SWEEPS):
            final = sweep == SWEEPS - 1
            for j in needed[region][sweep]:
                res = so[region, ext] if j == source else None
                h, w = rh[region, j - 1, ext], rw[region, j - 1, ext]
                if sweep > 0:
                    q = old[region, j, ext]
                    flow = h * around(old.at[region], j, ext) + around(hd.at[region], j, ext) - rd[region, j - 1, ext] * q
                    res = flow if res is None else res + flow
                    change = q + w * res
                else:
                    change = w * res
                if final:
                    i = j - 3 if region == 0 else thick - 5 + j
                    kept = i if region == 0 else 2 + j
                    mine = slice(W, W + rows)
                    tn[i] = tb[i] + change[mine]
                    full = rb[kept] + res[mine]
                    gained = gained + full * full
                else:
                    new[region, j, ext] = change
            if not final:
                for j in needed[region][sweep]:
                    hd[region, j, ext] = rh[region, j - 1, ext] * new[region, j, ext]
                old, new = new, old
    extra = jnp.sum(gained, axis=0, keepdims=True)
    row = lax.broadcasted_iota(jnp.int32, sq.shape, 0)
    sq = sq + jnp.where(row == fields, extra, 0.0)
    for j in range(blocks):
        out[j, :rows] = tn[thick - 1]
        out[j, rows:] = sq


def return_kernel(blocks, arrived, idx, coef, added, sq):
    rows = added.shape[0]
    row = lax.broadcasted_iota(jnp.int32, (rows, rows), 0).astype(F32)
    taken, squares = None, None
    for j in range(blocks):
        hot = jnp.where(idx[...] - float(j * rows) == row, 1.0, 0.0)
        got = lax.dot_general(
            hot,
            arrived[j, :rows],
            (((0,), (0,)), ((), ())),
            precision=HIGHEST,
            preferred_element_type=F32,
        )
        taken = got if taken is None else taken + got
        squares = arrived[j, rows:] if squares is None else squares + arrived[j, rows:]
    added[...] = coef[0] * taken
    sq[...] = squares


def shards(
    blocks,
    spans,
    fluid_adjoint_in,
    fluid_source,
    velocity,
    diffusion,
    jacobian,
    wall_coefficient,
    metal_costate_prior,
    solid_source,
    conductivity,
    tile_owner,
    tile_target,
):
    p, src, vel = fluid_adjoint_in, fluid_source, velocity
    t, heat, k = metal_costate_prior, solid_source, conductivity
    fields, depth, rows, z = p.shape
    thick = t.shape[0]
    tall = rows + 2 * W
    buf = tall + 2 * B
    forward = {
        "blk": [(i, (i + 1) % blocks) for i in range(blocks)],
        "span": [(i, (i + 1) % spans) for i in range(spans)],
    }
    backward = {axis: [(j, i) for i, j in pairs] for axis, pairs in forward.items()}

    def ahead(x, axis):
        return lax.ppermute(x, axis, forward[axis])

    def behind(x, axis):
        return lax.ppermute(x, axis, backward[axis])

    edges = Edges(fields, depth, thick)
    inputs = [p, src, vel, t, heat, k]
    p, src, vel, t, heat, k, yf, yb, xf, zf, zb = call(
        functools.partial(early_kernel, edges),
        held(*[x.shape for x in inputs])
        + [(edges.size, z)] * 2
        + [((fields + 16) * rows, z)]
        + [(edges.solid_size, z)] * 2,
        [pltpu.SemaphoreType.DMA((6,))],
        [HBM] * 6,
        *[pltpu.with_memory_space_constraint(x, pltpu.HBM) for x in inputs],
    )
    yl, yr = ahead(yf, "span"), behind(yb, "span")
    xe = ahead(xf, "blk")
    sent_ahead = Arrivals((fields + 11) * 2 * W, rows, fields, (2, 1, 0))
    (out,) = call(
        functools.partial(ahead_kernel, blocks, spans, edges),
        [(sent_ahead.size(), z)],
        [(fields, 4, buf, z), (fields, 3, buf, z), (fields, 2, buf, z), (fields, 3, buf, z)]
        + [(3, 3, buf, z), (fields, 3, buf, z)],
        [SMEM] * 2 + [VMEM] * 5,
        diffusion,
        jacobian,
        p,
        src,
        vel,
        yl,
        yr,
        cost=COSTS[1],
    )
    xn = ahead(out, "blk")
    full = (fields, depth, buf, z)
    part = [(fields, depth - 2 * (level + 1), buf, z) for level in range(3)]
    solid = (thick, buf, z)
    p0, s0, v0, w0, p1, p2, p3, place, meta, idx = call(
        functools.partial(inner_kernel, blocks, spans, edges),
        held(full, full, (3, depth, buf, z), full, *part)
        + held((blocks * CHUNK, rows), (blocks, 8, z), (1, rows)),
        [],
        [SMEM] * 2 + [VMEM] * 7,
        diffusion,
        jacobian,
        tile_owner.reshape(1, rows),
        tile_target,
        p,
        src,
        vel,
        yl,
        yr,
        cost=COSTS[2],
    )
    zl, zr = ahead(zf, "span"), behind(zb, "span")
    te, he, so, ti, tb, sqi, dg, ws = call(
        functools.partial(inner_solid_kernel, blocks, spans, edges, fields),
        held(solid, solid, solid, (3, 4, buf, z), (thick - 2 * SWEEPS, rows, z), (8, z), solid, solid),
        [solid] * 4,
        [VMEM] * 6,
        t,
        heat,
        k,
        zl,
        zr,
        idx,
        cost=COSTS[2],
    )
    sent_back = Arrivals(6 * tall, rows, fields, (3, 2, 1, 0))
    one, six = (fields, buf, z), (6, buf, z)
    back, n2, c2, c3, d1, d2, vm, wm, sl_, *lefts = call(
        functools.partial(cone_kernel, blocks, spans, sent_ahead),
        [(sent_back.size(), z)]
        + held(one, one, one, one, one, (3, buf, z), one, (2, 4, buf, z))
        + held(six, six, six, six, (4, buf, z), (4, buf, z)),
        [one] * 2 + [six],
        [SMEM] * 2 + [VMEM] * 13,
        diffusion,
        jacobian,
        p0,
        s0,
        v0,
        w0,
        p1,
        te,
        he,
        so,
        ti,
        dg,
        ws,
        xe,
        xn,
        cost=COSTS[3],
    )
    xr = behind(back, "blk")
    parts, half, sq = call(
        functools.partial(flux_kernel, blocks, spans, sent_ahead),
        [(blocks * CHUNK, z)] + held((fields, 4, rows, z), (8, z)),
        [(fields, 2, buf, z), one],
        [SMEM] * 2 + [VMEM] * 17,
        diffusion,
        jacobian,
        s0,
        v0,
        w0,
        p2,
        p3,
        n2,
        c2,
        c3,
        d1,
        d2,
        vm,
        wm,
        xe,
        xn,
        wall_coefficient,
        place,
        meta,
        cost=COSTS[2],
    )
    arrived = lax.all_to_all(parts.reshape(blocks, CHUNK, z), "blk", 0, 0)
    surface, yf, yb = call(
        functools.partial(surface_kernel, blocks),
        [(2 * rows, z), (2 * W, z), (2 * W, z)],
        [],
        [VMEM],
        arrived,
    )
    yl, yr = ahead(yf, "span"), behind(yb, "span")
    gas, sqf = call(
        functools.partial(rest_kernel, blocks, spans, sent_back),
        held(p.shape, (8, z)),
        [(fields, 1, buf, z), (fields, 2, buf, z), (fields, 3, buf, z)],
        [SMEM] * 2 + [VMEM] * 11,
        diffusion,
        jacobian,
        p0,
        s0,
        v0,
        w0,
        p1,
        p2,
        p3,
        half,
        sq,
        xr,
        yf,
        cost=COSTS[4],
    )
    two, edge = (2, buf, z), (2, 5, buf, z)
    tb, rb, sqs, rh, rd, rw = call(
        functools.partial(solid_kernel, blocks, spans),
        held(t.shape, (7, rows, z), (8, z), edge, edge, edge),
        [two] * 3 + [six] * 3,
        [VMEM] * 17,
        te,
        he,
        so,
        ti,
        tb,
        sqi,
        dg,
        ws,
        sl_,
        *lefts,
        xr,
        yf,
        cost=COSTS[5],
    )
    region = (2, 7, buf, z)
    t, out = call(
        functools.partial(response_kernel, blocks, spans, fields),
        held(t.shape, (blocks, rows + 8, z)),
        [region] * 3 + [(2, buf, z)],
        [VMEM] * 10,
        surface,
        yl,
        yr,
        rh,
        rd,
        rw,
        tb,
        rb,
        sqf,
        sqs,
    )
    arrived = lax.all_to_all(out, "blk", 0, 0)
    added, sq = call(
        functools.partial(return_kernel, blocks),
        [(rows, z), (8, z)],
        [],
        [VMEM] * 3,
        arrived,
        idx,
        wall_coefficient,
    )
    step = 1
    while step < spans:
        sq = sq + lax.ppermute(sq, "span", [(i, i ^ step) for i in range(spans)])
        step = step * 2
    gas = gas.at[fields - 1, 0].add(added)
    everyone = blocks * spans
    counts = [float(depth * rows * z * everyone)] * fields + [float(thick * rows * z * everyone)]
    totals = jnp.sum(sq[: fields + 1], axis=1)
    norms = jnp.sqrt(totals / jnp.array(counts, F32))
    return gas, t, norms


def solution(mesh):
    placed = (
        P(None, "blk", "span", None),
        P(None, "blk", "span", None),
        P(None, "blk", "span", None),
        P(),
        P(),
        P("blk", "span", None),
        P("blk", "span", None),
        P("blk", "span", None),
        P("blk", "span", None),
        P("span", "blk", None),
        P("span", "blk"),
    )
    return jax.shard_map(
        functools.partial(shards, mesh.shape["blk"], mesh.shape["span"]),
        mesh=mesh,
        in_specs=placed,
        out_specs=(P(None, "blk", "span", None), P("blk", "span", None), P()),
        check_vma=False,
    )
```

```python
import functools

import jax
import jax.numpy as jnp
from jax import lax
from jax.experimental import pallas as pl
from jax.experimental.pallas import tpu as pltpu
from jax.sharding import PartitionSpec as P

SWEEPS = 4
DAMPING = 0.8
HIGHEST = lax.Precision.HIGHEST
F32 = jnp.float32
VMEM = pl.BlockSpec(memory_space=pltpu.VMEM)
SMEM = pl.BlockSpec(memory_space=pltpu.SMEM)
HBM = pl.BlockSpec(memory_space=pltpu.HBM)
COSTS = (1.0, 30.0, 0.01, 2.0, 3.0, 3.0)
LIMIT = 12 * 1024 * 1024
W = 4
CAP = 12
CHUNK = 32
B = 8


def held(*shapes):
    return [pltpu.VMEM(s, F32) for s in shapes]


def call(kernel, outs, scratch, specs, *args, out_specs=None, cost=1.0):
    return pl.pallas_call(
        kernel,
        out_shape=[jax.ShapeDtypeStruct(s, F32) if isinstance(s, tuple) else s for s in outs],
        in_specs=specs,
        out_specs=out_specs or [VMEM] * len(outs),
        scratch_shapes=[pltpu.VMEM(s, F32) if isinstance(s, tuple) else s for s in scratch],
        compiler_params=pltpu.CompilerParams(vmem_limit_bytes=LIMIT),
        cost_estimate=pl.CostEstimate(
            flops=int(cost * 1e6), bytes_accessed=int(cost * 3e6), transcendentals=0
        ),
    )(*args)


def beside(x):
    lane = lax.broadcasted_iota(jnp.int32, x.shape, 1)
    last = x.shape[1] - 1
    before = jnp.where(lane == 0, 0.0, pltpu.roll(x, 1, 1))
    after = jnp.where(lane == last, 0.0, pltpu.roll(x, last, 1))
    return before, after


def unless(flag, x):
    return jnp.where(flag, 0.0, x)


class Place:
    def __init__(self, rows, blocks, spans):
        b, s = lax.axis_index("blk"), lax.axis_index("span")
        self.rows, self.tall = rows, rows + 2 * W
        self.no_left, self.no_right = b == 0, b == blocks - 1
        self.no_low, self.no_high = s == 0, s == spans - 1
        self.ext = slice(B, B + self.tall)
        self.own = slice(B + W, B + W + rows)
        self.low = slice(B, B + W)
        self.high = slice(B + W + rows, B + self.tall)

    def reach(self, by):
        return slice(B + W - by, B + W + self.rows + by)

    def fill(self, store, own, low, high, hide=None):
        no_low, no_high = self.no_low, self.no_high
        if hide is not None:
            own, no_low, no_high = unless(hide, own), no_low | hide, no_high | hide
        store(self.own, own)
        store(slice(self.low.stop - low.shape[0], self.low.stop), unless(no_low, low))
        store(slice(self.high.start, self.high.start + high.shape[0]), unless(no_high, high))

    def inside(self, z):
        row = lax.broadcasted_iota(jnp.int32, (self.tall, z), 0)
        out = ((row < W) & self.no_low) | ((row >= W + self.rows) & self.no_high)
        return jnp.logical_not(out)


def beyond(sl, by):
    return slice(sl.start + by, sl.stop + by)


def rows_at(ref, n, count):
    return ref[n : n + count]


class Arrivals:
    def __init__(self, first, rows, fields, reaches):
        self.first, self.rows, self.fields, self.reaches = first, rows, fields, reaches

    def window(self, level, f, ext=True):
        n = self.first
        for reach in self.reaches[:level]:
            n = n + self.fields * (self.rows + 2 * reach)
        reach = self.reaches[level]
        n = n + f * (self.rows + 2 * reach)
        if ext:
            return slice(n + reach - W, n + reach + W + self.rows)
        return slice(n + reach, n + reach + self.rows)

    def size(self):
        return self.first + sum(self.fields * (self.rows + 2 * reach) for reach in self.reaches)


class Edges:
    def __init__(self, fields, depth, thick):
        n = 0
        self.fluid, self.outer, self.solid = {}, {}, {}
        for name, count, reach in (("p", fields, W), ("src", fields, W - 1), ("vel", 3, W - 1)):
            for f in range(count):
                for i in range(depth):
                    self.fluid[name, f, i] = slice(n, n + reach)
                    n = n + reach
        for name, near, reach in (("t", 3, W), ("k", 3, W), ("heat", 2, W - 1)):
            for i in range(thick - near, thick):
                self.outer[name, i] = slice(n, n + reach)
                n = n + reach
        self.size = (n + 7) // 8 * 8
        n = 0
        for name, reach in (("t", W), ("k", W), ("heat", W - 1)):
            for i in range(thick):
                self.solid[name, i] = slice(n, n + reach)
                n = n + reach
        self.solid_size = (n + 7) // 8 * 8


class Fluid:
    def __init__(self, spread, jacobian, fields):
        self.n = fields
        self.d = [spread[f] for f in range(fields)]
        self.jac = [[jacobian[f, g] for g in range(fields)] for f in range(fields)]

    def diagonal(self, f, us):
        return us + (6.0 * self.d[f] + self.jac[f][f])

    def advance(self, cur, left, right, vel, w, src, rows, store):
        for n in range(rows.start, rows.stop, 8):
            sl = slice(n, n + 8)
            u0, u1, u2 = (u(sl) for u in vel)
            us = u0 + u1 + u2
            centre = [cur(f, sl) for f in range(self.n)]
            for f in range(self.n):
                c = centre[f]
                zm, zp = beside(c)
                yp = cur(f, beyond(sl, 1))
                near = (cur(f, beyond(sl, -1)) + yp) + (zm + zp)
                if left is not None:
                    near = near + left(f, sl)
                res = u1 * yp + u2 * zp - self.diagonal(f, us) * c
                if right is not None:
                    xp = right(f, sl)
                    near = near + xp
                    res = res + u0 * xp
                res = res + self.d[f] * near
                for g in range(self.n):
                    if g != f:
                        res = res - self.jac[f][g] * centre[g]
                if src is not None:
                    res = res + src(f, sl)
                store(f, sl, res, c + w(f, sl) * res)


def at(ref, i):
    return lambda f, sl: ref[f, i, sl]


def flat(ref):
    return lambda f, sl: ref[f, sl]


def speeds(ref, i):
    return [lambda sl, c=c: ref[c, i, sl] for c in range(3)]


def into(ref, i):
    def store(f, sl, _, value):
        ref[f, i, sl] = value

    return store


def into_flat(ref):
    def store(f, sl, _, value):
        ref[f, sl] = value

    return store


def early_kernel(edges, *refs):
    bufs = refs[6:12]
    yf, yb, xf, zf, zb, sems = refs[12:]
    copies = [
        pltpu.make_async_copy(ref, buf, sems.at[j])
        for j, (ref, buf) in enumerate(zip(refs[:6], bufs, strict=True))
    ]
    for copy in copies:
        copy.start()
    p, src, vel, t, heat, k = bufs
    fields, depth, rows = p.shape[0], p.shape[1], p.shape[2]
    thick = t.shape[0]
    named = {"p": p, "src": src, "vel": vel, "t": t, "heat": heat, "k": k}

    def pack(up, down, places, names):
        for (name, *at_plane), sl in places.items():
            if name in names:
                ref, reach = named[name], sl.stop - sl.start
                up[sl] = ref[*at_plane, rows - reach :]
                down[sl] = ref[*at_plane, :reach]

    for j, name in enumerate(named):
        copies[j].wait()
        if j < 3:
            pack(yf, yb, edges.fluid, (name,))
    planes = [p[f, depth - 1] for f in range(fields)]
    planes += [vel[f, depth - 1] for f in range(3)]
    planes += [vel[0, depth - 2], vel[0, depth - 2] + vel[1, depth - 2] + vel[2, depth - 2]]
    planes += [t[thick - 4 + j] for j in range(4)]
    planes += [k[thick - 4 + j] for j in range(4)]
    planes += [heat[thick - 3 + j] for j in range(3)]
    for j, plane in enumerate(planes):
        xf[j * rows : (j + 1) * rows] = plane
    for up, down, places in ((yf, yb, edges.outer), (zf, zb, edges.solid)):
        pack(up, down, places, named)


def ahead_kernel(blocks, spans, edges, spread, jacobian, p, src, vel, yl, yr, out, a0, a1, a2, sa, va, wa):
    fields, depth, rows, z = p.shape
    at_place = Place(rows, blocks, spans)
    ext, own = at_place.ext, at_place.own
    fluid = Fluid(spread, jacobian, fields)
    inside = at_place.inside(z)

    def fill(buf, f, j, ref, name, i):
        def store(sl, x):
            buf[f, j, sl] = x

        sl = edges.fluid[name, f, i]
        at_place.fill(store, ref[f, i], yl[sl], yr[sl])

    for f in range(fields):
        for j in range(4):
            fill(a0, f, j, p, "p", depth - 4 + j)
        for j in range(3):
            fill(sa, f, j, src, "src", depth - 3 + j)
    for f in range(3):
        for j in range(3):
            fill(va, f, j, vel, "vel", depth - 3 + j)
    for j in range(3):
        us = va[0, j, ext] + va[1, j, ext] + va[2, j, ext]
        for f in range(fields):
            wa[f, j, ext] = jnp.where(inside, DAMPING / fluid.diagonal(f, us), 0.0)

    def step(old, i, store, j):
        fluid.advance(
            at(old, i),
            at(old, i - 1),
            None if j == 2 else at(old, i + 1),
            speeds(va, j),
            at(wa, j),
            at(sa, j),
            ext,
            store,
        )

    for j in range(3):
        step(a0, j + 1, into(a1, j), j)
    for j in range(1, 3):
        step(a1, j, into(a2, j - 1), j)
    corners = [edges.fluid["p", f, depth - 1] for f in range(fields)]
    corners += [edges.fluid["vel", c, depth - 1] for c in range(3)]
    corners += list(edges.outer.values())
    n = 0
    for sl in corners:
        reach = sl.stop - sl.start
        out[n + W - reach : n + W] = yl[sl]
        out[n + W : n + W + reach] = yr[sl]
        n = n + 2 * W
    for reach, buf, j in ((2, a1, 2), (1, a2, 1)):
        size = rows + 2 * reach
        for f in range(fields):
            out[n : n + size] = buf[f, j, at_place.reach(reach)]
            n = n + size

    def last(f, sl, _, value):
        m = n + f * rows + sl.start - own.start
        out[m : m + 8] = value

    fluid.advance(
        at(a2, 1), at(a2, 0), None, speeds(va, 2), at(wa, 2), at(sa, 2), own, last
    )


def around(buf, j, sl):
    zm, zp = beside(buf[j, sl])
    return (
        (buf[j - 1, sl] + buf[j + 1, sl])
        + (buf[j, beyond(sl, -1)] + buf[j, beyond(sl, 1)])
        + (zm + zp)
    )


def solid_diagonal(h_of, i, sl):
    zm, zp = beside(h_of(i, sl))
    near = (h_of(i - 1, sl) + h_of(i + 1, sl)) + (zm + zp)
    near = near + (h_of(i, beyond(sl, -1)) + h_of(i, beyond(sl, 1)))
    return 6.0 * h_of(i, sl) + near


def solid_weight(h, diagonal):
    return jnp.where(h > 0.0, DAMPING / jnp.where(h > 0.0, diagonal, 1.0), 0.0)


def plan(blocks, owner, target, place, meta, idx):
    rows = target.shape[1]
    me = lax.axis_index("blk")
    row = lax.broadcasted_iota(jnp.int32, (rows, rows), 0)
    lane = lax.broadcasted_iota(jnp.int32, (rows, rows), 1)
    owner = owner[...].astype(F32)
    column = jnp.where(row == lane, jnp.broadcast_to(owner, (rows, rows)), 0.0)
    column = jnp.sum(column, axis=1, keepdims=True)
    idx[...] = owner * rows + target[...].astype(F32)
    before = jnp.where((column == owner) & (row < lane), 1.0, 0.0)
    rank = jnp.sum(before, axis=0, keepdims=True)
    n = lax.broadcasted_iota(jnp.int32, (blocks * CHUNK, rows), 0)
    slot = n % CHUNK
    second = slot >= CAP
    named = n // CHUNK - jnp.where(second, 0, 1)
    at_rank = (slot - jnp.where(second, CAP, 0)).astype(F32)
    hot = jnp.where((owner == named.astype(F32)) & (rank == at_rank), 1.0, 0.0)
    hot = jnp.where(slot < 2 * CAP, hot, 0.0)
    place[...] = hot
    targets = jnp.broadcast_to((target[...] + 1).astype(F32), (8, rows))
    lanes = lax.dot_general(
        targets, hot, (((1,), (1,)), ((), ())), precision=HIGHEST, preferred_element_type=F32
    )
    row = lax.broadcasted_iota(jnp.int32, (8, 4 * CHUNK), 0)
    lane = lax.broadcasted_iota(jnp.int32, (8, 4 * CHUNK), 1)
    for j in range(blocks):
        group = lanes[:, j // 4 * 4 * CHUNK : (j // 4 + 1) * 4 * CHUNK]
        group = jnp.where(lane // CHUNK == j % 4, group, 0.0)
        group = pltpu.roll(group, lax.rem(me - j + 4 * blocks, 4) * CHUNK, 1)
        meta[j] = jnp.where(row == me // 4, group, 0.0)


def inner_kernel(
    blocks, spans, edges, spread, jacobian, owner, target, p, src, vel, yl, yr, *outs
):
    p0, s0, v0, w0, p1, p2, p3, place, meta, idx = outs
    plan(blocks, owner, target, place, meta, idx)
    fields, depth, rows, z = p.shape
    here = Place(rows, blocks, spans)
    ext = here.ext
    fluid = Fluid(spread, jacobian, fields)
    inside = here.inside(z)
    for name, buf, ref in (("p", p0, p), ("src", s0, src), ("vel", v0, vel)):
        for f in range(ref.shape[0]):
            for i in range(depth):

                def store(sl, x, buf=buf, f=f, i=i):
                    buf[f, i, sl] = x

                sl = edges.fluid[name, f, i]
                here.fill(store, ref[f, i], yl[sl], yr[sl])
    for i in range(depth):
        us = v0[0, i, ext] + v0[1, i, ext] + v0[2, i, ext]
        for f in range(fields):
            w0[f, i, ext] = jnp.where(inside, DAMPING / fluid.diagonal(f, us), 0.0)
    for level, (old, new) in enumerate(((p0, p1), (p1, p2), (p2, p3))):
        for i in range(level + 1, depth - 1 - level):
            fluid.advance(
                at(old, i - level),
                at(old, i - level - 1),
                at(old, i - level + 1),
                speeds(v0, i),
                at(w0, i),
                at(s0, i),
                ext,
                into(new, i - level - 1),
            )


def inner_solid_kernel(blocks, spans, edges, fields, t, heat, k, yl, yr, _, *refs):
    te, he, so, ti, tb, sqi, dg, ws, ta, tc, qa, qc = refs
    thick, rows, z = t.shape
    here = Place(rows, blocks, spans)
    ext = here.ext
    for name, buf, ref, scale in (("t", te, t, 1.0), ("k", he, k, 0.5), ("heat", so, heat, 1.0)):
        for i in range(thick):

            def store(sl, x, buf=buf, i=i, scale=scale):
                buf[i, sl] = scale * x

            sl = edges.solid[name, i]
            here.fill(store, ref[i], yl[sl], yr[sl])
    for i in range(1, thick - 1):
        h = he[i, ext]
        diagonal = 6.0 * h + around(he, i, ext)
        dg[i, ext] = diagonal
        ws[i, ext] = solid_weight(h, diagonal)
    for i in range(thick):
        qa[i, ext] = he[i, ext] * te[i, ext]
    old, oldq, new, newq = te, qa, ta, qc
    total = None
    for level in range(SWEEPS):
        last = level == SWEEPS - 1
        sl = here.own if last else ext
        for i in range(level + 1, thick - 1 - level):
            h, q = he[i, sl], old[i, sl]
            res = so[i, sl] - dg[i, sl] * q + h * around(old, i, sl) + around(oldq, i, sl)
            value = q + ws[i, sl] * res
            if last:
                tb[i - SWEEPS] = value
                square = res * res
                total = square if total is None else total + square
            else:
                new[i, sl] = value
                newq[i, sl] = h * value
        if not last:
            one = level + 1
            for j, i in enumerate((one, one + 1, thick - 2 - one, thick - 1 - one)):
                ti[level, j] = new[i]
            old, new = new, (tc if new is ta else ta)
            oldq, newq = newq, oldq
    sqi[...] = jnp.zeros_like(sqi)
    sqi[fields : fields + 1] = jnp.sum(total, axis=0, keepdims=True)


def cone_kernel(blocks, spans, sent, solid, spread, jacobian, *refs):
    p0, s0, v0, w0, p1, te, he, so, ti, dg, ws, xe, xn = refs[:13]
    back, n2, c2, c3, d1, d2, vm, wm, sl_, t0, t1, t2, t3, dl, wl = refs[13:28]
    l0, n1, qa = refs[28:]
    fields, z = p0.shape[0], p0.shape[3]
    rows = p0.shape[2] - 2 * (B + W)
    here = Place(rows, blocks, spans)
    ext, own, tall = here.ext, here.own, here.tall
    fluid = Fluid(spread, jacobian, fields)
    inside = jnp.logical_and(here.inside(z), jnp.logical_not(here.no_left))
    corner = 0
    for f in range(fields):

        def store(sl, x, f=f):
            l0[f, sl] = x

        n = corner + f * 2 * W
        here.fill(
            store, xe[f * rows : (f + 1) * rows], xn[n : n + W], xn[n + W : n + 2 * W], here.no_left
        )
    for c in range(3):

        def store(sl, x, c=c):
            vm[c, sl] = x

        n = corner + (fields + c) * 2 * W
        m = (fields + c) * rows
        here.fill(store, xe[m : m + rows], xn[n : n + W], xn[n + W : n + 2 * W])
    um = [vm[c, ext] for c in range(3)]
    usm = um[0] + um[1] + um[2]
    for f in range(fields):
        wm[f, ext] = jnp.where(inside, DAMPING / fluid.diagonal(f, usm), 0.0)
    def sum_of(level, ref):
        def read(f, sl):
            n = sent.window(level - 1, f).start + sl.start - B
            return unless(here.no_left, xn[n : n + 8]) + ref[f, sl]

        return read

    def plane(cur, i, left, right, store, sl=ext):
        fluid.advance(cur, left, right, speeds(v0, i), at(w0, i), at(s0, i), sl, store)

    outer = [lambda sl, c=c: vm[c, sl] for c in range(3)]
    plane(at(p0, 0), 0, flat(l0), at(p0, 1), into_flat(n1))
    for f in range(fields):
        d1[f, ext] = wm[f, ext] * (fluid.d[f] + um[0]) * p0[f, 0, ext]
    plane(flat(n1), 0, sum_of(1, d1), at(p1, 0), into_flat(n2))
    plane(at(p1, 0), 1, flat(n1), at(p1, 1), into_flat(c2))
    fluid.advance(flat(d1), None, flat(n1), outer, flat(wm), None, ext, into_flat(d2))
    plane(flat(n2), 0, sum_of(2, d2), flat(c2), into_flat(c3))
    n = solid.size()
    for reach, read in (
        (3, at(p0, 0)),
        (2, flat(n1)),
        (1, flat(n2)),
        (0, flat(c3)),
    ):
        size = rows + 2 * reach
        for f in range(fields):
            back[n : n + size] = read(f, here.reach(reach))
            n = n + size
    corner = corner + (fields + 3) * 2 * W
    early = (fields + 5) * rows
    zero = jnp.zeros((W, z), F32)
    hl, sl_ = sl_.at[0], sl_.at[1]
    for buf, near, scale in ((t0, 4, 1.0), (hl, 4, 0.5), (sl_, 3, 1.0)):
        for i in range(near):

            def store(sl, x, buf=buf, j=4 - near + i, scale=scale):
                buf[j, sl] = scale * x

            if i > 0:
                low, high = xn[corner : corner + W], xn[corner + W : corner + 2 * W]
                corner = corner + 2 * W
            else:
                low, high = zero, zero
            here.fill(store, xe[early : early + rows], low, high, here.no_left)
            early = early + rows

    def h_of(i, sl):
        return hl[i + 4, sl] if i < 0 else he[i, sl]

    for i in range(-3, 1):
        dl[i + 3, ext] = solid_diagonal(h_of, i, ext)
        wl[i + 3, ext] = solid_weight(h_of(i, ext), dl[i + 3, ext])
    for j in range(4, 6):
        t0[j] = te[j - 4]
    for level, (old, new) in enumerate(((t0, t1), (t1, t2), (t2, t3))):
        for j in range(6):
            qa[j, ext] = h_of(level - 4 + j, ext) * old[j, ext]
        for j in range(4):
            i = level - 3 + j
            q = old[j + 1, ext]
            res = sl_[i + 4, ext] if i < 0 else so[i, ext]
            diagonal, w = (dl, wl) if i <= 0 else (dg, ws)
            m = i + 3 if i <= 0 else i
            res = res - diagonal[m, ext] * q
            res = res + h_of(i, ext) * around(old, j + 1, ext) + around(qa, j + 1, ext)
            new[j, ext] = q + w[m, ext] * res
        for j in range(4, 6):
            new[j] = ti[level, j - 4]
    for level, (ref, i) in enumerate(((he, 0), (he, 1), (t0, 4), (t1, 3), (t2, 2), (t3, 1))):
        sl = solid.window(level, 0)
        reach = solid.reaches[level]
        back[sl.start + W - reach : sl.stop - W + reach] = ref[i, here.reach(reach)]


def flux_kernel(blocks, spans, sent, spread, jacobian, *refs):
    s0, v0, w0, p2, p3, n2, c2, c3, d1, d2, vm, wm, xe, xn, coef, hot, meta = refs[:17]
    parts, left, sq, m3, d3 = refs[17:]
    fields, rows, z = left.shape[0], left.shape[2], left.shape[3]
    here = Place(rows, blocks, spans)
    ext, own = here.ext, here.own
    fluid = Fluid(spread, jacobian, fields)
    m = (fields + 3) * rows
    u0mm, usmm = xe[m : m + rows], xe[m + rows : m + 2 * rows]
    outer = [lambda sl, c=c: vm[c, sl] for c in range(3)]

    def third(f, sl):
        n = sent.window(2, f).start + sl.start - B
        return unless(here.no_left, xn[n : n + 8]) + d3[f, sl]

    def plane(cur, i, before, after, store, sl=ext):
        fluid.advance(cur, before, after, speeds(v0, i), at(w0, i), at(s0, i), sl, store)

    def farther(f, sl):
        n = sl.start - own.start
        w = unless(here.no_left, DAMPING / fluid.diagonal(f, usmm[n : n + 8]))
        return w * (fluid.d[f] + u0mm[n : n + 8]) * d1[f, sl]

    fluid.advance(flat(d2), farther, flat(n2), outer, flat(wm), None, own, into_flat(d3))
    plane(flat(c2), 1, flat(n2), at(p2, 0), into(m3, 0))
    plane(at(p2, 0), 2, flat(c2), at(p2, 1), into(m3, 1))
    squares = [None] * fields
    third_of = [flat(c3), at(m3, 0), at(m3, 1), at(p3, 0), at(p3, 1)]
    for i in range(4):

        def final(f, sl, res, value, i=i):
            left[f, i, sl.start - own.start : sl.stop - own.start] = value
            square = res * res
            squares[f] = square if squares[f] is None else squares[f] + square

        plane(third_of[i], i, third_of[i - 1] if i > 0 else third, third_of[i + 1], final, own)
    sq[...] = jnp.zeros_like(sq)
    for f in range(fields):
        sq[f : f + 1] = jnp.sum(squares[f], axis=0, keepdims=True)
    flux = coef[0] * left[fields - 1, 0]
    parts[...] = jnp.dot(hot[...], flux, precision=HIGHEST, preferred_element_type=F32)
    for j in range(blocks):
        parts[j * CHUNK + 2 * CAP : (j + 1) * CHUNK] = meta[j]


def rest_kernel(blocks, spans, sent, spread, jacobian, *refs):
    p0, s0, v0, w0, p1, p2, p3, left, sqb, xn, _, gas, sq, n1, n2, n3 = refs
    fields, depth = gas.shape[0], gas.shape[1]
    rows = gas.shape[2]
    here = Place(rows, blocks, spans)
    ext, own, tall = here.ext, here.own, here.tall
    fluid = Fluid(spread, jacobian, fields)
    def arrived(level):
        def read(f, sl):
            n = sent.window(level, f).start + sl.start - B
            return unless(here.no_right, xn[n : n + 8])

        return read

    known = [{i: (p0, i) for i in range(depth)}, {}, {}, {}]
    for level, buf in enumerate((p1, p2, p3)):
        for i in range(level + 1, depth - 1 - level):
            known[level + 1][i] = (buf, i - level - 1)

    def read(level, i):
        ref, j = known[level][i]
        return at(ref, j)

    def plane(level, i, store, sl=ext):
        fluid.advance(
            read(level, i),
            read(level, i - 1),
            read(level, i + 1) if i < depth - 1 else arrived(level),
            speeds(v0, i),
            at(w0, i),
            at(s0, i),
            sl,
            store,
        )

    todo = ((depth - 1,), (depth - 2, depth - 1), (depth - 3, depth - 2, depth - 1))
    for level, new in enumerate((n1, n2, n3)):
        for j, i in enumerate(todo[level]):
            plane(level, i, into(new, j))
            known[level + 1][i] = (new, j)
    total = [None] * fields
    for f in range(fields):
        for i in range(4):
            gas[f, i] = left[f, i]
    for i in range(4, depth):

        def final(f, sl, res, value, i=i):
            gas[f, i, sl.start - own.start : sl.stop - own.start] = value
            square = res * res
            total[f] = square if total[f] is None else total[f] + square

        plane(3, i, final, own)
    sq[...] = sqb[...]
    for f in range(fields):
        sq[f : f + 1] = sq[f : f + 1] + jnp.sum(total[f], axis=0, keepdims=True)


def solid_kernel(
    blocks, spans, sent, te, he, so, ti, tbi, sqi, dg, ws, sl_, tl0, tl1, tl2, tl3, dl, wl, xb, _, *refs
):
    tb, rb, sq, rh, rd, rw = refs[:6]
    hr, dr, wr, ta, tc, qa = refs[6:]
    thick, rows, z = tb.shape
    here = Place(rows, blocks, spans)
    ext, own, tall = here.ext, here.own, here.tall
    hl = sl_.at[0]

    def arrived(n):
        return unless(here.no_right, xb[sent.window(n, 0)])

    for j in range(2):
        hr[j, ext] = arrived(j)

    def h_of(i, sl):
        if i < 0:
            return hl[i + 4, sl]
        return he[i, sl] if i < thick else hr[i - thick, sl]

    for j in range(2):
        i = thick - 1 + j
        dr[j, ext] = solid_diagonal(h_of, i, ext)
        wr[j, ext] = solid_weight(h_of(i, ext), dr[j, ext])

    def d_of(left, inside, right, i, sl):
        if i <= 0:
            return left[i + 3, sl]
        return inside[i, sl] if i < thick - 1 else right[i - thick + 1, sl]

    def residual(old, j, i, sl):
        res = so[i, sl] - d_of(dl, dg, dr, i, sl) * old[j, sl]
        return res + h_of(i, sl) * around(old, j, sl) + around(qa, j, sl)

    sums = None
    for j in range(6):
        qa[j, ext] = h_of(j - 1, ext) * tl3[j, ext]
    for i in range(4):
        res = residual(tl3, i + 1, i, own)
        tb[i] = tl3[i + 1, own] + d_of(wl, ws, wr, i, own) * res
        if i < 3:
            rb[i] = res
        else:
            sums = res * res
    old, new = ta, tc
    old[0], old[1] = te[thick - 2], te[thick - 1]
    old[2, ext] = arrived(2)
    for level in range(SWEEPS):
        last = level == SWEEPS - 1
        sl = own if last else ext
        low = thick - 2 - level
        for j in range(level + 3):
            qa[j, ext] = h_of(low + j, ext) * old[j, ext]
        for j in range(1, level + 2):
            i = low + j
            res = residual(old, j, i, sl)
            value = old[j, sl] + d_of(wl, ws, wr, i, sl) * res
            if last:
                tb[i] = value
                rb[i - (thick - 7)] = res
            else:
                new[j + 1, ext] = value
        if not last:
            for j in range(2):
                new[j] = ti[level, j + 2]
            new[level + 3, ext] = arrived(3 + level)
            old, new = new, old
    for i in range(SWEEPS, thick - SWEEPS):
        tb[i] = tbi[i - SWEEPS]
    sq[...] = sqi[...]
    n = sq.shape[0] - 3
    sq[n : n + 1] = sq[n : n + 1] + jnp.sum(sums, axis=0, keepdims=True)
    for region in range(2):
        for j in range(5):
            i = j - 2 if region == 0 else thick - 4 + j
            rh[region, j, ext] = h_of(i, ext)
            rd[region, j, ext] = d_of(dl, dg, dr, i, ext)
            rw[region, j, ext] = d_of(wl, ws, wr, i, ext)


def surface_kernel(blocks, arrived, surface, yf, yb):
    rows = surface.shape[0] // 2
    meta = arrived[0, 2 * CAP :]
    for j in range(1, blocks):
        meta = meta + arrived[j, 2 * CAP :]
    row = lax.broadcasted_iota(jnp.int32, (2 * rows, 4 * CHUNK), 0)
    slot = lax.broadcasted_iota(jnp.int32, (2 * rows, 4 * CHUNK), 1) % CHUNK
    row = row + 1 - jnp.where(slot < CAP, 0, rows)
    row = jnp.where((row >= 1) & (row <= rows), row, -1).astype(F32)
    whole = None
    for j in range(0, blocks, 4):
        sent = jnp.concatenate([arrived[j + m] for m in range(4)], axis=0)
        hot = jnp.where(row == meta[j // 4 : j // 4 + 1], 1.0, 0.0)
        got = jnp.dot(hot, sent, precision=HIGHEST, preferred_element_type=F32)
        whole = got if whole is None else whole + got
    surface[...] = whole
    yf[:W] = whole[rows - W : rows]
    yf[W:] = whole[2 * rows - W :]
    yb[:W] = whole[:W]
    yb[W:] = whole[rows : rows + W]


def response_kernel(
    blocks, spans, fields, surface, yl, yr, rh, rd, rw, tb, rb, sqf, sqs, tn, out, da, db, hd, so
):
    thick, rows, z = tb.shape
    here = Place(rows, blocks, spans)
    ext, own = here.ext, here.own
    for buf in (da, db, hd):
        buf[...] = jnp.zeros_like(buf)
    sq = sqf[...] + sqs[...]
    gained = jnp.zeros((rows, z), F32)
    for region in range(2):

        def store(sl, x, region=region):
            so[region, sl] = x

        edge = slice(region * W, (region + 1) * W)
        here.fill(store, surface[region * rows : (region + 1) * rows], yl[edge], yr[edge])

    needed = (((2,), (1, 2, 3), (1, 2, 3, 4), (3, 4, 5)), ((4,), (3, 4, 5), (2, 3, 4, 5), (1, 2, 3, 4)))
    for i in range(3, thick - 4):
        tn[i] = tb[i]
    for region in range(2):
        old, new = da, db
        source = 2 if region == 0 else 4
        for sweep in range(SWEEPS):
            final = sweep == SWEEPS - 1
            for j in needed[region][sweep]:
                res = so[region, ext] if j == source else None
                h, w = rh[region, j - 1, ext], rw[region, j - 1, ext]
                if sweep > 0:
                    q = old[region, j, ext]
                    flow = h * around(old.at[region], j, ext) + around(hd.at[region], j, ext) - rd[region, j - 1, ext] * q
                    res = flow if res is None else res + flow
                    change = q + w * res
                else:
                    change = w * res
                if final:
                    i = j - 3 if region == 0 else thick - 5 + j
                    kept = i if region == 0 else 2 + j
                    mine = slice(W, W + rows)
                    tn[i] = tb[i] + change[mine]
                    full = rb[kept] + res[mine]
                    gained = gained + full * full
                else:
                    new[region, j, ext] = change
            if not final:
                for j in needed[region][sweep]:
                    hd[region, j, ext] = rh[region, j - 1, ext] * new[region, j, ext]
                old, new = new, old
    extra = jnp.sum(gained, axis=0, keepdims=True)
    row = lax.broadcasted_iota(jnp.int32, sq.shape, 0)
    sq = sq + jnp.where(row == fields, extra, 0.0)
    for j in range(blocks):
        out[j, :rows] = tn[thick - 1]
        out[j, rows:] = sq


def squares_kernel(blocks, rows, arrived, sq):
    whole = arrived[0, rows:]
    for j in range(1, blocks):
        whole = whole + arrived[j, rows:]
    sq[...] = whole


def return_kernel(blocks, arrived, idx, coef, gas, t, gas_out, t_out, plane, sems):
    fields, rows = gas.shape[0], gas.shape[2]
    last = fields - 1
    copies = [
        pltpu.make_async_copy(gas.at[pl.ds(0, last)], gas_out.at[pl.ds(0, last)], sems.at[0]),
        pltpu.make_async_copy(
            gas.at[last, pl.ds(1, gas.shape[1] - 1)],
            gas_out.at[last, pl.ds(1, gas.shape[1] - 1)],
            sems.at[1],
        ),
        pltpu.make_async_copy(t, t_out, sems.at[2]),
    ]
    for copy in copies:
        copy.start()
    row = lax.broadcasted_iota(jnp.int32, (rows, rows), 0).astype(F32)
    taken = None
    for j in range(blocks):
        hot = jnp.where(idx[...] - float(j * rows) == row, 1.0, 0.0)
        got = lax.dot_general(
            hot,
            arrived[j, :rows],
            (((0,), (0,)), ((), ())),
            precision=HIGHEST,
            preferred_element_type=F32,
        )
        taken = got if taken is None else taken + got
    plane[...] = gas[last, 0] + coef[0] * taken
    copy = pltpu.make_async_copy(plane, gas_out.at[last, 0], sems.at[3])
    copy.start()
    for other in copies:
        other.wait()
    copy.wait()


def shards(
    blocks,
    spans,
    fluid_adjoint_in,
    fluid_source,
    velocity,
    diffusion,
    jacobian,
    wall_coefficient,
    metal_costate_prior,
    solid_source,
    conductivity,
    tile_owner,
    tile_target,
):
    p, src, vel = fluid_adjoint_in, fluid_source, velocity
    t, heat, k = metal_costate_prior, solid_source, conductivity
    fields, depth, rows, z = p.shape
    thick = t.shape[0]
    tall = rows + 2 * W
    buf = tall + 2 * B
    forward = {
        "blk": [(i, (i + 1) % blocks) for i in range(blocks)],
        "span": [(i, (i + 1) % spans) for i in range(spans)],
    }
    backward = {axis: [(j, i) for i, j in pairs] for axis, pairs in forward.items()}

    def ahead(x, axis):
        return lax.ppermute(x, axis, forward[axis])

    def behind(x, axis):
        return lax.ppermute(x, axis, backward[axis])

    edges = Edges(fields, depth, thick)
    inputs = [p, src, vel, t, heat, k]
    p, src, vel, t, heat, k, yf, yb, xf, zf, zb = call(
        functools.partial(early_kernel, edges),
        held(*[x.shape for x in inputs])
        + [(edges.size, z)] * 2
        + [((fields + 16) * rows, z)]
        + [(edges.solid_size, z)] * 2,
        [pltpu.SemaphoreType.DMA((6,))],
        [HBM] * 6,
        *[pltpu.with_memory_space_constraint(x, pltpu.HBM) for x in inputs],
    )
    yl, yr = ahead(yf, "span"), behind(yb, "span")
    xe = ahead(xf, "blk")
    sent_ahead = Arrivals((fields + 11) * 2 * W, rows, fields, (2, 1, 0))
    (out,) = call(
        functools.partial(ahead_kernel, blocks, spans, edges),
        [(sent_ahead.size(), z)],
        [(fields, 4, buf, z), (fields, 3, buf, z), (fields, 2, buf, z), (fields, 3, buf, z)]
        + [(3, 3, buf, z), (fields, 3, buf, z)],
        [SMEM] * 2 + [VMEM] * 5,
        diffusion,
        jacobian,
        p,
        src,
        vel,
        yl,
        yr,
        cost=COSTS[1],
    )
    xn = ahead(out, "blk")
    full = (fields, depth, buf, z)
    part = [(fields, depth - 2 * (level + 1), buf, z) for level in range(3)]
    solid = (thick, buf, z)
    p0, s0, v0, w0, p1, p2, p3, place, meta, idx = call(
        functools.partial(inner_kernel, blocks, spans, edges),
        held(full, full, (3, depth, buf, z), full, *part)
        + held((blocks * CHUNK, rows), (blocks, 8, z), (1, rows)),
        [],
        [SMEM] * 2 + [VMEM] * 7,
        diffusion,
        jacobian,
        tile_owner.reshape(1, rows),
        tile_target,
        p,
        src,
        vel,
        yl,
        yr,
        cost=COSTS[2],
    )
    zl, zr = ahead(zf, "span"), behind(zb, "span")
    te, he, so, ti, tb, sqi, dg, ws = call(
        functools.partial(inner_solid_kernel, blocks, spans, edges, fields),
        held(solid, solid, solid, (3, 4, buf, z), (thick - 2 * SWEEPS, rows, z), (8, z), solid, solid),
        [solid] * 4,
        [VMEM] * 6,
        t,
        heat,
        k,
        zl,
        zr,
        idx,
        cost=COSTS[2],
    )
    solid_back = Arrivals(8, rows, 1, (3, 1, 3, 2, 1, 0))
    sent_back = Arrivals(solid_back.size(), rows, fields, (3, 2, 1, 0))
    one, six = (fields, buf, z), (6, buf, z)
    back, n2, c2, c3, d1, d2, vm, wm, sl_, *lefts = call(
        functools.partial(cone_kernel, blocks, spans, sent_ahead, solid_back),
        [(sent_back.size(), z)]
        + held(one, one, one, one, one, (3, buf, z), one, (2, 4, buf, z))
        + held(six, six, six, six, (4, buf, z), (4, buf, z)),
        [one] * 2 + [six],
        [SMEM] * 2 + [VMEM] * 13,
        diffusion,
        jacobian,
        p0,
        s0,
        v0,
        w0,
        p1,
        te,
        he,
        so,
        ti,
        dg,
        ws,
        xe,
        xn,
        cost=COSTS[3],
    )
    xr = lax.ppermute(back, "blk", backward["blk"][: blocks - 1])
    parts, half, sq = call(
        functools.partial(flux_kernel, blocks, spans, sent_ahead),
        [(blocks * CHUNK, z)] + held((fields, 4, rows, z), (8, z)),
        [(fields, 2, buf, z), one],
        [SMEM] * 2 + [VMEM] * 17,
        diffusion,
        jacobian,
        s0,
        v0,
        w0,
        p2,
        p3,
        n2,
        c2,
        c3,
        d1,
        d2,
        vm,
        wm,
        xe,
        xn,
        wall_coefficient,
        place,
        meta,
        cost=COSTS[2],
    )
    arrived = lax.all_to_all(parts.reshape(blocks, CHUNK, z), "blk", 0, 0)
    surface, yf, yb = call(
        functools.partial(surface_kernel, blocks),
        [(2 * rows, z), (2 * W, z), (2 * W, z)],
        [],
        [VMEM],
        arrived,
    )
    yl, yr = ahead(yf, "span"), behind(yb, "span")
    gas, sqf = call(
        functools.partial(rest_kernel, blocks, spans, sent_back),
        held(p.shape, (8, z)),
        [(fields, 1, buf, z), (fields, 2, buf, z), (fields, 3, buf, z)],
        [SMEM] * 2 + [VMEM] * 11,
        diffusion,
        jacobian,
        p0,
        s0,
        v0,
        w0,
        p1,
        p2,
        p3,
        half,
        sq,
        xr,
        yf,
        cost=COSTS[4],
    )
    two, edge = (2, buf, z), (2, 5, buf, z)
    tb, rb, sqs, rh, rd, rw = call(
        functools.partial(solid_kernel, blocks, spans, solid_back),
        held(t.shape, (7, rows, z), (8, z), edge, edge, edge),
        [two] * 3 + [six] * 3,
        [VMEM] * 17,
        te,
        he,
        so,
        ti,
        tb,
        sqi,
        dg,
        ws,
        sl_,
        *lefts,
        xr,
        yf,
        cost=COSTS[5],
    )
    region = (2, 7, buf, z)
    t, out = call(
        functools.partial(response_kernel, blocks, spans, fields),
        held(t.shape, (blocks, rows + 8, z)),
        [region] * 3 + [(2, buf, z)],
        [VMEM] * 10,
        surface,
        yl,
        yr,
        rh,
        rd,
        rw,
        tb,
        rb,
        sqf,
        sqs,
    )
    arrived = lax.all_to_all(out, "blk", 0, 0)
    (sq,) = call(
        functools.partial(squares_kernel, blocks, rows), held((8, z)), [], [VMEM], arrived
    )
    others = [
        lax.ppermute(sq, "span", [(i, i ^ step) for i in range(spans)]) for step in range(1, spans)
    ]
    gas, t = call(
        functools.partial(return_kernel, blocks),
        [gas.shape, t.shape],
        [(rows, z), pltpu.SemaphoreType.DMA((4,))],
        [VMEM] * 5,
        arrived,
        idx,
        wall_coefficient,
        gas,
        t,
        out_specs=[pl.BlockSpec(memory_space=pl.ANY)] * 2,
        cost=2.0,
    )
    sq = functools.reduce(jnp.add, others, sq)
    everyone = blocks * spans
    counts = [float(depth * rows * z * everyone)] * fields + [float(thick * rows * z * everyone)]
    totals = jnp.sum(sq[: fields + 1], axis=1)
    norms = jnp.sqrt(totals / jnp.array(counts, F32))
    return gas, t, norms


def solution(mesh):
    placed = (
        P(None, "blk", "span", None),
        P(None, "blk", "span", None),
        P(None, "blk", "span", None),
        P(),
        P(),
        P("blk", "span", None),
        P("blk", "span", None),
        P("blk", "span", None),
        P("blk", "span", None),
        P("span", "blk", None),
        P("span", "blk"),
    )
    return jax.shard_map(
        functools.partial(shards, mesh.shape["blk"], mesh.shape["span"]),
        mesh=mesh,
        in_specs=placed,
        out_specs=(P(None, "blk", "span", None), P("blk", "span", None), P()),
        check_vma=False,
    )
```

```python
import functools

import jax
import jax.numpy as jnp
from jax import lax
from jax.experimental import pallas as pl
from jax.experimental.pallas import tpu as pltpu
from jax.sharding import PartitionSpec as P

SWEEPS = 4
DAMPING = 0.8
HIGHEST = lax.Precision.HIGHEST
F32 = jnp.float32
VMEM = pl.BlockSpec(memory_space=pltpu.VMEM)
SMEM = pl.BlockSpec(memory_space=pltpu.SMEM)
HBM = pl.BlockSpec(memory_space=pltpu.HBM)
COSTS = (1.0, 30.0, 0.01, 2.0, 3.0, 3.0)
LIMIT = 12 * 1024 * 1024
W = 4
CAP = 12
CHUNK = 32
B = 8


def held(*shapes):
    return [pltpu.VMEM(s, F32) for s in shapes]


def call(kernel, outs, scratch, specs, *args, out_specs=None, cost=1.0):
    return pl.pallas_call(
        kernel,
        out_shape=[jax.ShapeDtypeStruct(s, F32) if isinstance(s, tuple) else s for s in outs],
        in_specs=specs,
        out_specs=out_specs or [VMEM] * len(outs),
        scratch_shapes=[pltpu.VMEM(s, F32) if isinstance(s, tuple) else s for s in scratch],
        compiler_params=pltpu.CompilerParams(vmem_limit_bytes=LIMIT),
        cost_estimate=pl.CostEstimate(
            flops=int(cost * 1e6), bytes_accessed=int(cost * 3e6), transcendentals=0
        ),
    )(*args)


def beside(x):
    lane = lax.broadcasted_iota(jnp.int32, x.shape, 1)
    last = x.shape[1] - 1
    before = jnp.where(lane == 0, 0.0, pltpu.roll(x, 1, 1))
    after = jnp.where(lane == last, 0.0, pltpu.roll(x, last, 1))
    return before, after


def unless(flag, x):
    return jnp.where(flag, 0.0, x)


class Place:
    def __init__(self, rows, blocks, spans):
        b, s = lax.axis_index("blk"), lax.axis_index("span")
        self.rows, self.tall = rows, rows + 2 * W
        self.no_left, self.no_right = b == 0, b == blocks - 1
        self.no_low, self.no_high = s == 0, s == spans - 1
        self.ext = slice(B, B + self.tall)
        self.own = slice(B + W, B + W + rows)
        self.low = slice(B, B + W)
        self.high = slice(B + W + rows, B + self.tall)

    def reach(self, by):
        return slice(B + W - by, B + W + self.rows + by)

    def fill(self, store, own, low, high, hide=None):
        no_low, no_high = self.no_low, self.no_high
        if hide is not None:
            own, no_low, no_high = unless(hide, own), no_low | hide, no_high | hide
        store(self.own, own)
        store(slice(self.low.stop - low.shape[0], self.low.stop), unless(no_low, low))
        store(slice(self.high.start, self.high.start + high.shape[0]), unless(no_high, high))

    def inside(self, z):
        row = lax.broadcasted_iota(jnp.int32, (self.tall, z), 0)
        out = ((row < W) & self.no_low) | ((row >= W + self.rows) & self.no_high)
        return jnp.logical_not(out)


def beyond(sl, by):
    return slice(sl.start + by, sl.stop + by)


def rows_at(ref, n, count):
    return ref[n : n + count]


class Arrivals:
    def __init__(self, first, rows, fields, reaches):
        self.first, self.rows, self.fields, self.reaches = first, rows, fields, reaches

    def window(self, level, f, ext=True):
        n = self.first
        for reach in self.reaches[:level]:
            n = n + self.fields * (self.rows + 2 * reach)
        reach = self.reaches[level]
        n = n + f * (self.rows + 2 * reach)
        if ext:
            return slice(n + reach - W, n + reach + W + self.rows)
        return slice(n + reach, n + reach + self.rows)

    def size(self):
        return self.first + sum(self.fields * (self.rows + 2 * reach) for reach in self.reaches)


class Edges:
    def __init__(self, fields, depth, thick):
        n, later = 0, 0
        self.fluid, self.late, self.outer, self.solid = {}, {}, {}, {}
        for name, count, reach, near in (
            ("p", fields, W, 4),
            ("src", fields, W - 1, 3),
            ("vel", 3, W - 1, 3),
        ):
            for f in range(count):
                for i in range(depth):
                    if i < depth - near:
                        self.late[name, f, i] = slice(later, later + reach)
                        later = later + reach
                    else:
                        self.fluid[name, f, i] = slice(n, n + reach)
                        n = n + reach
        for name, near, reach in (("t", 4, W), ("k", 4, W), ("heat", 3, W - 1)):
            for i in range(thick - near, thick):
                self.outer[name, i] = slice(n, n + reach)
                n = n + reach
        self.size = (n + 7) // 8 * 8
        for name, reach in (("t", W), ("k", W), ("heat", W - 1)):
            for i in range(thick):
                self.solid[name, i] = slice(later, later + reach)
                later = later + reach
        self.late_size = (later + 7) // 8 * 8


class Fluid:
    def __init__(self, spread, jacobian, fields):
        self.n = fields
        self.d = [spread[f] for f in range(fields)]
        self.jac = [[jacobian[f, g] for g in range(fields)] for f in range(fields)]

    def diagonal(self, f, us):
        return us + (6.0 * self.d[f] + self.jac[f][f])

    def advance(self, cur, left, right, vel, w, src, rows, store):
        for n in range(rows.start, rows.stop, 8):
            sl = slice(n, n + 8)
            u0, u1, u2 = (u(sl) for u in vel)
            us = u0 + u1 + u2
            centre = [cur(f, sl) for f in range(self.n)]
            for f in range(self.n):
                c = centre[f]
                zm, zp = beside(c)
                yp = cur(f, beyond(sl, 1))
                near = (cur(f, beyond(sl, -1)) + yp) + (zm + zp)
                if left is not None:
                    near = near + left(f, sl)
                res = u1 * yp + u2 * zp - self.diagonal(f, us) * c
                if right is not None:
                    xp = right(f, sl)
                    near = near + xp
                    res = res + u0 * xp
                res = res + self.d[f] * near
                for g in range(self.n):
                    if g != f:
                        res = res - self.jac[f][g] * centre[g]
                if src is not None:
                    res = res + src(f, sl)
                store(f, sl, res, c + w(f, sl) * res)


def at(ref, i):
    return lambda f, sl: ref[f, i, sl]


def flat(ref):
    return lambda f, sl: ref[f, sl]


def speeds(ref, i):
    return [lambda sl, c=c: ref[c, i, sl] for c in range(3)]


def into(ref, i):
    def store(f, sl, _, value):
        ref[f, i, sl] = value

    return store


def into_flat(ref):
    def store(f, sl, _, value):
        ref[f, sl] = value

    return store


def early_kernel(edges, *refs):
    bufs = refs[6:12]
    yf, yb, xf, zf, zb, sems = refs[12:]
    copies = [
        pltpu.make_async_copy(ref, buf, sems.at[j])
        for j, (ref, buf) in enumerate(zip(refs[:6], bufs, strict=True))
    ]
    for copy in copies:
        copy.start()
    p, src, vel, t, heat, k = bufs
    fields, depth, rows = p.shape[0], p.shape[1], p.shape[2]
    thick = t.shape[0]
    named = {"p": p, "src": src, "vel": vel, "t": t, "heat": heat, "k": k}

    def pack(up, down, places, names):
        for (name, *at_plane), sl in places.items():
            if name in names:
                ref, reach = named[name], sl.stop - sl.start
                up[sl] = ref[*at_plane, rows - reach :]
                down[sl] = ref[*at_plane, :reach]

    for j, name in enumerate(named):
        copies[j].wait()
        if j < 3:
            pack(yf, yb, edges.fluid, (name,))
            pack(zf, zb, edges.late, (name,))
    planes = [p[f, depth - 1] for f in range(fields)]
    planes += [vel[f, depth - 1] for f in range(3)]
    planes += [vel[0, depth - 2], vel[0, depth - 2] + vel[1, depth - 2] + vel[2, depth - 2]]
    planes += [t[thick - 1], t[thick - 2], k[thick - 1], k[thick - 2], k[thick - 3]]
    planes += [heat[thick - 1]]
    for j, plane in enumerate(planes):
        xf[j * rows : (j + 1) * rows] = plane
    for up, down, places in ((yf, yb, edges.outer), (zf, zb, edges.solid)):
        pack(up, down, places, named)


def ahead_kernel(blocks, spans, edges, solid, third, spread, jacobian, *refs):
    p, src, vel, t, heat, k, yl, yr, out, later = refs[:10]
    a0, a1, a2, sa, va, wa, ta, ha, so, qa, tb, qb = refs[10:]
    fields, depth, rows, z = p.shape
    at_place = Place(rows, blocks, spans)
    ext, own = at_place.ext, at_place.own
    fluid = Fluid(spread, jacobian, fields)
    inside = at_place.inside(z)

    def fill(buf, f, j, ref, name, i):
        def store(sl, x):
            buf[f, j, sl] = x

        sl = edges.fluid[name, f, i]
        at_place.fill(store, ref[f, i], yl[sl], yr[sl])

    for f in range(fields):
        for j in range(4):
            fill(a0, f, j, p, "p", depth - 4 + j)
        for j in range(3):
            fill(sa, f, j, src, "src", depth - 3 + j)
    for f in range(3):
        for j in range(3):
            fill(va, f, j, vel, "vel", depth - 3 + j)
    for j in range(3):
        us = va[0, j, ext] + va[1, j, ext] + va[2, j, ext]
        for f in range(fields):
            wa[f, j, ext] = jnp.where(inside, DAMPING / fluid.diagonal(f, us), 0.0)

    def step(old, i, store, j):
        fluid.advance(
            at(old, i),
            at(old, i - 1),
            None if j == 2 else at(old, i + 1),
            speeds(va, j),
            at(wa, j),
            at(sa, j),
            ext,
            store,
        )

    for j in range(3):
        step(a0, j + 1, into(a1, j), j)
    for j in range(1, 3):
        step(a1, j, into(a2, j - 1), j)
    corners = [edges.fluid["p", f, depth - 1] for f in range(fields)]
    corners += [edges.fluid["vel", c, depth - 1] for c in range(3)]
    thick = t.shape[0]
    corners += [edges.outer["t", thick - 1], edges.outer["t", thick - 2]]
    corners += [edges.outer["k", thick - 1], edges.outer["k", thick - 2]]
    corners += [edges.outer["heat", thick - 1]]
    n = 0
    for sl in corners:
        reach = sl.stop - sl.start
        out[n + W - reach : n + W] = yl[sl]
        out[n + W : n + W + reach] = yr[sl]
        n = n + 2 * W
    for reach, buf, j in ((2, a1, 2), (1, a2, 1)):
        size = rows + 2 * reach
        for f in range(fields):
            out[n : n + size] = buf[f, j, at_place.reach(reach)]
            n = n + size

    def last(f, sl, _, value):
        m = third.window(0, f).start + sl.start - B
        later[m : m + 8] = value

    fluid.advance(
        at(a2, 1), at(a2, 0), None, speeds(va, 2), at(wa, 2), at(sa, 2), own, last
    )
    for name, buf, ref, near, scale in (
        ("t", ta, t, 4, 1.0),
        ("k", ha, k, 4, 0.5),
        ("heat", so, heat, 3, 1.0),
    ):
        for j in range(4 - near, 4):
            i = thick - 4 + j

            def store(sl, x, buf=buf, j=j, scale=scale):
                buf[j, sl] = scale * x

            sl = edges.outer[name, i]
            at_place.fill(store, ref[i], yl[sl], yr[sl])
    for j in range(4):
        qa[j, ext] = ha[j, ext] * ta[j, ext]

    def h_of(j, sl):
        return ha[j, sl]

    kept = {}
    for j in (1, 2):
        h = ha[j, ext]
        diagonal = solid_diagonal(h_of, j, ext)
        w = solid_weight(h, diagonal)
        res = so[j, ext] - diagonal * ta[j, ext] + h * around(ta, j, ext) + around(qa, j, ext)
        tb[j, ext] = ta[j, ext] + w * res
        qb[j, ext] = h * tb[j, ext]
        kept[j] = (h, diagonal, w)
    tb[3] = jnp.zeros_like(tb[3])
    qb[3] = jnp.zeros_like(qb[3])
    h, diagonal, w = kept[2]
    res = so[2, ext] - diagonal * tb[2, ext] + h * around(tb, 2, ext) + around(qb, 2, ext)
    value = tb[2, ext] + w * res
    m = solid.window(0, 0).start + W - 1
    later[m : m + rows + 2] = tb[2, at_place.reach(1)]
    m = solid.window(1, 0).start + W
    later[m : m + rows] = value[W : W + rows]


def around(buf, j, sl):
    zm, zp = beside(buf[j, sl])
    return (
        (buf[j - 1, sl] + buf[j + 1, sl])
        + (buf[j, beyond(sl, -1)] + buf[j, beyond(sl, 1)])
        + (zm + zp)
    )


def solid_diagonal(h_of, i, sl):
    zm, zp = beside(h_of(i, sl))
    near = (h_of(i - 1, sl) + h_of(i + 1, sl)) + (zm + zp)
    near = near + (h_of(i, beyond(sl, -1)) + h_of(i, beyond(sl, 1)))
    return 6.0 * h_of(i, sl) + near


def solid_weight(h, diagonal):
    return jnp.where(h > 0.0, DAMPING / jnp.where(h > 0.0, diagonal, 1.0), 0.0)


def plan(blocks, owner, target, place, meta, idx):
    rows = target.shape[1]
    me = lax.axis_index("blk")
    row = lax.broadcasted_iota(jnp.int32, (rows, rows), 0)
    lane = lax.broadcasted_iota(jnp.int32, (rows, rows), 1)
    owner = owner[...].astype(F32)
    column = jnp.where(row == lane, jnp.broadcast_to(owner, (rows, rows)), 0.0)
    column = jnp.sum(column, axis=1, keepdims=True)
    idx[...] = owner * rows + target[...].astype(F32)
    before = jnp.where((column == owner) & (row < lane), 1.0, 0.0)
    rank = jnp.sum(before, axis=0, keepdims=True)
    n = lax.broadcasted_iota(jnp.int32, (blocks * CHUNK, rows), 0)
    slot = n % CHUNK
    second = slot >= CAP
    named = n // CHUNK - jnp.where(second, 0, 1)
    at_rank = (slot - jnp.where(second, CAP, 0)).astype(F32)
    hot = jnp.where((owner == named.astype(F32)) & (rank == at_rank), 1.0, 0.0)
    hot = jnp.where(slot < 2 * CAP, hot, 0.0)
    place[...] = hot
    targets = jnp.broadcast_to((target[...] + 1).astype(F32), (8, rows))
    lanes = lax.dot_general(
        targets, hot, (((1,), (1,)), ((), ())), precision=HIGHEST, preferred_element_type=F32
    )
    row = lax.broadcasted_iota(jnp.int32, (8, 4 * CHUNK), 0)
    lane = lax.broadcasted_iota(jnp.int32, (8, 4 * CHUNK), 1)
    for j in range(blocks):
        group = lanes[:, j // 4 * 4 * CHUNK : (j // 4 + 1) * 4 * CHUNK]
        group = jnp.where(lane // CHUNK == j % 4, group, 0.0)
        group = pltpu.roll(group, lax.rem(me - j + 4 * blocks, 4) * CHUNK, 1)
        meta[j] = jnp.where(row == me // 4, group, 0.0)


def inner_kernel(
    blocks, spans, edges, spread, jacobian, owner, target, p, src, vel, yl, yr, zl, zr, *outs
):
    p0, s0, v0, w0, p1, place, meta, idx = outs
    plan(blocks, owner, target, place, meta, idx)
    fields, depth, rows, z = p.shape
    here = Place(rows, blocks, spans)
    ext = here.ext
    fluid = Fluid(spread, jacobian, fields)
    inside = here.inside(z)
    for name, buf, ref in (("p", p0, p), ("src", s0, src), ("vel", v0, vel)):
        for f in range(ref.shape[0]):
            for i in range(depth):

                def store(sl, x, buf=buf, f=f, i=i):
                    buf[f, i, sl] = x

                if (name, f, i) in edges.late:
                    sl = edges.late[name, f, i]
                    here.fill(store, ref[f, i], zl[sl], zr[sl])
                else:
                    sl = edges.fluid[name, f, i]
                    here.fill(store, ref[f, i], yl[sl], yr[sl])
    for i in range(depth):
        us = v0[0, i, ext] + v0[1, i, ext] + v0[2, i, ext]
        for f in range(fields):
            w0[f, i, ext] = jnp.where(inside, DAMPING / fluid.diagonal(f, us), 0.0)
    for i in (1, 2):
        fluid.advance(
            at(p0, i),
            at(p0, i - 1),
            at(p0, i + 1),
            speeds(v0, i),
            at(w0, i),
            at(s0, i),
            ext,
            into(p1, i - 1),
        )


def inner_solid_kernel(blocks, spans, edges, fields, t, heat, k, yl, yr, _, *refs):
    te, he, so, ti, tb, sqi, dg, ws, ta, tc, qa, qc = refs
    thick, rows, z = t.shape
    here = Place(rows, blocks, spans)
    ext = here.ext
    for name, buf, ref, scale in (("t", te, t, 1.0), ("k", he, k, 0.5), ("heat", so, heat, 1.0)):
        for i in range(thick):

            def store(sl, x, buf=buf, i=i, scale=scale):
                buf[i, sl] = scale * x

            sl = edges.solid[name, i]
            here.fill(store, ref[i], yl[sl], yr[sl])
    for i in range(1, thick - 1):
        h = he[i, ext]
        diagonal = 6.0 * h + around(he, i, ext)
        dg[i, ext] = diagonal
        ws[i, ext] = solid_weight(h, diagonal)
    for i in range(thick):
        qa[i, ext] = he[i, ext] * te[i, ext]
    old, oldq, new, newq = te, qa, ta, qc
    total = None
    for level in range(SWEEPS):
        last = level == SWEEPS - 1
        sl = here.own if last else ext
        for i in range(level + 1, thick - 1 - level):
            h, q = he[i, sl], old[i, sl]
            res = so[i, sl] - dg[i, sl] * q + h * around(old, i, sl) + around(oldq, i, sl)
            value = q + ws[i, sl] * res
            if last:
                tb[i - SWEEPS] = value
                square = res * res
                total = square if total is None else total + square
            else:
                new[i, sl] = value
                newq[i, sl] = h * value
        if not last:
            one = level + 1
            for j, i in enumerate((one, one + 1, thick - 2 - one, thick - 1 - one)):
                ti[level, j] = new[i]
            old, new = new, (tc if new is ta else ta)
            oldq, newq = newq, oldq
    sqi[...] = jnp.zeros_like(sqi)
    sqi[fields : fields + 1] = jnp.sum(total, axis=0, keepdims=True)


def cone_kernel(blocks, spans, sent, sent_solid, solid, spread, jacobian, *refs):
    p0, s0, v0, w0, p1, te, he, so, ti, dg, ws, xe, xn, xl = refs[:14]
    back, n2, c2, c3, d1, d2, vm, wm, sl_, t0, t1, t2, t3, dl, wl = refs[14:29]
    l0, n1, qa = refs[29:]
    fields, z = p0.shape[0], p0.shape[3]
    rows = p0.shape[2] - 2 * (B + W)
    here = Place(rows, blocks, spans)
    ext, own, tall = here.ext, here.own, here.tall
    fluid = Fluid(spread, jacobian, fields)
    inside = jnp.logical_and(here.inside(z), jnp.logical_not(here.no_left))
    corner = 0
    for f in range(fields):

        def store(sl, x, f=f):
            l0[f, sl] = x

        n = corner + f * 2 * W
        here.fill(
            store, xe[f * rows : (f + 1) * rows], xn[n : n + W], xn[n + W : n + 2 * W], here.no_left
        )
    for c in range(3):

        def store(sl, x, c=c):
            vm[c, sl] = x

        n = corner + (fields + c) * 2 * W
        m = (fields + c) * rows
        here.fill(store, xe[m : m + rows], xn[n : n + W], xn[n + W : n + 2 * W])
    um = [vm[c, ext] for c in range(3)]
    usm = um[0] + um[1] + um[2]
    for f in range(fields):
        wm[f, ext] = jnp.where(inside, DAMPING / fluid.diagonal(f, usm), 0.0)
    def sum_of(level, ref):
        def read(f, sl):
            n = sent.window(level - 1, f).start + sl.start - B
            return unless(here.no_left, xn[n : n + 8]) + ref[f, sl]

        return read

    def plane(cur, i, left, right, store, sl=ext):
        fluid.advance(cur, left, right, speeds(v0, i), at(w0, i), at(s0, i), sl, store)

    outer = [lambda sl, c=c: vm[c, sl] for c in range(3)]
    plane(at(p0, 0), 0, flat(l0), at(p0, 1), into_flat(n1))
    for f in range(fields):
        d1[f, ext] = wm[f, ext] * (fluid.d[f] + um[0]) * p0[f, 0, ext]
    plane(flat(n1), 0, sum_of(1, d1), at(p1, 0), into_flat(n2))
    plane(at(p1, 0), 1, flat(n1), at(p1, 1), into_flat(c2))
    fluid.advance(flat(d1), None, flat(n1), outer, flat(wm), None, ext, into_flat(d2))
    plane(flat(n2), 0, sum_of(2, d2), flat(c2), into_flat(c3))
    n = solid.size()
    for reach, read in (
        (3, at(p0, 0)),
        (2, flat(n1)),
        (1, flat(n2)),
        (0, flat(c3)),
    ):
        size = rows + 2 * reach
        for f in range(fields):
            back[n : n + size] = read(f, here.reach(reach))
            n = n + size
    corner = corner + (fields + 3) * 2 * W
    early = (fields + 5) * rows
    zero = jnp.zeros((W, z), F32)
    hl, sl_ = sl_.at[0], sl_.at[1]
    for buf, j, scale in ((t0, 1, 1.0), (t0, 0, 1.0), (hl, 3, 0.5), (hl, 2, 0.5), (hl, 1, 0.5), (sl_, 3, 1.0)):

        def store(sl, x, buf=buf, j=j, scale=scale):
            buf[j, sl] = scale * x

        low, high = zero, zero
        if buf is not hl or j > 1:
            low, high = xn[corner : corner + W], xn[corner + W : corner + 2 * W]
            corner = corner + 2 * W
        here.fill(store, xe[early : early + rows], low, high, here.no_left)
        early = early + rows

    def h_of(i, sl):
        return hl[i + 4, sl] if i < 0 else he[i, sl]

    for i in range(-2, 1):
        dl[i + 3, ext] = solid_diagonal(h_of, i, ext)
        wl[i + 3, ext] = solid_weight(h_of(i, ext), dl[i + 3, ext])

    def sweep(old, shift, new, i, j):
        q = old[i + shift, ext]
        diagonal, w, m = (dl, wl, i + 3) if i <= 0 else (dg, ws, i)
        res = (sl_[3, ext] if i < 0 else so[i, ext]) - diagonal[m, ext] * q
        res = res + h_of(i, ext) * around(old, i + shift, ext) + around(qa, i + shift, ext)
        new[j, ext] = q + w[m, ext] * res

    def weigh(old, count):
        for j in range(count):
            qa[j, ext] = h_of(j - 2, ext) * old[j, ext]

    t0[2], t0[3] = te[0], te[1]
    weigh(t0, 4)
    for i in (-1, 0):
        sweep(t0, 2, t1, i, i + 2)
    t1[0, ext] = unless(here.no_left, xl[sent_solid.window(0, 0)])
    t1[3], t1[4] = ti[0, 0], ti[0, 1]
    weigh(t1, 5)
    for i in (-1, 0, 1):
        sweep(t1, 2, t2, i, i + 2)
    t2[0, ext] = unless(here.no_left, xl[sent_solid.window(1, 0)])
    t2[0, ext] = t2[0, ext] + wl[1, ext] * (hl[2, ext] + hl[3, ext]) * t1[1, ext]
    t2[4], t2[5] = ti[1, 0], ti[1, 1]
    weigh(t2, 6)
    for i in (-1, 0, 1, 2):
        sweep(t2, 2, t3, i, i + 1)
    t3[4], t3[5] = ti[2, 0], ti[2, 1]
    for level, (ref, i) in enumerate(((he, 0), (he, 1), (t0, 2), (t1, 2), (t2, 2), (t3, 1))):
        sl = solid.window(level, 0)
        reach = solid.reaches[level]
        back[sl.start + W - reach : sl.stop - W + reach] = ref[i, here.reach(reach)]


def flux_kernel(blocks, spans, third_at, spread, jacobian, *refs):
    p0, s0, v0, w0, p1, n2, c2, c3, d1, d2, vm, wm, xe, xl, coef, hot, meta = refs[:17]
    parts, left, sq, q1, p2, p3, m3, d3 = refs[17:]
    depth = p0.shape[1]
    fields, rows, z = left.shape[0], left.shape[2], left.shape[3]
    here = Place(rows, blocks, spans)
    ext, own = here.ext, here.own
    fluid = Fluid(spread, jacobian, fields)
    m = (fields + 3) * rows
    u0mm, usmm = xe[m : m + rows], xe[m + rows : m + 2 * rows]
    outer = [lambda sl, c=c: vm[c, sl] for c in range(3)]

    def third(f, sl):
        n = third_at.window(0, f).start + sl.start - B
        return unless(here.no_left, xl[n : n + 8]) + d3[f, sl]

    def plane(cur, i, before, after, store, sl=ext):
        fluid.advance(cur, before, after, speeds(v0, i), at(w0, i), at(s0, i), sl, store)

    def farther(f, sl):
        n = sl.start - own.start
        w = unless(here.no_left, DAMPING / fluid.diagonal(f, usmm[n : n + 8]))
        return w * (fluid.d[f] + u0mm[n : n + 8]) * d1[f, sl]

    def first(i):
        return at(p1, i - 1) if i < 3 else at(q1, i - 3)

    for i in range(3, depth - 1):
        plane(at(p0, i), i, at(p0, i - 1), at(p0, i + 1), into(q1, i - 3))
    for i in range(2, depth - 2):
        plane(first(i), i, first(i - 1), first(i + 1), into(p2, i - 2))
    for i in range(3, depth - 3):
        plane(at(p2, i - 2), i, at(p2, i - 3), at(p2, i - 1), into(p3, i - 3))
    fluid.advance(flat(d2), farther, flat(n2), outer, flat(wm), None, own, into_flat(d3))
    plane(flat(c2), 1, flat(n2), at(p2, 0), into(m3, 0))
    plane(at(p2, 0), 2, flat(c2), at(p2, 1), into(m3, 1))
    squares = [None] * fields
    third_of = [flat(c3), at(m3, 0), at(m3, 1), at(p3, 0), at(p3, 1)]
    for i in range(4):

        def final(f, sl, res, value, i=i):
            left[f, i, sl.start - own.start : sl.stop - own.start] = value
            square = res * res
            squares[f] = square if squares[f] is None else squares[f] + square

        plane(third_of[i], i, third_of[i - 1] if i > 0 else third, third_of[i + 1], final, own)
    sq[...] = jnp.zeros_like(sq)
    for f in range(fields):
        sq[f : f + 1] = jnp.sum(squares[f], axis=0, keepdims=True)
    flux = coef[0] * left[fields - 1, 0]
    parts[...] = jnp.dot(hot[...], flux, precision=HIGHEST, preferred_element_type=F32)
    for j in range(blocks):
        parts[j * CHUNK + 2 * CAP : (j + 1) * CHUNK] = meta[j]


def rest_kernel(blocks, spans, sent, spread, jacobian, *refs):
    p0, s0, v0, w0, p1, p2, p3, left, sqb, xn, _, gas, sq, n1, n2, n3 = refs
    fields, depth = gas.shape[0], gas.shape[1]
    rows = gas.shape[2]
    here = Place(rows, blocks, spans)
    ext, own, tall = here.ext, here.own, here.tall
    fluid = Fluid(spread, jacobian, fields)
    def arrived(level):
        def read(f, sl):
            n = sent.window(level, f).start + sl.start - B
            return unless(here.no_right, xn[n : n + 8])

        return read

    known = [{i: (p0, i) for i in range(depth)}, {}, {}, {}]
    for level, (buf, low) in enumerate(((p1, 3), (p2, 2), (p3, 3))):
        for i in range(low, depth - 1 - level):
            known[level + 1][i] = (buf, i - low)

    def read(level, i):
        ref, j = known[level][i]
        return at(ref, j)

    def plane(level, i, store, sl=ext):
        fluid.advance(
            read(level, i),
            read(level, i - 1),
            read(level, i + 1) if i < depth - 1 else arrived(level),
            speeds(v0, i),
            at(w0, i),
            at(s0, i),
            sl,
            store,
        )

    todo = ((depth - 1,), (depth - 2, depth - 1), (depth - 3, depth - 2, depth - 1))
    for level, new in enumerate((n1, n2, n3)):
        for j, i in enumerate(todo[level]):
            plane(level, i, into(new, j))
            known[level + 1][i] = (new, j)
    total = [None] * fields
    for f in range(fields):
        for i in range(4):
            gas[f, i] = left[f, i]
    for i in range(4, depth):

        def final(f, sl, res, value, i=i):
            gas[f, i, sl.start - own.start : sl.stop - own.start] = value
            square = res * res
            total[f] = square if total[f] is None else total[f] + square

        plane(3, i, final, own)
    sq[...] = sqb[...]
    for f in range(fields):
        sq[f : f + 1] = sq[f : f + 1] + jnp.sum(total[f], axis=0, keepdims=True)


def solid_kernel(
    blocks, spans, sent, te, he, so, ti, tbi, sqi, dg, ws, sl_, tl0, tl1, tl2, tl3, dl, wl, xb, _, *refs
):
    tb, rb, sq, rh, rd, rw = refs[:6]
    hr, dr, wr, ta, tc, qa = refs[6:]
    thick, rows, z = tb.shape
    here = Place(rows, blocks, spans)
    ext, own, tall = here.ext, here.own, here.tall
    hl = sl_.at[0]

    def arrived(n):
        return unless(here.no_right, xb[sent.window(n, 0)])

    for j in range(2):
        hr[j, ext] = arrived(j)

    def h_of(i, sl):
        if i < 0:
            return hl[i + 4, sl]
        return he[i, sl] if i < thick else hr[i - thick, sl]

    for j in range(2):
        i = thick - 1 + j
        dr[j, ext] = solid_diagonal(h_of, i, ext)
        wr[j, ext] = solid_weight(h_of(i, ext), dr[j, ext])

    def d_of(left, inside, right, i, sl):
        if i <= 0:
            return left[i + 3, sl]
        return inside[i, sl] if i < thick - 1 else right[i - thick + 1, sl]

    def residual(old, j, i, sl):
        res = so[i, sl] - d_of(dl, dg, dr, i, sl) * old[j, sl]
        return res + h_of(i, sl) * around(old, j, sl) + around(qa, j, sl)

    sums = None
    for j in range(6):
        qa[j, ext] = h_of(j - 1, ext) * tl3[j, ext]
    for i in range(4):
        res = residual(tl3, i + 1, i, own)
        tb[i] = tl3[i + 1, own] + d_of(wl, ws, wr, i, own) * res
        if i < 3:
            rb[i] = res
        else:
            sums = res * res
    old, new = ta, tc
    old[0], old[1] = te[thick - 2], te[thick - 1]
    old[2, ext] = arrived(2)
    for level in range(SWEEPS):
        last = level == SWEEPS - 1
        sl = own if last else ext
        low = thick - 2 - level
        for j in range(level + 3):
            qa[j, ext] = h_of(low + j, ext) * old[j, ext]
        for j in range(1, level + 2):
            i = low + j
            res = residual(old, j, i, sl)
            value = old[j, sl] + d_of(wl, ws, wr, i, sl) * res
            if last:
                tb[i] = value
                rb[i - (thick - 7)] = res
            else:
                new[j + 1, ext] = value
        if not last:
            for j in range(2):
                new[j] = ti[level, j + 2]
            new[level + 3, ext] = arrived(3 + level)
            old, new = new, old
    for i in range(SWEEPS, thick - SWEEPS):
        tb[i] = tbi[i - SWEEPS]
    sq[...] = sqi[...]
    n = sq.shape[0] - 3
    sq[n : n + 1] = sq[n : n + 1] + jnp.sum(sums, axis=0, keepdims=True)
    for region in range(2):
        for j in range(5):
            i = j - 2 if region == 0 else thick - 4 + j
            rh[region, j, ext] = h_of(i, ext)
            rd[region, j, ext] = d_of(dl, dg, dr, i, ext)
            rw[region, j, ext] = d_of(wl, ws, wr, i, ext)


def surface_kernel(blocks, arrived, surface, yf, yb):
    rows = surface.shape[0] // 2
    meta = arrived[0, 2 * CAP :]
    for j in range(1, blocks):
        meta = meta + arrived[j, 2 * CAP :]
    row = lax.broadcasted_iota(jnp.int32, (2 * rows, 4 * CHUNK), 0)
    slot = lax.broadcasted_iota(jnp.int32, (2 * rows, 4 * CHUNK), 1) % CHUNK
    row = row + 1 - jnp.where(slot < CAP, 0, rows)
    row = jnp.where((row >= 1) & (row <= rows), row, -1).astype(F32)
    whole = None
    for j in range(0, blocks, 4):
        sent = jnp.concatenate([arrived[j + m] for m in range(4)], axis=0)
        hot = jnp.where(row == meta[j // 4 : j // 4 + 1], 1.0, 0.0)
        got = jnp.dot(hot, sent, precision=HIGHEST, preferred_element_type=F32)
        whole = got if whole is None else whole + got
    surface[...] = whole
    yf[:W] = whole[rows - W : rows]
    yf[W:] = whole[2 * rows - W :]
    yb[:W] = whole[:W]
    yb[W:] = whole[rows : rows + W]


def response_kernel(
    blocks, spans, fields, surface, yl, yr, rh, rd, rw, tb, rb, sqf, sqs, tn, out, da, db, hd, so
):
    thick, rows, z = tb.shape
    here = Place(rows, blocks, spans)
    ext, own = here.ext, here.own
    for buf in (da, db, hd):
        buf[...] = jnp.zeros_like(buf)
    sq = sqf[...] + sqs[...]
    gained = jnp.zeros((rows, z), F32)
    for region in range(2):

        def store(sl, x, region=region):
            so[region, sl] = x

        edge = slice(region * W, (region + 1) * W)
        here.fill(store, surface[region * rows : (region + 1) * rows], yl[edge], yr[edge])

    needed = (((2,), (1, 2, 3), (1, 2, 3, 4), (3, 4, 5)), ((4,), (3, 4, 5), (2, 3, 4, 5), (1, 2, 3, 4)))
    for i in range(3, thick - 4):
        tn[i] = tb[i]
    for region in range(2):
        old, new = da, db
        source = 2 if region == 0 else 4
        for sweep in range(SWEEPS):
            final = sweep == SWEEPS - 1
            for j in needed[region][sweep]:
                res = so[region, ext] if j == source else None
                h, w = rh[region, j - 1, ext], rw[region, j - 1, ext]
                if sweep > 0:
                    q = old[region, j, ext]
                    flow = h * around(old.at[region], j, ext) + around(hd.at[region], j, ext) - rd[region, j - 1, ext] * q
                    res = flow if res is None else res + flow
                    change = q + w * res
                else:
                    change = w * res
                if final:
                    i = j - 3 if region == 0 else thick - 5 + j
                    kept = i if region == 0 else 2 + j
                    mine = slice(W, W + rows)
                    tn[i] = tb[i] + change[mine]
                    full = rb[kept] + res[mine]
                    gained = gained + full * full
                else:
                    new[region, j, ext] = change
            if not final:
                for j in needed[region][sweep]:
                    hd[region, j, ext] = rh[region, j - 1, ext] * new[region, j, ext]
                old, new = new, old
    extra = jnp.sum(gained, axis=0, keepdims=True)
    row = lax.broadcasted_iota(jnp.int32, sq.shape, 0)
    sq = sq + jnp.where(row == fields, extra, 0.0)
    for j in range(blocks):
        out[j, :rows] = tn[thick - 1]
        out[j, rows:] = sq


def squares_kernel(blocks, rows, arrived, sq):
    whole = arrived[0, rows:]
    for j in range(1, blocks):
        whole = whole + arrived[j, rows:]
    sq[...] = whole


def return_kernel(blocks, arrived, idx, coef, gas, t, gas_out, t_out, plane, sems):
    fields, rows = gas.shape[0], gas.shape[2]
    last = fields - 1
    copies = [
        pltpu.make_async_copy(gas.at[pl.ds(0, last)], gas_out.at[pl.ds(0, last)], sems.at[0]),
        pltpu.make_async_copy(
            gas.at[last, pl.ds(1, gas.shape[1] - 1)],
            gas_out.at[last, pl.ds(1, gas.shape[1] - 1)],
            sems.at[1],
        ),
        pltpu.make_async_copy(t, t_out, sems.at[2]),
    ]
    for copy in copies:
        copy.start()
    row = lax.broadcasted_iota(jnp.int32, (rows, rows), 0).astype(F32)
    taken = None
    for j in range(blocks):
        hot = jnp.where(idx[...] - float(j * rows) == row, 1.0, 0.0)
        got = lax.dot_general(
            hot,
            arrived[j, :rows],
            (((0,), (0,)), ((), ())),
            precision=HIGHEST,
            preferred_element_type=F32,
        )
        taken = got if taken is None else taken + got
    plane[...] = gas[last, 0] + coef[0] * taken
    copy = pltpu.make_async_copy(plane, gas_out.at[last, 0], sems.at[3])
    copy.start()
    for other in copies:
        other.wait()
    copy.wait()


def shards(
    blocks,
    spans,
    fluid_adjoint_in,
    fluid_source,
    velocity,
    diffusion,
    jacobian,
    wall_coefficient,
    metal_costate_prior,
    solid_source,
    conductivity,
    tile_owner,
    tile_target,
):
    p, src, vel = fluid_adjoint_in, fluid_source, velocity
    t, heat, k = metal_costate_prior, solid_source, conductivity
    fields, depth, rows, z = p.shape
    thick = t.shape[0]
    tall = rows + 2 * W
    buf = tall + 2 * B
    forward = {
        "blk": [(i, (i + 1) % blocks) for i in range(blocks)],
        "span": [(i, (i + 1) % spans) for i in range(spans)],
    }
    backward = {axis: [(j, i) for i, j in pairs] for axis, pairs in forward.items()}

    def ahead(x, axis):
        return lax.ppermute(x, axis, forward[axis])

    def behind(x, axis):
        return lax.ppermute(x, axis, backward[axis])

    edges = Edges(fields, depth, thick)
    inputs = [p, src, vel, t, heat, k]
    p, src, vel, t, heat, k, yf, yb, xf, zf, zb = call(
        functools.partial(early_kernel, edges),
        held(*[x.shape for x in inputs])
        + [(edges.size, z)] * 2
        + [((fields + 11) * rows, z)]
        + [(edges.late_size, z)] * 2,
        [pltpu.SemaphoreType.DMA((6,))],
        [HBM] * 6,
        *[pltpu.with_memory_space_constraint(x, pltpu.HBM) for x in inputs],
    )
    yl, yr = ahead(yf, "span"), behind(yb, "span")
    xe = ahead(xf, "blk")
    sent_ahead = Arrivals((fields + 8) * 2 * W, rows, fields, (2, 1))
    solid_ahead = Arrivals(8, rows, 1, (1, 0))
    third_ahead = Arrivals((solid_ahead.size() + 7) // 8 * 8, rows, fields, (0,))
    four = (4, buf, z)
    out, later = call(
        functools.partial(ahead_kernel, blocks, spans, edges, solid_ahead, third_ahead),
        [((sent_ahead.size() + W + 7) // 8 * 8, z), (third_ahead.size(), z)],
        [(fields, 4, buf, z), (fields, 3, buf, z), (fields, 2, buf, z), (fields, 3, buf, z)]
        + [(3, 3, buf, z), (fields, 3, buf, z)]
        + [four] * 6,
        [SMEM] * 2 + [VMEM] * 8,
        diffusion,
        jacobian,
        p,
        src,
        vel,
        t,
        heat,
        k,
        yl,
        yr,
        cost=COSTS[1],
    )
    xn, xl = ahead(out, "blk"), ahead(later, "blk")
    full = (fields, depth, buf, z)
    part = [(fields, depth - 2 * (level + 1), buf, z) for level in range(3)]
    solid = (thick, buf, z)
    zl, zr = ahead(zf, "span"), behind(zb, "span")
    p0, s0, v0, w0, p1, place, meta, idx = call(
        functools.partial(inner_kernel, blocks, spans, edges),
        held(full, full, (3, depth, buf, z), full, (fields, 2, buf, z))
        + held((blocks * CHUNK, rows), (blocks, 8, z), (1, rows)),
        [],
        [SMEM] * 2 + [VMEM] * 9,
        diffusion,
        jacobian,
        tile_owner.reshape(1, rows),
        tile_target,
        p,
        src,
        vel,
        yl,
        yr,
        zl,
        zr,
        cost=COSTS[2],
    )
    te, he, so, ti, tb, sqi, dg, ws = call(
        functools.partial(inner_solid_kernel, blocks, spans, edges, fields),
        held(solid, solid, solid, (3, 4, buf, z), (thick - 2 * SWEEPS, rows, z), (8, z), solid, solid),
        [solid] * 4,
        [VMEM] * 6,
        t,
        heat,
        k,
        zl,
        zr,
        idx,
        cost=COSTS[2],
    )
    solid_back = Arrivals(8, rows, 1, (3, 1, 3, 2, 1, 0))
    sent_back = Arrivals(solid_back.size(), rows, fields, (3, 2, 1, 0))
    one, six = (fields, buf, z), (6, buf, z)
    back, n2, c2, c3, d1, d2, vm, wm, sl_, *lefts = call(
        functools.partial(cone_kernel, blocks, spans, sent_ahead, solid_ahead, solid_back),
        [(sent_back.size(), z)]
        + held(one, one, one, one, one, (3, buf, z), one, (2, 4, buf, z))
        + held(six, six, six, six, (4, buf, z), (4, buf, z)),
        [one] * 2 + [six],
        [SMEM] * 2 + [VMEM] * 14,
        diffusion,
        jacobian,
        p0,
        s0,
        v0,
        w0,
        p1,
        te,
        he,
        so,
        ti,
        dg,
        ws,
        xe,
        xn,
        xl,
        cost=COSTS[3],
    )
    xr = lax.ppermute(back, "blk", backward["blk"][: blocks - 1])
    parts, half, sq, q1, p2, p3 = call(
        functools.partial(flux_kernel, blocks, spans, third_ahead),
        [(blocks * CHUNK, z)]
        + held((fields, 4, rows, z), (8, z), (fields, depth - 4, buf, z), *part[1:]),
        [(fields, 2, buf, z), one],
        [SMEM] * 2 + [VMEM] * 17,
        diffusion,
        jacobian,
        p0,
        s0,
        v0,
        w0,
        p1,
        n2,
        c2,
        c3,
        d1,
        d2,
        vm,
        wm,
        xe,
        xl,
        wall_coefficient,
        place,
        meta,
        cost=COSTS[2],
    )
    arrived = lax.all_to_all(parts.reshape(blocks, CHUNK, z), "blk", 0, 0)
    surface, yf, yb = call(
        functools.partial(surface_kernel, blocks),
        [(2 * rows, z), (2 * W, z), (2 * W, z)],
        [],
        [VMEM],
        arrived,
    )
    yl, yr = ahead(yf, "span"), behind(yb, "span")
    gas, sqf = call(
        functools.partial(rest_kernel, blocks, spans, sent_back),
        held(p.shape, (8, z)),
        [(fields, 1, buf, z), (fields, 2, buf, z), (fields, 3, buf, z)],
        [SMEM] * 2 + [VMEM] * 11,
        diffusion,
        jacobian,
        p0,
        s0,
        v0,
        w0,
        q1,
        p2,
        p3,
        half,
        sq,
        xr,
        yf,
        cost=COSTS[4],
    )
    two, edge = (2, buf, z), (2, 5, buf, z)
    tb, rb, sqs, rh, rd, rw = call(
        functools.partial(solid_kernel, blocks, spans, solid_back),
        held(t.shape, (7, rows, z), (8, z), edge, edge, edge),
        [two] * 3 + [six] * 3,
        [VMEM] * 17,
        te,
        he,
        so,
        ti,
        tb,
        sqi,
        dg,
        ws,
        sl_,
        *lefts,
        xr,
        yf,
        cost=COSTS[5],
    )
    region = (2, 7, buf, z)
    t, out = call(
        functools.partial(response_kernel, blocks, spans, fields),
        held(t.shape, (blocks, rows + 8, z)),
        [region] * 3 + [(2, buf, z)],
        [VMEM] * 10,
        surface,
        yl,
        yr,
        rh,
        rd,
        rw,
        tb,
        rb,
        sqf,
        sqs,
    )
    arrived = lax.all_to_all(out, "blk", 0, 0)
    (sq,) = call(
        functools.partial(squares_kernel, blocks, rows), held((8, z)), [], [VMEM], arrived
    )
    others = [
        lax.ppermute(sq, "span", [(i, i ^ step) for i in range(spans)]) for step in range(1, spans)
    ]
    gas, t = call(
        functools.partial(return_kernel, blocks),
        [gas.shape, t.shape],
        [(rows, z), pltpu.SemaphoreType.DMA((4,))],
        [VMEM] * 5,
        arrived,
        idx,
        wall_coefficient,
        gas,
        t,
        out_specs=[pl.BlockSpec(memory_space=pl.ANY)] * 2,
        cost=2.0,
    )
    sq = functools.reduce(jnp.add, others, sq)
    everyone = blocks * spans
    counts = [float(depth * rows * z * everyone)] * fields + [float(thick * rows * z * everyone)]
    totals = jnp.sum(sq[: fields + 1], axis=1)
    norms = jnp.sqrt(totals / jnp.array(counts, F32))
    return gas, t, norms


def solution(mesh):
    placed = (
        P(None, "blk", "span", None),
        P(None, "blk", "span", None),
        P(None, "blk", "span", None),
        P(),
        P(),
        P("blk", "span", None),
        P("blk", "span", None),
        P("blk", "span", None),
        P("blk", "span", None),
        P("span", "blk", None),
        P("span", "blk"),
    )
    return jax.shard_map(
        functools.partial(shards, mesh.shape["blk"], mesh.shape["span"]),
        mesh=mesh,
        in_specs=placed,
        out_specs=(P(None, "blk", "span", None), P("blk", "span", None), P()),
        check_vma=False,
    )
```

```python
import functools

import jax
import jax.numpy as jnp
from jax import lax
from jax.experimental import pallas as pl
from jax.experimental.pallas import tpu as pltpu
from jax.sharding import PartitionSpec as P

SWEEPS = 4
DAMPING = 0.8
HIGHEST = lax.Precision.HIGHEST
F32 = jnp.float32
VMEM = pl.BlockSpec(memory_space=pltpu.VMEM)
SMEM = pl.BlockSpec(memory_space=pltpu.SMEM)
HBM = pl.BlockSpec(memory_space=pltpu.HBM)
COSTS = (1.0, 30.0, 0.01, 2.0, 3.0, 3.0)
LIMIT = 12 * 1024 * 1024
W = 4
CAP = 12
CHUNK = 32
B = 8


def held(*shapes):
    return [pltpu.VMEM(s, F32) for s in shapes]


def call(kernel, outs, scratch, specs, *args, out_specs=None, cost=0.01):
    return pl.pallas_call(
        kernel,
        out_shape=[jax.ShapeDtypeStruct(s, F32) if isinstance(s, tuple) else s for s in outs],
        in_specs=specs,
        out_specs=out_specs or [VMEM] * len(outs),
        scratch_shapes=[pltpu.VMEM(s, F32) if isinstance(s, tuple) else s for s in scratch],
        compiler_params=pltpu.CompilerParams(vmem_limit_bytes=LIMIT),
        cost_estimate=pl.CostEstimate(
            flops=int(cost * 1e6), bytes_accessed=int(cost * 3e6), transcendentals=0
        ),
    )(*args)


def beside(x):
    lane = lax.broadcasted_iota(jnp.int32, x.shape, 1)
    last = x.shape[1] - 1
    before = jnp.where(lane == 0, 0.0, pltpu.roll(x, 1, 1))
    after = jnp.where(lane == last, 0.0, pltpu.roll(x, last, 1))
    return before, after


def unless(flag, x):
    return jnp.where(flag, 0.0, x)


class Place:
    def __init__(self, rows, blocks, spans):
        b, s = lax.axis_index("blk"), lax.axis_index("span")
        self.rows, self.tall = rows, rows + 2 * W
        self.no_left, self.no_right = b == 0, b == blocks - 1
        self.no_low, self.no_high = s == 0, s == spans - 1
        self.ext = slice(B, B + self.tall)
        self.own = slice(B + W, B + W + rows)
        self.low = slice(B, B + W)
        self.high = slice(B + W + rows, B + self.tall)

    def reach(self, by):
        return slice(B + W - by, B + W + self.rows + by)

    def fill(self, store, own, low, high, hide=None):
        no_low, no_high = self.no_low, self.no_high
        if hide is not None:
            own, no_low, no_high = unless(hide, own), no_low | hide, no_high | hide
        store(self.own, own)
        store(slice(self.low.stop - low.shape[0], self.low.stop), unless(no_low, low))
        store(slice(self.high.start, self.high.start + high.shape[0]), unless(no_high, high))

    def inside(self, z):
        row = lax.broadcasted_iota(jnp.int32, (self.tall, z), 0)
        out = ((row < W) & self.no_low) | ((row >= W + self.rows) & self.no_high)
        return jnp.logical_not(out)


def beyond(sl, by):
    return slice(sl.start + by, sl.stop + by)


def rows_at(ref, n, count):
    return ref[n : n + count]


class Arrivals:
    def __init__(self, first, rows, fields, reaches):
        self.first, self.rows, self.fields, self.reaches = first, rows, fields, reaches

    def window(self, level, f, ext=True):
        n = self.first
        for reach in self.reaches[:level]:
            n = n + self.fields * (self.rows + 2 * reach)
        reach = self.reaches[level]
        n = n + f * (self.rows + 2 * reach)
        if ext:
            return slice(n + reach - W, n + reach + W + self.rows)
        return slice(n + reach, n + reach + self.rows)

    def size(self):
        return self.first + sum(self.fields * (self.rows + 2 * reach) for reach in self.reaches)


class Edges:
    def __init__(self, fields, depth, thick):
        n, later = 0, 0
        self.fluid, self.late, self.outer, self.solid = {}, {}, {}, {}
        for name, count, reach, near in (
            ("p", fields, W, 4),
            ("src", fields, W - 1, 3),
            ("vel", 3, W - 1, 3),
        ):
            for f in range(count):
                for i in range(depth):
                    if i < depth - near:
                        self.late[name, f, i] = slice(later, later + reach)
                        later = later + reach
                    else:
                        self.fluid[name, f, i] = slice(n, n + reach)
                        n = n + reach
        for name, near, reach in (("t", 4, W), ("k", 4, W), ("heat", 3, W - 1)):
            for i in range(thick - near, thick):
                self.outer[name, i] = slice(n, n + reach)
                n = n + reach
        self.size = (n + 7) // 8 * 8
        for name, reach in (("t", W), ("k", W), ("heat", W - 1)):
            for i in range(thick):
                self.solid[name, i] = slice(later, later + reach)
                later = later + reach
        self.late_size = (later + 7) // 8 * 8


class Fluid:
    def __init__(self, spread, jacobian, fields):
        self.n = fields
        self.d = [spread[f] for f in range(fields)]
        self.jac = [[jacobian[f, g] for g in range(fields)] for f in range(fields)]

    def diagonal(self, f, us):
        return us + (6.0 * self.d[f] + self.jac[f][f])

    def advance(self, cur, left, right, vel, w, src, rows, store):
        for n in range(rows.start, rows.stop, 8):
            sl = slice(n, n + 8)
            u0, u1, u2 = (u(sl) for u in vel)
            us = u0 + u1 + u2
            centre = [cur(f, sl) for f in range(self.n)]
            for f in range(self.n):
                c = centre[f]
                zm, zp = beside(c)
                yp = cur(f, beyond(sl, 1))
                near = (cur(f, beyond(sl, -1)) + yp) + (zm + zp)
                if left is not None:
                    near = near + left(f, sl)
                res = u1 * yp + u2 * zp - self.diagonal(f, us) * c
                if right is not None:
                    xp = right(f, sl)
                    near = near + xp
                    res = res + u0 * xp
                res = res + self.d[f] * near
                for g in range(self.n):
                    if g != f:
                        res = res - self.jac[f][g] * centre[g]
                if src is not None:
                    res = res + src(f, sl)
                store(f, sl, res, c + w(f, sl) * res)


def at(ref, i):
    return lambda f, sl: ref[f, i, sl]


def flat(ref):
    return lambda f, sl: ref[f, sl]


def speeds(ref, i):
    return [lambda sl, c=c: ref[c, i, sl] for c in range(3)]


def into(ref, i):
    def store(f, sl, _, value):
        ref[f, i, sl] = value

    return store


def into_flat(ref):
    def store(f, sl, _, value):
        ref[f, sl] = value

    return store


def early_kernel(edges, *refs):
    bufs = refs[6:12]
    yf, yb, xf, zf, zb, sems = refs[12:]
    copies = [
        pltpu.make_async_copy(ref, buf, sems.at[j])
        for j, (ref, buf) in enumerate(zip(refs[:6], bufs, strict=True))
    ]
    for copy in copies:
        copy.start()
    p, src, vel, t, heat, k = bufs
    fields, depth, rows = p.shape[0], p.shape[1], p.shape[2]
    thick = t.shape[0]
    named = {"p": p, "src": src, "vel": vel, "t": t, "heat": heat, "k": k}

    def pack(up, down, places, names):
        for (name, *at_plane), sl in places.items():
            if name in names:
                ref, reach = named[name], sl.stop - sl.start
                up[sl] = ref[*at_plane, rows - reach :]
                down[sl] = ref[*at_plane, :reach]

    for j, name in enumerate(named):
        copies[j].wait()
        if j < 3:
            pack(yf, yb, edges.fluid, (name,))
            pack(zf, zb, edges.late, (name,))
    planes = [p[f, depth - 1] for f in range(fields)]
    planes += [vel[f, depth - 1] for f in range(3)]
    planes += [vel[0, depth - 2], vel[0, depth - 2] + vel[1, depth - 2] + vel[2, depth - 2]]
    planes += [t[thick - 1], t[thick - 2], k[thick - 1], k[thick - 2], k[thick - 3]]
    planes += [heat[thick - 1]]
    for j, plane in enumerate(planes):
        xf[j * rows : (j + 1) * rows] = plane
    for up, down, places in ((yf, yb, edges.outer), (zf, zb, edges.solid)):
        pack(up, down, places, named)


def ahead_kernel(blocks, spans, edges, solid, third, spread, jacobian, *refs):
    p, src, vel, t, heat, k, yl, yr, out, later = refs[:10]
    a0, a1, a2, sa, va, wa, ta, ha, so, qa, tb, qb = refs[10:]
    fields, depth, rows, z = p.shape
    at_place = Place(rows, blocks, spans)
    ext, own = at_place.ext, at_place.own
    fluid = Fluid(spread, jacobian, fields)
    inside = at_place.inside(z)

    def fill(buf, f, j, ref, name, i):
        def store(sl, x):
            buf[f, j, sl] = x

        sl = edges.fluid[name, f, i]
        at_place.fill(store, ref[f, i], yl[sl], yr[sl])

    for f in range(fields):
        for j in range(4):
            fill(a0, f, j, p, "p", depth - 4 + j)
        for j in range(3):
            fill(sa, f, j, src, "src", depth - 3 + j)
    for f in range(3):
        for j in range(3):
            fill(va, f, j, vel, "vel", depth - 3 + j)
    for j in range(3):
        us = va[0, j, ext] + va[1, j, ext] + va[2, j, ext]
        for f in range(fields):
            wa[f, j, ext] = jnp.where(inside, DAMPING / fluid.diagonal(f, us), 0.0)

    def step(old, i, store, j):
        fluid.advance(
            at(old, i),
            at(old, i - 1),
            None if j == 2 else at(old, i + 1),
            speeds(va, j),
            at(wa, j),
            at(sa, j),
            ext,
            store,
        )

    for j in range(3):
        step(a0, j + 1, into(a1, j), j)
    for j in range(1, 3):
        step(a1, j, into(a2, j - 1), j)
    corners = [edges.fluid["p", f, depth - 1] for f in range(fields)]
    corners += [edges.fluid["vel", c, depth - 1] for c in range(3)]
    thick = t.shape[0]
    corners += [edges.outer["t", thick - 1], edges.outer["t", thick - 2]]
    corners += [edges.outer["k", thick - 1], edges.outer["k", thick - 2]]
    corners += [edges.outer["heat", thick - 1]]
    n = 0
    for sl in corners:
        reach = sl.stop - sl.start
        out[n + W - reach : n + W] = yl[sl]
        out[n + W : n + W + reach] = yr[sl]
        n = n + 2 * W
    for reach, buf, j in ((2, a1, 2), (1, a2, 1)):
        size = rows + 2 * reach
        for f in range(fields):
            out[n : n + size] = buf[f, j, at_place.reach(reach)]
            n = n + size

    def last(f, sl, _, value):
        m = third.window(0, f).start + sl.start - B
        later[m : m + 8] = value

    fluid.advance(
        at(a2, 1), at(a2, 0), None, speeds(va, 2), at(wa, 2), at(sa, 2), own, last
    )
    for name, buf, ref, near, scale in (
        ("t", ta, t, 4, 1.0),
        ("k", ha, k, 4, 0.5),
        ("heat", so, heat, 3, 1.0),
    ):
        for j in range(4 - near, 4):
            i = thick - 4 + j

            def store(sl, x, buf=buf, j=j, scale=scale):
                buf[j, sl] = scale * x

            sl = edges.outer[name, i]
            at_place.fill(store, ref[i], yl[sl], yr[sl])
    for j in range(4):
        qa[j, ext] = ha[j, ext] * ta[j, ext]

    def h_of(j, sl):
        return ha[j, sl]

    kept = {}
    for j in (1, 2):
        h = ha[j, ext]
        diagonal = solid_diagonal(h_of, j, ext)
        w = solid_weight(h, diagonal)
        res = so[j, ext] - diagonal * ta[j, ext] + h * around(ta, j, ext) + around(qa, j, ext)
        tb[j, ext] = ta[j, ext] + w * res
        qb[j, ext] = h * tb[j, ext]
        kept[j] = (h, diagonal, w)
    tb[3] = jnp.zeros_like(tb[3])
    qb[3] = jnp.zeros_like(qb[3])
    h, diagonal, w = kept[2]
    res = so[2, ext] - diagonal * tb[2, ext] + h * around(tb, 2, ext) + around(qb, 2, ext)
    value = tb[2, ext] + w * res
    m = solid.window(0, 0).start + W - 1
    later[m : m + rows + 2] = tb[2, at_place.reach(1)]
    m = solid.window(1, 0).start + W
    later[m : m + rows] = value[W : W + rows]


def around(buf, j, sl):
    zm, zp = beside(buf[j, sl])
    return (
        (buf[j - 1, sl] + buf[j + 1, sl])
        + (buf[j, beyond(sl, -1)] + buf[j, beyond(sl, 1)])
        + (zm + zp)
    )


def solid_diagonal(h_of, i, sl):
    zm, zp = beside(h_of(i, sl))
    near = (h_of(i - 1, sl) + h_of(i + 1, sl)) + (zm + zp)
    near = near + (h_of(i, beyond(sl, -1)) + h_of(i, beyond(sl, 1)))
    return 6.0 * h_of(i, sl) + near


def solid_weight(h, diagonal):
    return jnp.where(h > 0.0, DAMPING / jnp.where(h > 0.0, diagonal, 1.0), 0.0)


def plan(blocks, owner, target, place, meta, idx):
    rows = target.shape[1]
    me = lax.axis_index("blk")
    row = lax.broadcasted_iota(jnp.int32, (rows, rows), 0)
    lane = lax.broadcasted_iota(jnp.int32, (rows, rows), 1)
    owner = owner[...].astype(F32)
    column = jnp.where(row == lane, jnp.broadcast_to(owner, (rows, rows)), 0.0)
    column = jnp.sum(column, axis=1, keepdims=True)
    idx[...] = owner * rows + target[...].astype(F32)
    before = jnp.where((column == owner) & (row < lane), 1.0, 0.0)
    rank = jnp.sum(before, axis=0, keepdims=True)
    n = lax.broadcasted_iota(jnp.int32, (blocks * CHUNK, rows), 0)
    slot = n % CHUNK
    second = slot >= CAP
    named = n // CHUNK - jnp.where(second, 0, 1)
    at_rank = (slot - jnp.where(second, CAP, 0)).astype(F32)
    hot = jnp.where((owner == named.astype(F32)) & (rank == at_rank), 1.0, 0.0)
    hot = jnp.where(slot < 2 * CAP, hot, 0.0)
    place[...] = hot
    targets = jnp.broadcast_to((target[...] + 1).astype(F32), (8, rows))
    lanes = lax.dot_general(
        targets, hot, (((1,), (1,)), ((), ())), precision=HIGHEST, preferred_element_type=F32
    )
    row = lax.broadcasted_iota(jnp.int32, (8, 4 * CHUNK), 0)
    lane = lax.broadcasted_iota(jnp.int32, (8, 4 * CHUNK), 1)
    for j in range(blocks):
        group = lanes[:, j // 4 * 4 * CHUNK : (j // 4 + 1) * 4 * CHUNK]
        group = jnp.where(lane // CHUNK == j % 4, group, 0.0)
        group = pltpu.roll(group, lax.rem(me - j + 4 * blocks, 4) * CHUNK, 1)
        meta[j] = jnp.where(row == me // 4, group, 0.0)


def inner_kernel(
    blocks, spans, edges, spread, jacobian, owner, target, p, src, vel, yl, yr, zl, zr, *outs
):
    p0, s0, v0, w0, p1, place, meta, idx = outs
    plan(blocks, owner, target, place, meta, idx)
    fields, depth, rows, z = p.shape
    here = Place(rows, blocks, spans)
    ext = here.ext
    fluid = Fluid(spread, jacobian, fields)
    inside = here.inside(z)
    for name, buf, ref in (("p", p0, p), ("src", s0, src), ("vel", v0, vel)):
        for f in range(ref.shape[0]):
            for i in range(depth):

                def store(sl, x, buf=buf, f=f, i=i):
                    buf[f, i, sl] = x

                if (name, f, i) in edges.late:
                    sl = edges.late[name, f, i]
                    here.fill(store, ref[f, i], zl[sl], zr[sl])
                else:
                    sl = edges.fluid[name, f, i]
                    here.fill(store, ref[f, i], yl[sl], yr[sl])
    for i in range(depth):
        us = v0[0, i, ext] + v0[1, i, ext] + v0[2, i, ext]
        for f in range(fields):
            w0[f, i, ext] = jnp.where(inside, DAMPING / fluid.diagonal(f, us), 0.0)
    for i in (1, 2):
        fluid.advance(
            at(p0, i),
            at(p0, i - 1),
            at(p0, i + 1),
            speeds(v0, i),
            at(w0, i),
            at(s0, i),
            ext,
            into(p1, i - 1),
        )


def inner_solid_kernel(blocks, spans, edges, fields, t, heat, k, yl, yr, _, *refs):
    te, he, so, ti, tb, sqi, dg, ws, ta, tc, qa, qc = refs
    thick, rows, z = t.shape
    here = Place(rows, blocks, spans)
    ext = here.ext
    for name, buf, ref, scale in (("t", te, t, 1.0), ("k", he, k, 0.5), ("heat", so, heat, 1.0)):
        for i in range(thick):

            def store(sl, x, buf=buf, i=i, scale=scale):
                buf[i, sl] = scale * x

            sl = edges.solid[name, i]
            here.fill(store, ref[i], yl[sl], yr[sl])
    for i in range(1, thick - 1):
        h = he[i, ext]
        diagonal = 6.0 * h + around(he, i, ext)
        dg[i, ext] = diagonal
        ws[i, ext] = solid_weight(h, diagonal)
    for i in range(thick):
        qa[i, ext] = he[i, ext] * te[i, ext]
    old, oldq, new, newq = te, qa, ta, qc
    total = None
    for level in range(SWEEPS):
        last = level == SWEEPS - 1
        sl = here.own if last else ext
        for i in range(level + 1, thick - 1 - level):
            h, q = he[i, sl], old[i, sl]
            res = so[i, sl] - dg[i, sl] * q + h * around(old, i, sl) + around(oldq, i, sl)
            value = q + ws[i, sl] * res
            if last:
                tb[i - SWEEPS] = value
                square = res * res
                total = square if total is None else total + square
            else:
                new[i, sl] = value
                newq[i, sl] = h * value
        if not last:
            one = level + 1
            for j, i in enumerate((one, one + 1, thick - 2 - one, thick - 1 - one)):
                ti[level, j] = new[i]
            old, new = new, (tc if new is ta else ta)
            oldq, newq = newq, oldq
    sqi[...] = jnp.zeros_like(sqi)
    sqi[fields : fields + 1] = jnp.sum(total, axis=0, keepdims=True)


def cone_kernel(blocks, spans, sent, sent_solid, solid, spread, jacobian, *refs):
    p0, s0, v0, w0, p1, te, he, so, ti, dg, ws, xe, xn, xl = refs[:14]
    back, n2, c2, c3, d1, d2, vm, wm, sl_, t0, t1, t2, t3, dl, wl = refs[14:29]
    l0, n1, qa = refs[29:]
    fields, z = p0.shape[0], p0.shape[3]
    rows = p0.shape[2] - 2 * (B + W)
    here = Place(rows, blocks, spans)
    ext, own, tall = here.ext, here.own, here.tall
    fluid = Fluid(spread, jacobian, fields)
    inside = jnp.logical_and(here.inside(z), jnp.logical_not(here.no_left))
    corner = 0
    for f in range(fields):

        def store(sl, x, f=f):
            l0[f, sl] = x

        n = corner + f * 2 * W
        here.fill(
            store, xe[f * rows : (f + 1) * rows], xn[n : n + W], xn[n + W : n + 2 * W], here.no_left
        )
    for c in range(3):

        def store(sl, x, c=c):
            vm[c, sl] = x

        n = corner + (fields + c) * 2 * W
        m = (fields + c) * rows
        here.fill(store, xe[m : m + rows], xn[n : n + W], xn[n + W : n + 2 * W])
    um = [vm[c, ext] for c in range(3)]
    usm = um[0] + um[1] + um[2]
    for f in range(fields):
        wm[f, ext] = jnp.where(inside, DAMPING / fluid.diagonal(f, usm), 0.0)
    def sum_of(level, ref):
        def read(f, sl):
            n = sent.window(level - 1, f).start + sl.start - B
            return unless(here.no_left, xn[n : n + 8]) + ref[f, sl]

        return read

    def plane(cur, i, left, right, store, sl=ext):
        fluid.advance(cur, left, right, speeds(v0, i), at(w0, i), at(s0, i), sl, store)

    outer = [lambda sl, c=c: vm[c, sl] for c in range(3)]
    plane(at(p0, 0), 0, flat(l0), at(p0, 1), into_flat(n1))
    for f in range(fields):
        d1[f, ext] = wm[f, ext] * (fluid.d[f] + um[0]) * p0[f, 0, ext]
    plane(flat(n1), 0, sum_of(1, d1), at(p1, 0), into_flat(n2))
    plane(at(p1, 0), 1, flat(n1), at(p1, 1), into_flat(c2))
    fluid.advance(flat(d1), None, flat(n1), outer, flat(wm), None, ext, into_flat(d2))
    plane(flat(n2), 0, sum_of(2, d2), flat(c2), into_flat(c3))
    n = solid.size()
    for reach, read in (
        (3, at(p0, 0)),
        (2, flat(n1)),
        (1, flat(n2)),
        (0, flat(c3)),
    ):
        size = rows + 2 * reach
        for f in range(fields):
            back[n : n + size] = read(f, here.reach(reach))
            n = n + size
    corner = corner + (fields + 3) * 2 * W
    early = (fields + 5) * rows
    zero = jnp.zeros((W, z), F32)
    hl, sl_ = sl_.at[0], sl_.at[1]
    for buf, j, scale in ((t0, 1, 1.0), (t0, 0, 1.0), (hl, 3, 0.5), (hl, 2, 0.5), (hl, 1, 0.5), (sl_, 3, 1.0)):

        def store(sl, x, buf=buf, j=j, scale=scale):
            buf[j, sl] = scale * x

        low, high = zero, zero
        if buf is not hl or j > 1:
            low, high = xn[corner : corner + W], xn[corner + W : corner + 2 * W]
            corner = corner + 2 * W
        here.fill(store, xe[early : early + rows], low, high, here.no_left)
        early = early + rows

    def h_of(i, sl):
        return hl[i + 4, sl] if i < 0 else he[i, sl]

    for i in range(-2, 1):
        dl[i + 3, ext] = solid_diagonal(h_of, i, ext)
        wl[i + 3, ext] = solid_weight(h_of(i, ext), dl[i + 3, ext])

    def sweep(old, shift, new, i, j):
        q = old[i + shift, ext]
        diagonal, w, m = (dl, wl, i + 3) if i <= 0 else (dg, ws, i)
        res = (sl_[3, ext] if i < 0 else so[i, ext]) - diagonal[m, ext] * q
        res = res + h_of(i, ext) * around(old, i + shift, ext) + around(qa, i + shift, ext)
        new[j, ext] = q + w[m, ext] * res

    def weigh(old, count):
        for j in range(count):
            qa[j, ext] = h_of(j - 2, ext) * old[j, ext]

    t0[2], t0[3] = te[0], te[1]
    weigh(t0, 4)
    for i in (-1, 0):
        sweep(t0, 2, t1, i, i + 2)
    t1[0, ext] = unless(here.no_left, xl[sent_solid.window(0, 0)])
    t1[3], t1[4] = ti[0, 0], ti[0, 1]
    weigh(t1, 5)
    for i in (-1, 0, 1):
        sweep(t1, 2, t2, i, i + 2)
    t2[0, ext] = unless(here.no_left, xl[sent_solid.window(1, 0)])
    t2[0, ext] = t2[0, ext] + wl[1, ext] * (hl[2, ext] + hl[3, ext]) * t1[1, ext]
    t2[4], t2[5] = ti[1, 0], ti[1, 1]
    weigh(t2, 6)
    for i in (-1, 0, 1, 2):
        sweep(t2, 2, t3, i, i + 1)
    t3[4], t3[5] = ti[2, 0], ti[2, 1]
    for level, (ref, i) in enumerate(((he, 0), (he, 1), (t0, 2), (t1, 2), (t2, 2), (t3, 1))):
        sl = solid.window(level, 0)
        reach = solid.reaches[level]
        back[sl.start + W - reach : sl.stop - W + reach] = ref[i, here.reach(reach)]


def flux_kernel(blocks, spans, third_at, spread, jacobian, *refs):
    p0, s0, v0, w0, p1, n2, c2, c3, d1, d2, vm, wm, xe, xl, coef, hot, meta = refs[:17]
    parts, left, sq, q1, p2, p3, m3, d3 = refs[17:]
    depth = p0.shape[1]
    fields, rows, z = left.shape[0], left.shape[2], left.shape[3]
    here = Place(rows, blocks, spans)
    ext, own = here.ext, here.own
    fluid = Fluid(spread, jacobian, fields)
    m = (fields + 3) * rows
    u0mm, usmm = xe[m : m + rows], xe[m + rows : m + 2 * rows]
    outer = [lambda sl, c=c: vm[c, sl] for c in range(3)]

    def third(f, sl):
        n = third_at.window(0, f).start + sl.start - B
        return unless(here.no_left, xl[n : n + 8]) + d3[f, sl]

    def plane(cur, i, before, after, store, sl=ext):
        fluid.advance(cur, before, after, speeds(v0, i), at(w0, i), at(s0, i), sl, store)

    def farther(f, sl):
        n = sl.start - own.start
        w = unless(here.no_left, DAMPING / fluid.diagonal(f, usmm[n : n + 8]))
        return w * (fluid.d[f] + u0mm[n : n + 8]) * d1[f, sl]

    def first(i):
        return at(p1, i - 1) if i < 3 else at(q1, i - 3)

    for i in range(3, depth - 1):
        plane(at(p0, i), i, at(p0, i - 1), at(p0, i + 1), into(q1, i - 3))
    for i in range(2, depth - 2):
        plane(first(i), i, first(i - 1), first(i + 1), into(p2, i - 2))
    for i in range(3, depth - 3):
        plane(at(p2, i - 2), i, at(p2, i - 3), at(p2, i - 1), into(p3, i - 3))
    fluid.advance(flat(d2), farther, flat(n2), outer, flat(wm), None, own, into_flat(d3))
    plane(flat(c2), 1, flat(n2), at(p2, 0), into(m3, 0))
    plane(at(p2, 0), 2, flat(c2), at(p2, 1), into(m3, 1))
    squares = [None] * fields
    third_of = [flat(c3), at(m3, 0), at(m3, 1), at(p3, 0), at(p3, 1)]
    for i in range(4):

        def final(f, sl, res, value, i=i):
            left[f, i, sl.start - own.start : sl.stop - own.start] = value
            square = res * res
            squares[f] = square if squares[f] is None else squares[f] + square

        plane(third_of[i], i, third_of[i - 1] if i > 0 else third, third_of[i + 1], final, own)
    sq[...] = jnp.zeros_like(sq)
    for f in range(fields):
        sq[f : f + 1] = jnp.sum(squares[f], axis=0, keepdims=True)
    flux = coef[0] * left[fields - 1, 0]
    parts[...] = jnp.dot(hot[...], flux, precision=HIGHEST, preferred_element_type=F32)
    for j in range(blocks):
        parts[j * CHUNK + 2 * CAP : (j + 1) * CHUNK] = meta[j]


def rest_kernel(blocks, spans, sent, spread, jacobian, *refs):
    p0, s0, v0, w0, p1, p2, p3, left, sqb, xn, _, gas, sq, n1, n2, n3 = refs
    fields, depth = gas.shape[0], gas.shape[1]
    rows = gas.shape[2]
    here = Place(rows, blocks, spans)
    ext, own, tall = here.ext, here.own, here.tall
    fluid = Fluid(spread, jacobian, fields)
    def arrived(level):
        def read(f, sl):
            n = sent.window(level, f).start + sl.start - B
            return unless(here.no_right, xn[n : n + 8])

        return read

    known = [{i: (p0, i) for i in range(depth)}, {}, {}, {}]
    for level, (buf, low) in enumerate(((p1, 3), (p2, 2), (p3, 3))):
        for i in range(low, depth - 1 - level):
            known[level + 1][i] = (buf, i - low)

    def read(level, i):
        ref, j = known[level][i]
        return at(ref, j)

    def plane(level, i, store, sl=ext):
        fluid.advance(
            read(level, i),
            read(level, i - 1),
            read(level, i + 1) if i < depth - 1 else arrived(level),
            speeds(v0, i),
            at(w0, i),
            at(s0, i),
            sl,
            store,
        )

    todo = ((depth - 1,), (depth - 2, depth - 1), (depth - 3, depth - 2, depth - 1))
    for level, new in enumerate((n1, n2, n3)):
        for j, i in enumerate(todo[level]):
            plane(level, i, into(new, j))
            known[level + 1][i] = (new, j)
    total = [None] * fields
    for f in range(fields):
        for i in range(4):
            gas[f, i] = left[f, i]
    for i in range(4, depth):

        def final(f, sl, res, value, i=i):
            gas[f, i, sl.start - own.start : sl.stop - own.start] = value
            square = res * res
            total[f] = square if total[f] is None else total[f] + square

        plane(3, i, final, own)
    sq[...] = sqb[...]
    for f in range(fields):
        sq[f : f + 1] = sq[f : f + 1] + jnp.sum(total[f], axis=0, keepdims=True)


def solid_kernel(
    blocks, spans, sent, te, he, so, ti, tbi, sqi, dg, ws, sl_, tl0, tl1, tl2, tl3, dl, wl, xb, _, *refs
):
    tb, rb, sq, rh, rd, rw = refs[:6]
    hr, dr, wr, ta, tc, qa = refs[6:]
    thick, rows, z = tb.shape
    here = Place(rows, blocks, spans)
    ext, own, tall = here.ext, here.own, here.tall
    hl = sl_.at[0]

    def arrived(n):
        return unless(here.no_right, xb[sent.window(n, 0)])

    for j in range(2):
        hr[j, ext] = arrived(j)

    def h_of(i, sl):
        if i < 0:
            return hl[i + 4, sl]
        return he[i, sl] if i < thick else hr[i - thick, sl]

    for j in range(2):
        i = thick - 1 + j
        dr[j, ext] = solid_diagonal(h_of, i, ext)
        wr[j, ext] = solid_weight(h_of(i, ext), dr[j, ext])

    def d_of(left, inside, right, i, sl):
        if i <= 0:
            return left[i + 3, sl]
        return inside[i, sl] if i < thick - 1 else right[i - thick + 1, sl]

    def residual(old, j, i, sl):
        res = so[i, sl] - d_of(dl, dg, dr, i, sl) * old[j, sl]
        return res + h_of(i, sl) * around(old, j, sl) + around(qa, j, sl)

    sums = None
    for j in range(6):
        qa[j, ext] = h_of(j - 1, ext) * tl3[j, ext]
    for i in range(4):
        res = residual(tl3, i + 1, i, own)
        tb[i] = tl3[i + 1, own] + d_of(wl, ws, wr, i, own) * res
        if i < 3:
            rb[i] = res
        else:
            sums = res * res
    old, new = ta, tc
    old[0], old[1] = te[thick - 2], te[thick - 1]
    old[2, ext] = arrived(2)
    for level in range(SWEEPS):
        last = level == SWEEPS - 1
        sl = own if last else ext
        low = thick - 2 - level
        for j in range(level + 3):
            qa[j, ext] = h_of(low + j, ext) * old[j, ext]
        for j in range(1, level + 2):
            i = low + j
            res = residual(old, j, i, sl)
            value = old[j, sl] + d_of(wl, ws, wr, i, sl) * res
            if last:
                tb[i] = value
                rb[i - (thick - 7)] = res
            else:
                new[j + 1, ext] = value
        if not last:
            for j in range(2):
                new[j] = ti[level, j + 2]
            new[level + 3, ext] = arrived(3 + level)
            old, new = new, old
    for i in range(SWEEPS, thick - SWEEPS):
        tb[i] = tbi[i - SWEEPS]
    sq[...] = sqi[...]
    n = sq.shape[0] - 3
    sq[n : n + 1] = sq[n : n + 1] + jnp.sum(sums, axis=0, keepdims=True)
    for region in range(2):
        for j in range(5):
            i = j - 2 if region == 0 else thick - 4 + j
            rh[region, j, ext] = h_of(i, ext)
            rd[region, j, ext] = d_of(dl, dg, dr, i, ext)
            rw[region, j, ext] = d_of(wl, ws, wr, i, ext)


def surface_kernel(blocks, arrived, surface, yf, yb):
    rows = surface.shape[0] // 2
    meta = arrived[0, 2 * CAP :]
    for j in range(1, blocks):
        meta = meta + arrived[j, 2 * CAP :]
    row = lax.broadcasted_iota(jnp.int32, (2 * rows, 4 * CHUNK), 0)
    slot = lax.broadcasted_iota(jnp.int32, (2 * rows, 4 * CHUNK), 1) % CHUNK
    row = row + 1 - jnp.where(slot < CAP, 0, rows)
    row = jnp.where((row >= 1) & (row <= rows), row, -1).astype(F32)
    whole = None
    for j in range(0, blocks, 4):
        sent = jnp.concatenate([arrived[j + m] for m in range(4)], axis=0)
        hot = jnp.where(row == meta[j // 4 : j // 4 + 1], 1.0, 0.0)
        got = jnp.dot(hot, sent, precision=HIGHEST, preferred_element_type=F32)
        whole = got if whole is None else whole + got
    surface[...] = whole
    yf[:W] = whole[rows - W : rows]
    yf[W:] = whole[2 * rows - W :]
    yb[:W] = whole[:W]
    yb[W:] = whole[rows : rows + W]


def response_kernel(
    blocks, spans, fields, surface, yl, yr, rh, rd, rw, tb, rb, sqf, sqs, tn, out, da, db, hd, so
):
    thick, rows, z = tb.shape
    here = Place(rows, blocks, spans)
    ext, own = here.ext, here.own
    for buf in (da, db, hd):
        buf[...] = jnp.zeros_like(buf)
    sq = sqf[...] + sqs[...]
    gained = jnp.zeros((rows, z), F32)
    for region in range(2):

        def store(sl, x, region=region):
            so[region, sl] = x

        edge = slice(region * W, (region + 1) * W)
        here.fill(store, surface[region * rows : (region + 1) * rows], yl[edge], yr[edge])

    needed = (((2,), (1, 2, 3), (1, 2, 3, 4), (3, 4, 5)), ((4,), (3, 4, 5), (2, 3, 4, 5), (1, 2, 3, 4)))
    for i in range(3, thick - 4):
        tn[i] = tb[i]
    for region in range(2):
        old, new = da, db
        source = 2 if region == 0 else 4
        for sweep in range(SWEEPS):
            final = sweep == SWEEPS - 1
            for j in needed[region][sweep]:
                res = so[region, ext] if j == source else None
                h, w = rh[region, j - 1, ext], rw[region, j - 1, ext]
                if sweep > 0:
                    q = old[region, j, ext]
                    flow = h * around(old.at[region], j, ext) + around(hd.at[region], j, ext) - rd[region, j - 1, ext] * q
                    res = flow if res is None else res + flow
                    change = q + w * res
                else:
                    change = w * res
                if final:
                    i = j - 3 if region == 0 else thick - 5 + j
                    kept = i if region == 0 else 2 + j
                    mine = slice(W, W + rows)
                    tn[i] = tb[i] + change[mine]
                    full = rb[kept] + res[mine]
                    gained = gained + full * full
                else:
                    new[region, j, ext] = change
            if not final:
                for j in needed[region][sweep]:
                    hd[region, j, ext] = rh[region, j - 1, ext] * new[region, j, ext]
                old, new = new, old
    extra = jnp.sum(gained, axis=0, keepdims=True)
    row = lax.broadcasted_iota(jnp.int32, sq.shape, 0)
    sq = sq + jnp.where(row == fields, extra, 0.0)
    for j in range(blocks):
        out[j, :rows] = tn[thick - 1]
        out[j, rows:] = sq


def squares_kernel(blocks, rows, arrived, sq):
    whole = arrived[0, rows:]
    for j in range(1, blocks):
        whole = whole + arrived[j, rows:]
    sq[...] = whole


def return_kernel(blocks, arrived, idx, coef, gas, t, gas_out, t_out, plane, sems):
    fields, rows = gas.shape[0], gas.shape[2]
    last = fields - 1
    copies = [
        pltpu.make_async_copy(gas.at[pl.ds(0, last)], gas_out.at[pl.ds(0, last)], sems.at[0]),
        pltpu.make_async_copy(
            gas.at[last, pl.ds(1, gas.shape[1] - 1)],
            gas_out.at[last, pl.ds(1, gas.shape[1] - 1)],
            sems.at[1],
        ),
        pltpu.make_async_copy(t, t_out, sems.at[2]),
    ]
    for copy in copies:
        copy.start()
    row = lax.broadcasted_iota(jnp.int32, (rows, rows), 0).astype(F32)
    taken = None
    for j in range(blocks):
        hot = jnp.where(idx[...] - float(j * rows) == row, 1.0, 0.0)
        got = lax.dot_general(
            hot,
            arrived[j, :rows],
            (((0,), (0,)), ((), ())),
            precision=HIGHEST,
            preferred_element_type=F32,
        )
        taken = got if taken is None else taken + got
    plane[...] = gas[last, 0] + coef[0] * taken
    copy = pltpu.make_async_copy(plane, gas_out.at[last, 0], sems.at[3])
    copy.start()
    for other in copies:
        other.wait()
    copy.wait()


def shards(
    blocks,
    spans,
    fluid_adjoint_in,
    fluid_source,
    velocity,
    diffusion,
    jacobian,
    wall_coefficient,
    metal_costate_prior,
    solid_source,
    conductivity,
    tile_owner,
    tile_target,
):
    p, src, vel = fluid_adjoint_in, fluid_source, velocity
    t, heat, k = metal_costate_prior, solid_source, conductivity
    fields, depth, rows, z = p.shape
    thick = t.shape[0]
    tall = rows + 2 * W
    buf = tall + 2 * B
    forward = {
        "blk": [(i, (i + 1) % blocks) for i in range(blocks)],
        "span": [(i, (i + 1) % spans) for i in range(spans)],
    }
    backward = {axis: [(j, i) for i, j in pairs] for axis, pairs in forward.items()}

    def ahead(x, axis):
        return lax.ppermute(x, axis, forward[axis])

    def behind(x, axis):
        return lax.ppermute(x, axis, backward[axis])

    edges = Edges(fields, depth, thick)
    inputs = [p, src, vel, t, heat, k]
    p, src, vel, t, heat, k, yf, yb, xf, zf, zb = call(
        functools.partial(early_kernel, edges),
        held(*[x.shape for x in inputs])
        + [(edges.size, z)] * 2
        + [((fields + 11) * rows, z)]
        + [(edges.late_size, z)] * 2,
        [pltpu.SemaphoreType.DMA((6,))],
        [HBM] * 6,
        *[pltpu.with_memory_space_constraint(x, pltpu.HBM) for x in inputs],
    )
    yl, yr = ahead(yf, "span"), behind(yb, "span")
    xe = ahead(xf, "blk")
    sent_ahead = Arrivals((fields + 8) * 2 * W, rows, fields, (2, 1))
    solid_ahead = Arrivals(8, rows, 1, (1, 0))
    third_ahead = Arrivals((solid_ahead.size() + 7) // 8 * 8, rows, fields, (0,))
    four = (4, buf, z)
    out, later = call(
        functools.partial(ahead_kernel, blocks, spans, edges, solid_ahead, third_ahead),
        [((sent_ahead.size() + W + 7) // 8 * 8, z), (third_ahead.size(), z)],
        [(fields, 4, buf, z), (fields, 3, buf, z), (fields, 2, buf, z), (fields, 3, buf, z)]
        + [(3, 3, buf, z), (fields, 3, buf, z)]
        + [four] * 6,
        [SMEM] * 2 + [VMEM] * 8,
        diffusion,
        jacobian,
        p,
        src,
        vel,
        t,
        heat,
        k,
        yl,
        yr,
        cost=COSTS[1],
    )
    xn, xl = ahead(out, "blk"), ahead(later, "blk")
    full = (fields, depth, buf, z)
    part = [(fields, depth - 2 * (level + 1), buf, z) for level in range(3)]
    solid = (thick, buf, z)
    zl, zr = ahead(zf, "span"), behind(zb, "span")
    p0, s0, v0, w0, p1, place, meta, idx = call(
        functools.partial(inner_kernel, blocks, spans, edges),
        held(full, full, (3, depth, buf, z), full, (fields, 2, buf, z))
        + held((blocks * CHUNK, rows), (blocks, 8, z), (1, rows)),
        [],
        [SMEM] * 2 + [VMEM] * 9,
        diffusion,
        jacobian,
        tile_owner.reshape(1, rows),
        tile_target,
        p,
        src,
        vel,
        yl,
        yr,
        zl,
        zr,
        cost=COSTS[2],
    )
    te, he, so, ti, tb, sqi, dg, ws = call(
        functools.partial(inner_solid_kernel, blocks, spans, edges, fields),
        held(solid, solid, solid, (3, 4, buf, z), (thick - 2 * SWEEPS, rows, z), (8, z), solid, solid),
        [solid] * 4,
        [VMEM] * 6,
        t,
        heat,
        k,
        zl,
        zr,
        idx,
        cost=COSTS[2],
    )
    solid_back = Arrivals(8, rows, 1, (3, 1, 3, 2, 1, 0))
    sent_back = Arrivals(solid_back.size(), rows, fields, (3, 2, 1, 0))
    one, six = (fields, buf, z), (6, buf, z)
    back, n2, c2, c3, d1, d2, vm, wm, sl_, *lefts = call(
        functools.partial(cone_kernel, blocks, spans, sent_ahead, solid_ahead, solid_back),
        [(sent_back.size(), z)]
        + held(one, one, one, one, one, (3, buf, z), one, (2, 4, buf, z))
        + held(six, six, six, six, (4, buf, z), (4, buf, z)),
        [one] * 2 + [six],
        [SMEM] * 2 + [VMEM] * 14,
        diffusion,
        jacobian,
        p0,
        s0,
        v0,
        w0,
        p1,
        te,
        he,
        so,
        ti,
        dg,
        ws,
        xe,
        xn,
        xl,
        cost=COSTS[3],
    )
    xr = lax.ppermute(back, "blk", backward["blk"][: blocks - 1])
    parts, half, sq, q1, p2, p3 = call(
        functools.partial(flux_kernel, blocks, spans, third_ahead),
        [(blocks * CHUNK, z)]
        + held((fields, 4, rows, z), (8, z), (fields, depth - 4, buf, z), *part[1:]),
        [(fields, 2, buf, z), one],
        [SMEM] * 2 + [VMEM] * 17,
        diffusion,
        jacobian,
        p0,
        s0,
        v0,
        w0,
        p1,
        n2,
        c2,
        c3,
        d1,
        d2,
        vm,
        wm,
        xe,
        xl,
        wall_coefficient,
        place,
        meta,
        cost=COSTS[2],
    )
    arrived = lax.all_to_all(parts.reshape(blocks, CHUNK, z), "blk", 0, 0)
    surface, yf, yb = call(
        functools.partial(surface_kernel, blocks),
        [(2 * rows, z), (2 * W, z), (2 * W, z)],
        [],
        [VMEM],
        arrived,
    )
    yl, yr = ahead(yf, "span"), behind(yb, "span")
    gas, sqf = call(
        functools.partial(rest_kernel, blocks, spans, sent_back),
        held(p.shape, (8, z)),
        [(fields, 1, buf, z), (fields, 2, buf, z), (fields, 3, buf, z)],
        [SMEM] * 2 + [VMEM] * 11,
        diffusion,
        jacobian,
        p0,
        s0,
        v0,
        w0,
        q1,
        p2,
        p3,
        half,
        sq,
        xr,
        yf,
        cost=COSTS[4],
    )
    two, edge = (2, buf, z), (2, 5, buf, z)
    tb, rb, sqs, rh, rd, rw = call(
        functools.partial(solid_kernel, blocks, spans, solid_back),
        held(t.shape, (7, rows, z), (8, z), edge, edge, edge),
        [two] * 3 + [six] * 3,
        [VMEM] * 17,
        te,
        he,
        so,
        ti,
        tb,
        sqi,
        dg,
        ws,
        sl_,
        *lefts,
        xr,
        yf,
        cost=COSTS[5],
    )
    region = (2, 7, buf, z)
    t, out = call(
        functools.partial(response_kernel, blocks, spans, fields),
        held(t.shape, (blocks, rows + 8, z)),
        [region] * 3 + [(2, buf, z)],
        [VMEM] * 10,
        surface,
        yl,
        yr,
        rh,
        rd,
        rw,
        tb,
        rb,
        sqf,
        sqs,
    )
    arrived = lax.all_to_all(out, "blk", 0, 0)
    (sq,) = call(
        functools.partial(squares_kernel, blocks, rows), held((8, z)), [], [VMEM], arrived
    )
    others = [
        lax.ppermute(sq, "span", [(i, i ^ step) for i in range(spans)]) for step in range(1, spans)
    ]
    gas, t = call(
        functools.partial(return_kernel, blocks),
        [gas.shape, t.shape],
        [(rows, z), pltpu.SemaphoreType.DMA((4,))],
        [VMEM] * 5,
        arrived,
        idx,
        wall_coefficient,
        gas,
        t,
        out_specs=[pl.BlockSpec(memory_space=pl.ANY)] * 2,
        cost=2.0,
    )
    sq = functools.reduce(jnp.add, others, sq)
    everyone = blocks * spans
    fluid_cells = float(depth * rows * z * everyone)
    solid_cells = float(thick * rows * z * everyone)
    counts = jnp.where(jnp.arange(fields + 1) < fields, fluid_cells, solid_cells)
    totals = jnp.sum(sq[: fields + 1], axis=1)
    norms = jnp.sqrt(totals / counts)
    return gas, t, norms


def solution(mesh):
    placed = (
        P(None, "blk", "span", None),
        P(None, "blk", "span", None),
        P(None, "blk", "span", None),
        P(),
        P(),
        P("blk", "span", None),
        P("blk", "span", None),
        P("blk", "span", None),
        P("blk", "span", None),
        P("span", "blk", None),
        P("span", "blk"),
    )
    return jax.shard_map(
        functools.partial(shards, mesh.shape["blk"], mesh.shape["span"]),
        mesh=mesh,
        in_specs=placed,
        out_specs=(P(None, "blk", "span", None), P("blk", "span", None), P()),
        check_vma=False,
    )
```
